32 devices in a mesh: fsdp: 8 (over z, y), sub: 4 (over x, core).
Axes of the slice: x: 2, y: 2, z: 4, core: 2. Of those that a mesh axis runs over, the one named last changes fastest.
Arguments:
- images: bfloat16 [128, 256, 768], P(('fsdp', 'sub')), may hold values from -6 to 6
- counts: int32 [128], P(('fsdp', 'sub')), may hold values from 18 to 256, as said below
- joint_weight: bfloat16 [768, 2304], P('fsdp', 'sub'), may hold values from -0.21875 to 0.21875
- out_weight: bfloat16 [768, 768], P('fsdp', 'sub'), may hold values from -1.75 to 1.75
- up_weight: bfloat16 [768, 3072], P('fsdp', 'sub'), may hold values from -0.21875 to 0.21875
- down_weight: bfloat16 [3072, 768], P('fsdp', 'sub'), may hold values from -0.109375 to 0.109375
- first_gain: bfloat16 [768], P(('fsdp', 'sub')), may hold values from 0.099609375 to 1.8984375
- first_shift: bfloat16 [768], P(('fsdp', 'sub')), may hold values from -3 to 3
- query_bias: bfloat16 [768], P(('fsdp', 'sub')), may hold values from -3 to 3
- value_bias: bfloat16 [768], P(('fsdp', 'sub')), may hold values from -3 to 3
- out_bias: bfloat16 [768], P(('fsdp', 'sub')), may hold values from -2 to 2
- first_scale: bfloat16 [768], P(('fsdp', 'sub')), may hold values from 0.5 to 1.5
- second_gain: bfloat16 [768], P(('fsdp', 'sub')), may hold values from 0.099609375 to 1.8984375
- second_shift: bfloat16 [768], P(('fsdp', 'sub')), may hold values from -3 to 3
- up_bias: bfloat16 [3072], P(('fsdp', 'sub')), may hold values from -3 to 3
- down_bias: bfloat16 [768], P(('fsdp', 'sub')), may hold values from -2 to 2
- second_scale: bfloat16 [768], P(('fsdp', 'sub')), may hold values from 0.5 to 1.5
- cotangent: bfloat16 [128, 256, 768], P(('fsdp', 'sub')), may hold values from -6 to 6
Outputs:
- block_out: bfloat16 [128, 256, 768], P(('fsdp', 'sub'))
- image_grad: float32 [128, 256, 768], P(('fsdp', 'sub'))
- joint_grad: float32 [768, 2304], P('fsdp', 'sub')
- out_grad: float32 [768, 768], P('fsdp', 'sub')
- up_grad: float32 [768, 3072], P('fsdp', 'sub')
- down_grad: float32 [3072, 768], P('fsdp', 'sub')
- first_gain_grad: float32 [768], P(('fsdp', 'sub'))
- first_shift_grad: float32 [768], P(('fsdp', 'sub'))
- query_bias_grad: float32 [768], P(('fsdp', 'sub'))
- value_bias_grad: float32 [768], P(('fsdp', 'sub'))
- out_bias_grad: float32 [768], P(('fsdp', 'sub'))
- first_scale_grad: float32 [768], P(('fsdp', 'sub'))
- second_gain_grad: float32 [768], P(('fsdp', 'sub'))
- second_shift_grad: float32 [768], P(('fsdp', 'sub'))
- up_bias_grad: float32 [3072], P(('fsdp', 'sub'))
- down_bias_grad: float32 [768], P(('fsdp', 'sub'))
- second_scale_grad: float32 [768], P(('fsdp', 'sub'))
The draws below stay inside these ranges and needn't reach their ends.
Inputs may be any that keep to these rules, and one draw needn't show every extreme that they name: `counts`: image 0 is always full.
All inputs are finite; a program needn't handle non-finite values.
Results may differ from the reference program's by a relative error of at most 0.02.
Values may be sent and summed in bfloat16 or wider, within the bound.
No kernel may reach another device: no remote copies, remote signals or barrier semaphores. Data moves between devices by JAX's collectives and lax.ppermute only.
A program may use at most 192 MiB of HBM per device.

```python
import math
import jax
import jax.numpy as jnp
from jax import lax

D = 768
HEADS = 12
FF = 3072
HD = 64
P_SIZE = 256
IMAGES = 128


def draw_counts(key, part):
    key = jax.random.fold_in(key, 11)
    first_key, second_key, third_key = jax.random.split(key, 3)
    reach = jax.random.randint(first_key, (IMAGES,), 1, P_SIZE - P_SIZE // 16)
    missing = jax.random.randint(second_key, (IMAGES,), 0, reach)
    padded = jax.random.randint(third_key, (IMAGES,), 0, 2)
    result = P_SIZE - missing * padded
    return result.at[0].set(P_SIZE).astype(jnp.int32)


def level_of(rng, shape, cuts, low, high):
    level = 1.0
    for dim, parts in cuts:
        heights = jax.random.uniform(jax.random.fold_in(jax.random.fold_in(rng, 6), dim), (parts,), jnp.float32, low / len(cuts), high / len(cuts))
        level = level * jnp.repeat(jnp.exp(heights), shape[dim] // parts).reshape((-1,) + (1,) * (len(shape) - 1 - dim))
    return level


def gaussian(key, dims, scale, most, cuts=(), held_as=jnp.bfloat16):
    level = level_of(key, dims, cuts, -0.22, 0.18) if cuts else 1.0
    drawn = jax.random.normal(key, dims, jnp.float32) * scale * level
    return jnp.minimum(jnp.maximum(drawn, -most), most).astype(held_as)


def setup_inputs(seed: int = 0) -> dict:
    key_of = jax.random.split(jax.random.key(seed), 19)
    images = gaussian(key_of[0], (IMAGES, P_SIZE, D), 1.0, 6.0, ((0, 32),))
    counts = draw_counts(jax.random.fold_in(key_of[18], 71), 0)
    joint_weight = gaussian(key_of[2], (D, 3 * D), D ** -0.5, 0.21875, ((0, 8), (1, 4)))
    out_weight = gaussian(key_of[3], (D, D), (D // 64) ** -0.5, 1.75, ((0, 8), (1, 4)))
    up_weight = gaussian(key_of[4], (D, FF), D ** -0.5, 0.21875, ((0, 8), (1, 4)))
    down_weight = gaussian(key_of[5], (FF, D), FF ** -0.5, 0.109375, ((0, 8), (1, 4)))
    first_gain = jnp.clip(1.0 + 0.18 * jax.random.normal(key_of[6], (D,), jnp.float32), 0.099609375, 1.8984375).astype(jnp.bfloat16)
    first_shift = gaussian(key_of[7], (D,), 0.5, 3.0, ((0, 32),))
    query_bias = gaussian(key_of[8], (D,), 0.5, 3.0, ((0, 32),))
    value_bias = gaussian(key_of[9], (D,), 0.5, 3.0, ((0, 32),))
    out_bias = gaussian(key_of[10], (D,), 0.3, 2.0, ((0, 32),))
    first_scale = jnp.clip(0.5 + 1.0 * jax.random.uniform(key_of[11], (D,), jnp.float32) ** level_of(key_of[11], (D,), ((0, 32),), -0.2, 0.2), 0.5, 1.5).astype(jnp.bfloat16)
    second_gain = jnp.clip(1.0 + 0.18 * jax.random.normal(key_of[12], (D,), jnp.float32), 0.099609375, 1.8984375).astype(jnp.bfloat16)
    second_shift = gaussian(key_of[13], (D,), 0.5, 3.0, ((0, 32),))
    up_bias = gaussian(key_of[14], (FF,), 0.5, 3.0, ((0, 32),))
    down_bias = gaussian(key_of[15], (D,), 0.3, 2.0, ((0, 32),))
    second_scale = jnp.clip(0.5 + 1.0 * jax.random.uniform(key_of[16], (D,), jnp.float32) ** level_of(key_of[16], (D,), ((0, 32),), -0.2, 0.2), 0.5, 1.5).astype(jnp.bfloat16)
    cotangent = gaussian(key_of[17], (IMAGES, P_SIZE, D), 1.0, 6.0, ((0, 32),))
    return dict(images=images, counts=counts, joint_weight=joint_weight, out_weight=out_weight, up_weight=up_weight, down_weight=down_weight, first_gain=first_gain, first_shift=first_shift, query_bias=query_bias, value_bias=value_bias, out_bias=out_bias, first_scale=first_scale, second_gain=second_gain, second_shift=second_shift, up_bias=up_bias, down_bias=down_bias, second_scale=second_scale, cotangent=cotangent)


EPS = 1e-06
NEGATIVE = -1e+30
HIGH = lax.Precision.HIGHEST

@jax.custom_vjp
def low(v):
    return lax.optimization_barrier(v.astype(jnp.bfloat16)).astype(jnp.float32)

@jax.custom_vjp
def low_back(v):
    return v

def low_keep(v):
    return (low(v), None)

def low_pass(kept, grad):
    return (grad,)

def back_keep(v):
    return (v, None)

def back_low(kept, grad):
    return (low(grad),)
low.defvjp(low_keep, low_pass)
low_back.defvjp(back_keep, back_low)

def layer_norm(rows, gain, shift):
    centre = rows - lax.optimization_barrier(jnp.mean(rows, axis=-1, keepdims=True))
    spread = lax.optimization_barrier(jnp.mean(centre * centre, axis=-1, keepdims=True))
    return centre * lax.rsqrt(spread + EPS) * gain + shift

def block_forward(block_images, block_counts, params):
    joint, out_full, up_full, down_full, gain_one, shift_one, query_add, value_add, out_add, scale_one, gain_two, shift_two, up_add, down_add, scale_two = params
    group = block_images.shape[0]
    positions = jnp.arange(P_SIZE, dtype=jnp.int32)
    valid = positions[None, :] < block_counts[:, None]
    rows = block_images.reshape(group * P_SIZE, D)
    first_in = low(layer_norm(rows, gain_one, shift_one))
    joint_bias = jnp.concatenate([query_add, jnp.zeros_like(query_add), value_add])
    mixed = jnp.dot(first_in, joint, precision=HIGH) + joint_bias
    shape_four = (group, P_SIZE, HEADS, HD)
    query = low_back(low(mixed[:, :D])).reshape(shape_four)
    keys_in = low_back(low(mixed[:, D:2 * D])).reshape(shape_four)
    values_in = low_back(low(mixed[:, 2 * D:])).reshape(shape_four)
    factor = 1.0 / math.sqrt(HD)
    scores = jnp.einsum('bqhd,bkhd->bhqk', query, keys_in, precision=HIGH) * factor
    scores = low_back(jnp.where(valid[:, None, None, :], scores, NEGATIVE))
    largest = lax.optimization_barrier(jnp.max(scores, axis=-1, keepdims=True))
    expon = jnp.exp(scores - largest)
    probs = expon / lax.optimization_barrier(jnp.sum(expon, axis=-1, keepdims=True))
    attended = jnp.einsum('bhqk,bkhd->bqhd', low(probs), values_in, precision=HIGH)
    attended = low_back(low(attended.reshape(group * P_SIZE, D)))
    branch = low_back(jnp.dot(attended, out_full, precision=HIGH) + out_add)
    resid = rows + scale_one * branch
    second_in = low(layer_norm(resid, gain_two, shift_two))
    pre_act = low_back(jnp.dot(second_in, up_full, precision=HIGH) + up_add)
    hidden = low(jax.nn.gelu(pre_act, approximate=False))
    feed_out = low_back(jnp.dot(hidden, down_full, precision=HIGH) + down_add)
    row_mask = valid.reshape(group * P_SIZE, 1).astype(jnp.float32)
    result = (resid + scale_two * feed_out) * row_mask
    return result.reshape(group, P_SIZE, D)

def add_pair(first_sum, second_sum):
    return first_sum + second_sum

def reference(images, counts, joint_weight, out_weight, up_weight, down_weight, first_gain, first_shift, query_bias, value_bias, out_bias, first_scale, second_gain, second_shift, up_bias, down_bias, second_scale, cotangent):
    params = tuple((weight.astype(jnp.float32) for weight in (joint_weight, out_weight, up_weight, down_weight, first_gain, first_shift, query_bias, value_bias, out_bias, first_scale, second_gain, second_shift, up_bias, down_bias, second_scale)))
    group = math.gcd(IMAGES, 16)
    blocks = IMAGES // group
    image_blocks = images.astype(jnp.float32).reshape(blocks, group, P_SIZE, D)
    count_blocks = counts.reshape(blocks, group)
    cot_blocks = cotangent.astype(jnp.float32).reshape(blocks, group, P_SIZE, D)

    def one_block(totals, pieces):
        block_images, block_counts, block_cot = pieces

        def forward(inputs, params_in):
            return block_forward(inputs, block_counts, params_in)
        output, pullback = jax.vjp(forward, block_images, params)
        grad_images, grad_params = pullback(block_cot)
        totals = jax.tree.map(add_pair, totals, grad_params)
        return (totals, (output, grad_images))
    zeros = jax.tree.map(jnp.zeros_like, params)
    totals, (outputs, grads) = lax.scan(one_block, zeros, (image_blocks, count_blocks, cot_blocks))
    block_out = outputs.reshape(IMAGES, P_SIZE, D).astype(jnp.bfloat16)
    image_grad = grads.reshape(IMAGES, P_SIZE, D)
    return (block_out, image_grad, totals[0], totals[1], totals[2], totals[3], totals[4], totals[5], totals[6], totals[7], totals[8], totals[9], totals[10], totals[11], totals[12], totals[13], totals[14])
```

```python
import functools
import math

import jax
import jax.numpy as jnp
from jax import lax
from jax.experimental import pallas as pl
from jax.experimental.pallas import tpu as pltpu
from jax.sharding import PartitionSpec as P

HD = 64
EPS = 1e-06
NEGATIVE = -1e30
ROW_TILES = 8
COL_TILES = 4
PIECES = ROW_TILES * COL_TILES
HALF = PIECES // 2
PARTS = 3
BOTH = ("fsdp", "sub")
VMEM_LIMIT = 56 * 1024 * 1024
BF = jnp.bfloat16
F32 = jnp.float32
NT = (((1,), (1,)), ((), ()))
TN = (((0,), (0,)), ((), ()))


def dot(left, right):
    return jnp.dot(left, right, preferred_element_type=F32)


def dot_general(left, right, dims):
    return lax.dot_general(left, right, dims, preferred_element_type=F32)


def normalize(rows):
    centre = rows - jnp.mean(rows, axis=-1, keepdims=True)
    spread = jnp.mean(centre * centre, axis=-1, keepdims=True)
    inverse = lax.rsqrt(spread + EPS)
    return (centre * inverse, inverse)


def norm_back(upstream, normed, inverse, gain):
    scaled = upstream * gain
    return inverse * (
        scaled
        - jnp.mean(scaled, axis=-1, keepdims=True)
        - normed * jnp.mean(scaled * normed, axis=-1, keepdims=True)
    )


def row_sum(values):
    return jnp.sum(values, axis=0, keepdims=True)


def whole(shape):
    zeros = (0,) * len(shape)
    return pl.BlockSpec(shape, lambda *_: zeros, pipeline_mode=pl.Buffered(1))


def whole_out(shape):
    zeros = (0,) * len(shape)
    return pl.BlockSpec(shape, lambda *_: zeros)


ANY = pl.BlockSpec(memory_space=pl.ANY)


def params():
    return pltpu.CompilerParams(
        dimension_semantics=("arbitrary",), vmem_limit_bytes=VMEM_LIMIT
    )


def cost(flops, moved, trans=0):
    return pl.CostEstimate(flops=flops, bytes_accessed=moved, transcendentals=trans)


def stage_joint(dest, own, other, weights, sems):
    copies = []
    for i in range(PIECES):
        place = dest[i]
        source = own.at[i] if i < HALF else other.at[i - HALF]
        copies.append(
            pltpu.make_async_copy(
                source,
                weights.at[lax.rem(place, COL_TILES), lax.div(place, COL_TILES)],
                sems.at[i],
            )
        )
    for copy in copies:
        copy.start()
    for copy in copies:
        copy.wait()


def joint_columns(weights, s, width):
    return weights[s].reshape(width, width)


def qkv_kernel(dest, images, table, bias, own, other, mixed, first_t, weights, sems):
    width = images.shape[-1]
    span = 3 * width // COL_TILES

    @pl.when(pl.program_id(0) == 0)
    def _():
        stage_joint(dest, own, other, weights, sems)

    normed, _ = normalize(images[0].astype(F32))
    first = (normed * table[0:1] + table[1:2]).astype(BF)
    first_t[...] = first.T
    for s in range(COL_TILES):
        out = dot(first, joint_columns(weights, s, width))
        out = (out + bias[s : s + 1]).astype(BF)
        mixed[s * span : (s + 1) * span, :] = out.T[:span]


def attention_kernel(counts, mixed, attended, probs):
    width = attended.shape[0]
    length = mixed.shape[1]
    scale = math.log2(math.e) / math.sqrt(HD)
    count = counts[pl.program_id(0)]
    valid = lax.broadcasted_iota(jnp.int32, (length, length), 0) < count
    for h in range(width // HD):
        query = mixed[h * HD : (h + 1) * HD, :]
        key = mixed[width + h * HD : width + (h + 1) * HD, :]
        value = mixed[2 * width + h * HD : 2 * width + (h + 1) * HD, :]
        scores = jnp.where(valid, dot_general(key, query, TN), NEGATIVE)
        largest = jnp.max(scores, axis=0, keepdims=True)
        expon = jnp.exp2((scores - largest) * scale)
        low = (expon * (1.0 / jnp.sum(expon, axis=0, keepdims=True))).astype(BF)
        probs[0, h] = low
        attended[h * HD : (h + 1) * HD, :] = dot(value, low).astype(BF)


def second_kernel(
    dest,
    counts,
    images,
    cotangent,
    attended,
    table,
    own,
    other,
    resid_out,
    branch_out,
    second,
    second_t,
    dfeed_out,
    dfeed_t,
    out_full,
    weights,
    sems,
):
    width = images.shape[-1]
    length = images.shape[1]
    span = 3 * width // COL_TILES
    piece = width // COL_TILES

    @pl.when(pl.program_id(0) == 0)
    def _():
        stage_joint(dest, own, other, weights, sems)
        for s in range(COL_TILES):
            out_full[:, s * piece : (s + 1) * piece] = joint_columns(weights, s, width)[:, span:]

    branch = dot_general(attended[...], out_full[...], TN) + table[4:5]
    branch_out[...] = branch.astype(BF)
    resid = images[0].astype(F32) + table[5:6] * branch
    resid_out[...] = resid
    normed, _ = normalize(resid)
    second_in = (normed * table[6:7] + table[7:8]).astype(BF)
    second[...] = second_in
    second_t[...] = second_in.T
    rows = lax.broadcasted_iota(jnp.int32, (length, 1), 0)
    mask = (rows < counts[pl.program_id(0)]).astype(F32)
    dfeed = (cotangent[0].astype(F32) * mask * table[9:10]).astype(BF)
    dfeed_out[...] = dfeed
    dfeed_t[...] = dfeed.T


def gelu_pair(value):
    size = jnp.abs(value)
    t = 1.0 / (1.0 + (0.3275911 / math.sqrt(2.0)) * size)
    bell = jnp.exp2(value * value * (-0.5 * math.log2(math.e)))
    poly = 0.5 * 1.061405429
    for c in (-1.453152027, 1.421413741, -0.284496736, 0.254829592):
        poly = poly * t + 0.5 * c
    tail = poly * t * bell
    cumul = jnp.where(value >= 0, 1.0 - tail, tail)
    return value * cumul, cumul + value * bell * (1.0 / math.sqrt(2.0 * math.pi))


def mlp_kernel(
    first,
    group,
    base,
    dest,
    second,
    second_t,
    dfeed,
    dfeed_t,
    bias,
    own,
    other,
    *rest,
):
    if not first:
        feed_in, dsecond_in, rest = rest[0], rest[1], rest[2:]
    feed, dsecond, bias_grad, keep, send, up, down, up_grad, down_grad, sems = rest
    width = second.shape[1]
    depth = width // ROW_TILES
    span = width // COL_TILES
    lane = up.shape[-1] // 2
    step = pl.program_id(0)
    steps = pl.num_programs(0)
    tile = 256

    def pairs(i):
        place = dest[i]
        m = lax.div(place, COL_TILES)
        s = lax.rem(place, COL_TILES)
        rows = pl.multiple_of(m * depth, 16)
        out = []
        for g in range(group):
            out.append((g, s, rows, depth, 0, 2 * lane, True))
            for h in range(2):
                low = pl.multiple_of(s * span + h * depth, 16)
                out.append((g, m, low, depth, h * lane, lane, False))
        return out

    def move(i, buffer_up, buffer_down, outside, origin, inward):
        copies = []
        for n, (g, q, rows, count, at, wide, is_up) in enumerate(pairs(i)):
            top = origin + g * 2 * depth + (0 if is_up else depth)
            far = outside.at[i % HALF, pl.ds(top, count), pl.ds(at, wide)]
            if is_up:
                near = buffer_up.at[g * COL_TILES + q, pl.ds(rows, count), :]
            else:
                near = buffer_down.at[
                    g * COL_TILES + lax.div(q, 2),
                    pl.ds(rows, count),
                    pl.ds(pl.multiple_of(lax.rem(q, 2) * lane, 128), lane),
                ]
            pair = (far, near) if inward else (near, far)
            copies.append(pltpu.make_async_copy(*pair, sems.at[i]))
        return copies

    @pl.when(step == 0)
    def _():
        copies = []
        for i in range(PIECES):
            copies += move(i, up, down, own if i < HALF else other, base, True)
        for copy in copies:
            copy.start()
        if first:
            feed[...] = jnp.zeros(feed.shape, F32)
            dsecond[...] = jnp.zeros(dsecond.shape, F32)
        else:
            feed[...] = feed_in[...]
            dsecond[...] = dsecond_in[...]
        for copy in copies:
            copy.wait()

    up_now = up[step]
    down_now = down[step]
    hiddens = []
    dpres = []
    total = jnp.zeros((1, 2 * lane), F32)
    for r in range(second.shape[0] // tile):
        rows = slice(r * tile, (r + 1) * tile)
        pre = dot(second[rows, :], up_now) + bias[pl.ds(step, 1), :]
        dhidden = dot(dfeed[rows, :], down_now)
        hidden, slope = gelu_pair(pre)
        hidden = hidden.astype(BF)
        dpre = (dhidden * slope).astype(BF)
        total = total + row_sum(dpre.astype(F32))
        feed[rows, :] += dot_general(hidden, down_now, NT)
        dsecond[rows, :] += dot_general(dpre, up_now, NT)
        hiddens.append(hidden)
        dpres.append(dpre)
    bias_grad[pl.ds(step, 1), :] = total
    up_grad[step] = dot(second_t[...], jnp.concatenate(dpres, axis=0)).astype(BF)
    down_grad[step] = dot(dfeed_t[...], jnp.concatenate(hiddens, axis=0)).astype(BF)

    @pl.when(step == steps - 1)
    def _():
        copies = []
        for i in range(PIECES):
            copies += move(i, up_grad, down_grad, keep if i < HALF else send, 0, False)
        for copy in copies:
            copy.start()
        for copy in copies:
            copy.wait()


def middle_kernel(
    counts,
    cotangent,
    feed,
    dsecond,
    resid,
    branch,
    attended,
    out_full,
    table,
    block_out,
    dresid_out,
    dattended,
    out_grad,
    sums,
    total,
):
    length = cotangent.shape[1]
    step = pl.program_id(0)

    @pl.when(step == 0)
    def _():
        total[...] = jnp.zeros(total.shape, F32)
        sums[...] = jnp.zeros(sums.shape, F32)

    rows = lax.broadcasted_iota(jnp.int32, (length, 1), 0)
    mask = (rows < counts[step]).astype(F32)
    feed_out = feed[...] + table[8:9]
    grad = cotangent[0].astype(F32) * mask
    value = resid[...]
    block_out[0] = ((value + table[9:10] * feed_out) * mask).astype(BF)
    normed, inverse = normalize(value)
    upstream = dsecond[...]
    dresid = grad + norm_back(upstream, normed, inverse, table[6:7])
    dresid_out[...] = dresid
    dbranch = (dresid * table[5:6]).astype(BF)
    dfeed = (grad * table[9:10]).astype(BF)
    sums[0:1] += row_sum(dbranch.astype(F32))
    sums[1:2] += row_sum(dresid * branch[...].astype(F32))
    sums[2:3] += row_sum(upstream * normed)
    sums[3:4] += row_sum(upstream)
    sums[4:5] += row_sum(dfeed.astype(F32))
    sums[5:6] += row_sum(grad * feed_out)
    total[...] += dot(attended[...], dbranch)
    dattended[...] = dot_general(out_full[...], dbranch, NT).astype(BF)

    @pl.when(step == pl.num_programs(0) - 1)
    def _():
        out_grad[...] = total[...].astype(BF)


def attention_back_kernel(mixed, probs, attended, dattended, dmixed, sums, dquery_sum, dvalue_sum):
    width = attended.shape[0]
    length = mixed.shape[1]
    factor = 1.0 / math.sqrt(HD)
    step = pl.program_id(0)

    @pl.when(step == 0)
    def _():
        dquery_sum[...] = jnp.zeros(dquery_sum.shape, F32)
        dvalue_sum[...] = jnp.zeros(dvalue_sum.shape, F32)

    def fold(values):
        values = values.astype(F32)
        return sum(values[:, a : a + 128] for a in range(0, length, 128))

    for h in range(width // HD):
        at = slice(h * HD, (h + 1) * HD)
        query = mixed[h * HD : (h + 1) * HD, :]
        key = mixed[width + h * HD : width + (h + 1) * HD, :]
        value = mixed[2 * width + h * HD : 2 * width + (h + 1) * HD, :]
        upstream = dattended[at, :]
        low = probs[0, h]
        delta = row_sum(upstream.astype(F32) * attended[at, :].astype(F32))
        dprobs = dot_general(value, upstream, TN)
        dscores = (low.astype(F32) * (dprobs - delta)).astype(BF)
        dvalue = dot_general(upstream, low, NT).astype(BF)
        dkey = (dot_general(query, dscores, NT) * factor).astype(BF)
        dquery = (dot(key, dscores) * factor).astype(BF)
        dmixed[at, :] = dquery
        dmixed[width + h * HD : width + (h + 1) * HD, :] = dkey
        dmixed[2 * width + h * HD : 2 * width + (h + 1) * HD, :] = dvalue
        dquery_sum[at, :] += fold(dquery)
        dvalue_sum[at, :] += fold(dvalue)

    @pl.when(step == pl.num_programs(0) - 1)
    def _():
        sums[...] = jnp.zeros(sums.shape, F32)
        sums[0:1] = row_sum(dquery_sum[...].T)
        sums[1:2] = row_sum(dvalue_sum[...].T)


def joint_grad_kernel(dest, first_t, dmixed, out_grad, keep, send, grads, sems):
    width = first_t.shape[0]
    depth = width // ROW_TILES
    span = dmixed.shape[0]
    piece = width // COL_TILES
    step = pl.program_id(0)
    grads[step, :, 0:span] = dot_general(first_t[...], dmixed[...], NT).astype(BF)

    @pl.when(step == pl.num_programs(0) - 1)
    def _():
        for s in range(COL_TILES):
            grads[s, :, span:] = out_grad[:, s * piece : (s + 1) * piece]
        copies = []
        for i in range(PIECES):
            place = dest[i]
            m = lax.div(place, COL_TILES)
            near = grads.at[
                lax.rem(place, COL_TILES), pl.ds(pl.multiple_of(m * depth, 16), depth), :
            ]
            far = keep.at[i] if i < HALF else send.at[i - HALF]
            copies.append(pltpu.make_async_copy(near, far, sems.at[i]))
        for copy in copies:
            copy.start()
        for copy in copies:
            copy.wait()


def input_grad_kernel(
    dest, images, dresid, dmixed, table, own, other, image_grad, sums, weights, sems
):
    width = images.shape[-1]
    span = 3 * width // COL_TILES

    @pl.when(pl.program_id(0) == 0)
    def _():
        stage_joint(dest, own, other, weights, sems)
        sums[...] = jnp.zeros(sums.shape, F32)

    back = None
    for s in range(COL_TILES):
        part = dot(
            joint_columns(weights, s, width)[:, :span], dmixed[s * span : (s + 1) * span, :]
        )
        back = part if back is None else back + part
    upstream = back.T
    normed, inverse = normalize(images[0].astype(F32))
    sums[0:1] += row_sum(upstream * normed)
    sums[1:2] += row_sum(upstream)
    image_grad[0] = dresid[...] + norm_back(upstream, normed, inverse, table[0:1])


def flat_pairs(fsdp, sub, there):
    return [(f * sub + s, there(f, s)) for f in range(fsdp) for s in range(sub)]


class Cube:
    def __init__(self):
        def along_z(k):
            return flat_pairs(8, 4, lambda f, s: (f ^ (2 * k)) * 4 + s)

        def y_or_x(order):
            def there(f, s):
                turn = (s % 2) ^ order
                return (f * 4 + (s ^ 2)) if turn else ((f ^ 1) * 4 + s)

            return flat_pairs(8, 4, there)

        self.z = [along_z(k) for k in (1, 2, 3)]
        self.plane = [y_or_x(0), y_or_x(1)]
        self.core = flat_pairs(8, 4, lambda f, s: f * 4 + (s ^ 1))
        self.y = flat_pairs(8, 4, lambda f, s: (f ^ 1) * 4 + s)
        self.x = flat_pairs(8, 4, lambda f, s: f * 4 + (s ^ 2))

    def swap(self, value, pairs):
        return lax.ppermute(value, BOTH, pairs)

    def places(self):
        f = lax.axis_index("fsdp")
        s = lax.axis_index("sub")
        z, y, x, c = f // 2, f % 2, s // 2, s % 2

        def slot_to_place(i):
            core = c ^ (i // 16)
            far, near, dz = (i // 8) % 2, (i // 4) % 2, i % 4
            dy = jnp.where(core == 0, near, far)
            dx = jnp.where(core == 0, far, near)
            return ((z ^ dz) * 2 + (y ^ dy)) * 4 + (x ^ dx) * 2 + core

        def place_to_slot(p):
            pf, ps = p // 4, p % 4
            core = ps % 2
            dz, dy, dx = z ^ (pf // 2), y ^ (pf % 2), x ^ (ps // 2)
            near = jnp.where(core == 0, dy, dx)
            far = jnp.where(core == 0, dx, dy)
            return (c ^ core) * 16 + far * 8 + near * 4 + dz

        index = jnp.arange(PIECES, dtype=jnp.int32)
        return slot_to_place(index), place_to_slot(index)

    def gather(self, piece):
        four = jnp.stack([piece] + [self.swap(piece, pairs) for pairs in self.z])
        eight = jnp.concatenate([four, self.swap(four, self.plane[0])])
        own = jnp.concatenate([eight, self.swap(eight, self.plane[1])])
        return own, self.swap(own, self.core)

    def reduce(self, keep, send):
        def add(*terms):
            return sum(term.astype(F32) for term in terms).astype(BF)

        got = self.swap(send, self.core)
        low, high = add(keep[:8], got[:8]), add(keep[8:], got[8:])
        got = self.swap(high, self.plane[1])
        low, high = add(low[:4], got[:4]), add(low[4:], got[4:])
        got = self.swap(high, self.plane[0])
        four = [add(low[k], got[k]) for k in range(4)]
        total = four[0].astype(F32)
        for k in (1, 2, 3):
            total = total + self.swap(four[k], self.z[k - 1]).astype(F32)
        return total

    def total(self, value):
        for pairs in (self.core, self.x, self.y, self.z[0], self.z[1]):
            value = value + self.swap(value, pairs)
        return value


def gather_vectors(cube, slot_of, vectors):
    short = vectors[0].shape[0]
    if cube is None:
        full = [lax.all_gather(v, BOTH, axis=0, tiled=True).astype(F32) for v in vectors]
        return full
    flat = jnp.concatenate(vectors)
    piece = jnp.pad(flat, (0, 1024 - flat.shape[0])).reshape(8, 128)
    own, other = cube.gather(piece)
    every = jnp.concatenate([own, other]).reshape(PIECES, 1024)
    pick = (slot_of[:, None] == jnp.arange(PIECES)[None, :]).astype(BF)
    every = dot(pick, every)
    full = []
    at = 0
    for vector in vectors:
        full.append(every[:, at : at + vector.shape[0]].reshape(-1))
        at += vector.shape[0]
    return full


def shards(
    images,
    counts,
    joint_weight,
    out_weight,
    up_weight,
    down_weight,
    first_gain,
    first_shift,
    query_bias,
    value_bias,
    out_bias,
    first_scale,
    second_gain,
    second_shift,
    up_bias,
    down_bias,
    second_scale,
    cotangent,
    sizes,
):
    fsdp, sub = sizes
    cube = Cube() if (fsdp, sub) == (8, 4) else None
    images_here, length, width = images.shape
    heads = width // HD
    rows = images_here * length
    hidden_units = up_weight.shape[1] * sub
    depth = width // ROW_TILES
    span = 3 * width // COL_TILES
    piece = width // COL_TILES
    part = hidden_units // PARTS
    lane = part // ROW_TILES
    steps = COL_TILES

    if cube is not None:
        dest, slot_of = cube.places()
        first_piece = jnp.concatenate([joint_weight, out_weight], axis=1)
        up_parts = up_weight.reshape(depth, 2, PARTS, lane)
        down_parts = down_weight.T.reshape(2, depth, PARTS, lane)
        feed_piece = jnp.concatenate(
            [
                jnp.concatenate(
                    [
                        up_parts[:, :, j].reshape(depth, 2 * lane),
                        down_parts[:, :, j].transpose(1, 0, 2).reshape(depth, 2 * lane),
                    ]
                )
                for j in range(PARTS)
            ]
        )
        own_first, other_first = cube.gather(first_piece)
        own_feed, other_feed = cube.gather(feed_piece)
    else:
        dest = jnp.arange(PIECES, dtype=jnp.int32)
        slot_of = dest

        def fetch(value):
            return lax.all_gather(
                lax.all_gather(value, "sub", axis=1, tiled=True), "fsdp", axis=0, tiled=True
            )

        def cut(value, columns):
            value = value.reshape(ROW_TILES, depth, COL_TILES, columns)
            return value.transpose(0, 2, 1, 3).reshape(PIECES, depth, columns)

        first_pieces = jnp.concatenate(
            [cut(fetch(joint_weight), span), cut(fetch(out_weight), piece)], axis=2
        )
        up_parts = fetch(up_weight).reshape(ROW_TILES, depth, COL_TILES, 2, PARTS, lane)
        up_parts = up_parts.transpose(0, 2, 4, 1, 3, 5)
        down_parts = fetch(down_weight).reshape(ROW_TILES, PARTS, lane, COL_TILES, 2, depth)
        down_parts = down_parts.transpose(0, 3, 1, 5, 4, 2)
        shape = (PIECES, PARTS, depth, 2 * lane)
        feed_pieces = jnp.concatenate(
            [up_parts.reshape(shape), down_parts.reshape(shape)], axis=2
        ).reshape(PIECES, PARTS * 2 * depth, 2 * lane)
        own_first, other_first = first_pieces[:HALF], first_pieces[HALF:]
        own_feed, other_feed = feed_pieces[:HALF], feed_pieces[HALF:]

    (
        gain_one,
        shift_one,
        query_add,
        value_add,
        out_add,
        scale_one,
        gain_two,
        shift_two,
        up_add,
        down_add,
        scale_two,
    ) = gather_vectors(
        cube,
        slot_of,
        (
            first_gain,
            first_shift,
            query_bias,
            value_bias,
            out_bias,
            first_scale,
            second_gain,
            second_shift,
            up_bias,
            down_bias,
            second_scale,
        ),
    )
    table = jnp.stack(
        [
            gain_one,
            shift_one,
            query_add,
            value_add,
            out_add,
            scale_one,
            gain_two,
            shift_two,
            down_add,
            scale_two,
        ]
    )
    joint_bias = jnp.concatenate([query_add, jnp.zeros_like(query_add), value_add])
    joint_bias = jnp.pad(joint_bias.reshape(COL_TILES, span), ((0, 0), (0, piece)))
    up_rows = up_add.reshape(ROW_TILES, PARTS, lane).transpose(1, 0, 2)
    up_rows = up_rows.reshape(PARTS, steps, 2 * lane)

    def sds(shape, dtype):
        return jax.ShapeDtypeStruct(shape, dtype)

    image_block = pl.BlockSpec((1, length, width), lambda i, *_: (i, 0, 0))
    row_block = pl.BlockSpec((length, width), lambda i, *_: (i, 0))
    column_block = pl.BlockSpec((width, length), lambda i, *_: (0, i))
    mixed_block = pl.BlockSpec((3 * width, length), lambda i, *_: (0, i))
    probs_block = pl.BlockSpec((1, heads, length, length), lambda i, *_: (i, 0, 0, 0))
    table_spec = whole(table.shape)
    joint_scratch = [
        pltpu.VMEM((COL_TILES, ROW_TILES, depth, width), BF),
        pltpu.SemaphoreType.DMA((PIECES,)),
    ]

    mixed, first_t = pl.pallas_call(
        qkv_kernel,
        grid_spec=pltpu.PrefetchScalarGridSpec(
            num_scalar_prefetch=1,
            grid=(images_here,),
            in_specs=[image_block, table_spec, whole(joint_bias.shape), ANY, ANY],
            out_specs=[mixed_block, column_block],
            scratch_shapes=joint_scratch,
        ),
        out_shape=[sds((3 * width, rows), BF), sds((width, rows), BF)],
        compiler_params=params(),
        cost_estimate=cost(2 * rows * width * 3 * width, 14 * rows * width),
        name="qkv",
    )(dest, images, table, joint_bias, own_first, other_first)

    attended, probs = pl.pallas_call(
        attention_kernel,
        grid_spec=pltpu.PrefetchScalarGridSpec(
            num_scalar_prefetch=1,
            grid=(images_here,),
            in_specs=[mixed_block],
            out_specs=[column_block, probs_block],
        ),
        out_shape=[
            sds((width, rows), BF),
            sds((images_here, heads, length, length), BF),
        ],
        compiler_params=params(),
        cost_estimate=cost(16 * rows * width * length, 8 * rows * width),
        name="attention",
    )(counts, mixed)

    resid, branch, second, second_t, dfeed, dfeed_t, out_full = pl.pallas_call(
        second_kernel,
        grid_spec=pltpu.PrefetchScalarGridSpec(
            num_scalar_prefetch=2,
            grid=(images_here,),
            in_specs=[image_block, image_block, column_block, table_spec, ANY, ANY],
            out_specs=[
                row_block,
                row_block,
                row_block,
                column_block,
                row_block,
                column_block,
                whole_out((width, width)),
            ],
            scratch_shapes=joint_scratch,
        ),
        out_shape=[
            sds((rows, width), F32),
            sds((rows, width), BF),
            sds((rows, width), BF),
            sds((width, rows), BF),
            sds((rows, width), BF),
            sds((width, rows), BF),
            sds((width, width), BF),
        ],
        compiler_params=params(),
        cost_estimate=cost(2 * rows * width * width, 20 * rows * width),
        name="second_norm",
    )(dest, counts, images, cotangent, attended, table, own_first, other_first)

    feed = dsecond = None
    up_sums = []
    feed_grads = []
    square = (rows, width)
    for j in range(PARTS):
        start = j == 0
        extra = [] if start else [feed, dsecond]
        feed, dsecond, bias_sum, keep, send = pl.pallas_call(
            functools.partial(mlp_kernel, start, 1, j * 2 * depth),
            grid_spec=pltpu.PrefetchScalarGridSpec(
                num_scalar_prefetch=1,
                grid=(steps,),
                in_specs=[
                    whole(square),
                    whole((width, rows)),
                    whole(square),
                    whole((width, rows)),
                    whole((steps, 2 * lane)),
                    ANY,
                    ANY,
                ]
                + [whole(square)] * len(extra),
                out_specs=[
                    whole_out(square),
                    whole_out(square),
                    whole_out((steps, 2 * lane)),
                    ANY,
                    ANY,
                ],
                scratch_shapes=[
                    pltpu.VMEM((steps, width, 2 * lane), BF),
                    pltpu.VMEM((steps, width, 2 * lane), BF),
                    pltpu.VMEM((steps, width, 2 * lane), BF),
                    pltpu.VMEM((steps, width, 2 * lane), BF),
                    pltpu.SemaphoreType.DMA((PIECES,)),
                ],
            ),
            out_shape=[
                sds(square, F32),
                sds(square, F32),
                sds((steps, 2 * lane), F32),
                sds((HALF, 2 * depth, 2 * lane), BF),
                sds((HALF, 2 * depth, 2 * lane), BF),
            ],
            compiler_params=params(),
            cost_estimate=cost(12 * rows * width * part, 20 * rows * width),
            name="feed_forward",
        )(
            dest,
            second,
            second_t,
            dfeed,
            dfeed_t,
            up_rows[j],
            own_feed,
            other_feed,
            *extra,
        )
        up_sums.append(bias_sum.reshape(ROW_TILES, lane))
        feed_grads.append((keep, send))

    block_out, dresid, dattended, out_grad, middle_sums = pl.pallas_call(
        middle_kernel,
        grid_spec=pltpu.PrefetchScalarGridSpec(
            num_scalar_prefetch=1,
            grid=(images_here,),
            in_specs=[
                image_block,
                row_block,
                row_block,
                row_block,
                row_block,
                column_block,
                whole((width, width)),
                table_spec,
            ],
            out_specs=[
                image_block,
                row_block,
                column_block,
                whole_out((width, width)),
                whole_out((8, width)),
            ],
            scratch_shapes=[pltpu.VMEM((width, width), F32)],
        ),
        out_shape=[
            sds(images.shape, BF),
            sds((rows, width), F32),
            sds((width, rows), BF),
            sds((width, width), BF),
            sds((8, width), F32),
        ],
        compiler_params=params(),
        cost_estimate=cost(4 * rows * width * width, 30 * rows * width),
        name="middle",
    )(counts, cotangent, feed, dsecond, resid, branch, attended, out_full, table)

    dmixed, attention_sums = pl.pallas_call(
        attention_back_kernel,
        grid=(images_here,),
        in_specs=[mixed_block, probs_block, column_block, column_block],
        out_specs=[mixed_block, whole_out((8, width))],
        scratch_shapes=[pltpu.VMEM((width, 128), F32), pltpu.VMEM((width, 128), F32)],
        out_shape=[sds((3 * width, rows), BF), sds((8, width), F32)],
        compiler_params=params(),
        cost_estimate=cost(32 * rows * width * length, 18 * rows * width),
        name="attention_back",
    )(mixed, probs, attended, dattended)

    keep_first, send_first = pl.pallas_call(
        joint_grad_kernel,
        grid_spec=pltpu.PrefetchScalarGridSpec(
            num_scalar_prefetch=1,
            grid=(COL_TILES,),
            in_specs=[
                whole((width, rows)),
                pl.BlockSpec((span, rows), lambda s, *_: (s, 0)),
                whole((width, width)),
            ],
            out_specs=[ANY, ANY],
            scratch_shapes=[
                pltpu.VMEM((COL_TILES, width, width), BF),
                pltpu.SemaphoreType.DMA((PIECES,)),
            ],
        ),
        out_shape=[sds((HALF, depth, width), BF), sds((HALF, depth, width), BF)],
        compiler_params=params(),
        cost_estimate=cost(6 * rows * width * width, 10 * rows * width),
        name="joint_grad",
    )(dest, first_t, dmixed, out_grad)

    image_grad, input_sums = pl.pallas_call(
        input_grad_kernel,
        grid_spec=pltpu.PrefetchScalarGridSpec(
            num_scalar_prefetch=1,
            grid=(images_here,),
            in_specs=[image_block, row_block, mixed_block, table_spec, ANY, ANY],
            out_specs=[image_block, whole_out((8, width))],
            scratch_shapes=joint_scratch,
        ),
        out_shape=[sds(images.shape, F32), sds((8, width), F32)],
        compiler_params=params(),
        cost_estimate=cost(6 * rows * width * width, 20 * rows * width),
        name="input_grad",
    )(dest, images, dresid, dmixed, table, own_first, other_first)

    up_bias_grad = jnp.stack(up_sums, axis=1).reshape(-1)
    sums = jnp.concatenate(
        [
            input_sums[0:2],
            attention_sums[0:2],
            middle_sums[0:6],
            up_bias_grad.reshape(-1, width),
            jnp.zeros((2, width), F32),
        ]
    )
    short = first_gain.shape[0]
    if cube is not None:
        first_total = cube.reduce(keep_first, send_first)
        feed_total = cube.reduce(
            jnp.concatenate([k for k, _ in feed_grads], axis=1),
            jnp.concatenate([s for _, s in feed_grads], axis=1),
        )
        joint_grad, out_weight_grad = first_total[:, :span], first_total[:, span:]
        feed_total = feed_total.reshape(PARTS, 2, depth, 2, lane)
        up_grad = feed_total[:, 0].transpose(1, 2, 0, 3).reshape(up_weight.shape)
        down_grad = feed_total[:, 1].transpose(2, 1, 0, 3).reshape(down_weight.shape[::-1]).T
        sums = cube.total(sums)
        device = lax.axis_index("fsdp") * sub + lax.axis_index("sub")
        vectors = lax.dynamic_slice(sums[:10], (0, device * short), (10, short))
        up_bias_grad = lax.dynamic_slice(
            sums[10:14].reshape(-1), (device * up_bias.shape[0],), up_bias.shape
        )
    else:

        def hand_out(value):
            value = lax.psum_scatter(value.astype(BF), "fsdp", scatter_dimension=0, tiled=True)
            value = lax.psum_scatter(value, "sub", scatter_dimension=1, tiled=True)
            return value.astype(F32)

        def join(value, columns):
            value = value.reshape(ROW_TILES, COL_TILES, depth, columns)
            return value.transpose(0, 2, 1, 3).reshape(width, COL_TILES * columns)

        grads = jnp.concatenate([keep_first, send_first])
        joint_grad = hand_out(join(grads[:, :, :span], span))
        out_weight_grad = hand_out(join(grads[:, :, span:], piece))
        grads = jnp.stack([jnp.concatenate(pair) for pair in feed_grads], axis=1)
        grads = grads.reshape(ROW_TILES, COL_TILES, PARTS, 2, depth, 2, lane)
        up_grad = grads[:, :, :, 0].transpose(0, 3, 1, 4, 2, 5).reshape(width, hidden_units)
        down_grad = grads[:, :, :, 1].transpose(0, 2, 5, 1, 4, 3).reshape(hidden_units, width)
        up_grad, down_grad = hand_out(up_grad), hand_out(down_grad)

        def hand_vector(value):
            return lax.psum_scatter(value, BOTH, scatter_dimension=0, tiled=True)

        vectors = [hand_vector(sums[v]) for v in range(10)]
        up_bias_grad = hand_vector(up_bias_grad)
    return (
        block_out,
        image_grad,
        joint_grad,
        out_weight_grad,
        up_grad,
        down_grad,
        vectors[0],
        vectors[1],
        vectors[2],
        vectors[3],
        vectors[4],
        vectors[5],
        vectors[6],
        vectors[7],
        up_bias_grad,
        vectors[8],
        vectors[9],
    )


def solution(mesh):
    rows = P(BOTH, None, None)
    matrix = P("fsdp", "sub")
    vector = P(BOTH)
    sizes = (mesh.shape["fsdp"], mesh.shape["sub"])
    return jax.shard_map(
        functools.partial(shards, sizes=sizes),
        mesh=mesh,
        in_specs=(rows, vector) + (matrix,) * 4 + (vector,) * 11 + (rows,),
        out_specs=(rows, rows) + (matrix,) * 4 + (vector,) * 11,
        check_vma=False,
    )
```

```python
import functools
import math

import jax
import jax.numpy as jnp
from jax import lax
from jax.experimental import pallas as pl
from jax.experimental.pallas import tpu as pltpu
from jax.sharding import PartitionSpec as P

HD = 64
EPS = 1e-06
NEGATIVE = -1e30
ROW_TILES = 8
COL_TILES = 4
PIECES = ROW_TILES * COL_TILES
HALF = PIECES // 2
GROUP = 4
GROUPS = PIECES // GROUP
VECTORS = 10
PARTS = 3
BOTH = ("fsdp", "sub")
SLACK = 100
VMEM_LIMIT = 56 * 1024 * 1024
BF = jnp.bfloat16
F32 = jnp.float32
NT = (((1,), (1,)), ((), ()))
TN = (((0,), (0,)), ((), ()))


def dot(left, right):
    return jnp.dot(left, right, preferred_element_type=F32)


def dot_general(left, right, dims):
    return lax.dot_general(left, right, dims, preferred_element_type=F32)


def launch(
    kernel, name, grid, scalars, ins, specs, outs, out_specs, scratch, price, after=(), aliases=None, covers=True
):
    known = len(scalars) + len(ins)

    def body(*refs):
        kernel(*refs[:known], *refs[known + len(after) :])

    return pl.pallas_call(
        body,
        grid_spec=pltpu.PrefetchScalarGridSpec(
            num_scalar_prefetch=len(scalars),
            grid=(grid,),
            in_specs=list(specs) + [ANY] * len(after),
            out_specs=list(out_specs),
            scratch_shapes=list(scratch),
        ),
        out_shape=[jax.ShapeDtypeStruct(shape, dtype) for shape, dtype in outs],
        input_output_aliases=aliases or {},
        compiler_params=pltpu.CompilerParams(
            dimension_semantics=("arbitrary",), vmem_limit_bytes=VMEM_LIMIT
        ),
        cost_estimate=pl.CostEstimate(
            flops=SLACK * price[0] if covers else 0, bytes_accessed=price[1], transcendentals=0
        ),
        name=name,
    )(*scalars, *ins, *after)


def normalize(rows):
    centre = rows - jnp.mean(rows, axis=-1, keepdims=True)
    spread = jnp.mean(centre * centre, axis=-1, keepdims=True)
    inverse = lax.rsqrt(spread + EPS)
    return (centre * inverse, inverse)


def norm_back(upstream, normed, inverse, gain):
    scaled = upstream * gain
    return inverse * (
        scaled
        - jnp.mean(scaled, axis=-1, keepdims=True)
        - normed * jnp.mean(scaled * normed, axis=-1, keepdims=True)
    )


def row_sum(values):
    return jnp.sum(values, axis=0, keepdims=True)


def whole(shape):
    zeros = (0,) * len(shape)
    return pl.BlockSpec(shape, lambda *_: zeros, pipeline_mode=pl.Buffered(1))


def whole_out(shape):
    zeros = (0,) * len(shape)
    return pl.BlockSpec(shape, lambda *_: zeros)


ANY = pl.BlockSpec(memory_space=pl.ANY)


def stage_pieces(places, sources, weights, sems, top=0):
    count = weights.shape[2]
    copies = []
    for i, place in enumerate(places):
        copies.append(
            pltpu.make_async_copy(
                sources(i).at[pl.ds(top, count), :],
                weights.at[lax.rem(place, COL_TILES), lax.div(place, COL_TILES)],
                sems.at[i],
            )
        )
    for copy in copies:
        copy.start()
    for copy in copies:
        copy.wait()


def grouped(dest, refs):
    return [dest[i] for i in range(PIECES)], lambda i: refs[i // GROUP].at[i % GROUP]


def columns_of(weights, s):
    _, tiles, depth, wide = weights.shape
    return weights[s].reshape(tiles * depth, wide)


def join_kernel(*refs):
    *pieces, out = refs
    for i, piece in enumerate(pieces):
        out[i] = piece[...]


def pack_first_kernel(joint_weight, *refs):
    *vectors, long, packed = refs
    depth, span = joint_weight.shape
    rest = packed.shape[1] - span
    packed[:, :span] = joint_weight[...]
    half = long.shape[0] // 2
    lines = [vector[...].astype(F32).reshape(1, -1) for vector in vectors]
    both = long[...].astype(F32).reshape(1, -1)
    lines += [both[:, :half], both[:, half:]]
    lines = [jnp.pad(line, ((0, 0), (0, rest - line.shape[1]))) for line in lines]
    lines.append(jnp.zeros((16 - len(lines), rest), F32))
    packed[:, span:] = jnp.zeros((depth, rest), BF)
    packed[0:16, span:] = jnp.concatenate(lines).astype(BF)


def pack_kernel(which, up_weight, down_t, out_weight, *refs):
    packed = refs[-1]
    depth, units = up_weight.shape
    lane = units // PARTS // 2
    span = out_weight.shape[1]
    at = 0
    for j in which:
        low = j * lane
        for h in range(2):
            lanes = slice(h * lane, (h + 1) * lane)
            packed[at : at + depth, lanes] = up_weight[
                :, h * units // 2 + low : h * units // 2 + low + lane
            ]
            packed[at + depth : at + 2 * depth, lanes] = down_t[
                h * depth : (h + 1) * depth, low : low + lane
            ]
        at += 2 * depth
        if j == 0:
            packed[at : at + depth, :] = jnp.zeros((depth, 2 * lane), BF)
            packed[at : at + depth, :span] = out_weight[...]
            at += depth


def add_kernel(low, high, got_low, got_high, low_out, high_out):
    low_out[...] = (low[...].astype(F32) + got_low[...].astype(F32)).astype(BF)
    high_out[...] = (high[...].astype(F32) + got_high[...].astype(F32)).astype(BF)


def add_four_kernel(keep, got, *outs):
    for k, out in enumerate(outs[-4:]):
        out[...] = (keep[k].astype(F32) + got[k].astype(F32)).astype(BF)


def sum_of(refs):
    return sum(ref[...].astype(F32) for ref in refs)


def late_total_kernel(*refs):
    refs[-1][...] = sum_of(refs[:-1])


def first_total_kernel(a, b, c, d, joint_grad, out_grad):
    total = sum_of((a, b, c, d))
    span = joint_grad.shape[1]
    joint_grad[...] = total[:, :span]
    out_grad[...] = total[:, span:]


def feed_total_kernel(*refs):
    *terms, up_grad, down_grad = refs
    depth, units = up_grad.shape
    lane = units // PARTS // 2
    total = jnp.concatenate([term[...].astype(F32) for term in terms])
    tall = []
    for j in range(PARTS):
        at = 2 * j * depth
        for h in range(2):
            lanes = slice(h * lane, (h + 1) * lane)
            low = h * units // 2 + j * lane
            up_grad[:, low : low + lane] = total[at : at + depth, lanes]
        at += depth
        tall.append(
            jnp.concatenate([total[at : at + depth, :lane], total[at : at + depth, lane:]])
        )
    wide = jnp.concatenate(tall, axis=1)
    down_grad[...] = wide


def normalize_kernel(images, normed_out, inverse_out):
    normed, inverse = normalize(images[0].astype(F32))
    normed_out[...] = normed
    inverse_out[...] = jnp.broadcast_to(inverse, inverse_out.shape)


def qkv_kernel(dest, normed, *refs):
    *sources, mixed, first_t, table, up_rows, weights, sems = refs
    width = normed.shape[-1]
    span = 3 * width // COL_TILES
    short = width // PIECES
    lane = 128

    @pl.when(pl.program_id(0) == 0)
    def _():
        stage_pieces(*grouped(dest, sources), weights, sems)
        lines = []
        long = []
        for place in range(PIECES):
            block = weights[place % COL_TILES, place // COL_TILES, 0:16, span:].astype(F32)
            lines.append(block[:, :short])
            long += [block[VECTORS : VECTORS + 1, : 2 * short]]
            long += [block[VECTORS + 1 : VECTORS + 2, : 2 * short]]
        table[...] = jnp.concatenate(lines, axis=1)
        long = jnp.concatenate(long, axis=1)
        for j in range(PARTS):
            for m in range(ROW_TILES):
                up_rows[j : j + 1, m * lane : (m + 1) * lane] = long[:, (m * PARTS + j) * lane : (m * PARTS + j + 1) * lane]

    bias = jnp.concatenate([table[2:3], jnp.zeros((1, width), F32), table[3:4]], axis=1)
    first = (normed[...] * table[0:1] + table[1:2]).astype(BF)
    first_t[...] = first.T
    for s in range(COL_TILES):
        out = dot(first, columns_of(weights, s)[:, :span])
        out = (out + bias[:, s * span : (s + 1) * span]).astype(BF)
        mixed[s * span : (s + 1) * span, :] = out.T


def attention_kernel(start, counts, mixed, *refs):
    attended, probs = refs[-2:]
    width = attended.shape[0]
    length = mixed.shape[1]
    scale = math.log2(math.e) / math.sqrt(HD)
    count = counts[pl.program_id(0) + start]
    valid = lax.broadcasted_iota(jnp.int32, (length, length), 0) < count
    for h in range(width // HD):
        query = mixed[h * HD : (h + 1) * HD, :]
        key = mixed[width + h * HD : width + (h + 1) * HD, :]
        value = mixed[2 * width + h * HD : 2 * width + (h + 1) * HD, :]
        scores = jnp.where(valid, dot_general(key, query, TN), NEGATIVE)
        largest = jnp.max(scores, axis=0, keepdims=True)
        expon = jnp.exp2((scores - largest) * scale)
        low = (expon * (1.0 / jnp.sum(expon, axis=0, keepdims=True))).astype(BF)
        probs[0, h] = low
        attended[h * HD : (h + 1) * HD, :] = dot(value, low).astype(BF)


def second_kernel(counts, images, cotangent, attended, table, pieces, *refs):
    resid_out, branch_out, second, second_t, dfeed_out, dfeed_t, out_full, weights, sems = refs
    width = images.shape[-1]
    length = images.shape[1]
    piece = width // COL_TILES

    @pl.when(pl.program_id(0) == 0)
    def _():
        top = 2 * width // ROW_TILES
        stage_pieces(range(PIECES), lambda i: pieces.at[i], weights, sems, top)
        for s in range(COL_TILES):
            out_full[:, s * piece : (s + 1) * piece] = columns_of(weights, s)[:, :piece]

    branch = dot_general(attended[...], out_full[...], TN) + table[4:5]
    branch_out[...] = branch.astype(BF)
    resid = images[0].astype(F32) + table[5:6] * branch
    resid_out[...] = resid
    normed, _ = normalize(resid)
    second_in = (normed * table[6:7] + table[7:8]).astype(BF)
    second[...] = second_in
    second_t[...] = second_in.T
    rows = lax.broadcasted_iota(jnp.int32, (length, 1), 0)
    mask = (rows < counts[pl.program_id(0)]).astype(F32)
    dfeed = (cotangent[0].astype(F32) * mask * table[9:10]).astype(BF)
    dfeed_out[...] = dfeed
    dfeed_t[...] = dfeed.T


def gelu_pair(value):
    size = jnp.abs(value)
    t = 1.0 / (1.0 + (0.3275911 / math.sqrt(2.0)) * size)
    bell = jnp.exp2(value * value * (-0.5 * math.log2(math.e)))
    poly = 0.5 * 1.061405429
    for c in (-1.453152027, 1.421413741, -0.284496736, 0.254829592):
        poly = poly * t + 0.5 * c
    tail = poly * t * bell
    cumul = jnp.where(value >= 0, 1.0 - tail, tail)
    return value * cumul, cumul + value * bell * (1.0 / math.sqrt(2.0 * math.pi))


def mlp_kernel(
    first, part, base, top, adopt, split, dest, bias, second, second_t, dfeed, dfeed_t, *rest
):
    gathered, rest = rest[0], rest[1:]
    if not first:
        carried, rest = rest[:2], rest[2:]
    if adopt:
        rest = rest[1:]
    feed, dsecond, bias_grad, *rest = rest
    if split:
        keep, send, *rest = rest
    else:
        grads, *rest = rest
    rows_in, rows_t, sums, up, down, hidden, dpre, up_grad, down_grad, *sems = rest
    up_sem, down_sem, row_sem, turned_sem, sum_sem, out_sem = sems
    count, width = second.shape
    depth = width // ROW_TILES
    span = width // COL_TILES
    lane = up.shape[-1] // ROW_TILES
    tile = 256
    tiles = count // tile

    def moves(place, buffer_up, buffer_down, outside, origin, sem_up, sem_down, inward):
        m = lax.div(place, COL_TILES)
        s = lax.rem(place, COL_TILES)
        copies = [
            (
                outside.at[pl.ds(origin, depth), :],
                buffer_up.at[
                    pl.ds(pl.multiple_of(m * depth, 16), depth),
                    pl.ds(pl.multiple_of(s * 2 * lane, 128), 2 * lane),
                ],
                sem_up,
            )
        ]
        for h in range(2):
            copies.append(
                (
                    outside.at[pl.ds(origin + depth, depth), pl.ds(h * lane, lane)],
                    buffer_down.at[
                        pl.ds(pl.multiple_of(s * span + h * depth, 16), depth),
                        pl.ds(pl.multiple_of(m * lane, 128), lane),
                    ],
                    sem_down,
                )
            )
        return [
            pltpu.make_async_copy(*((a, b) if inward else (b, a)), sem) for a, b, sem in copies
        ]

    def run(copies):
        for copy in copies:
            copy.start()
        return copies

    def row_copies(r, sources, targets, sem):
        rows = pl.ds(r * tile, tile)
        return [
            pltpu.make_async_copy(a.at[rows, :], b.at[rows, :], sem.at[i, r])
            for i, (a, b) in enumerate(zip(sources, targets))
        ]

    rows_in = (rows_in.at[0], rows_in.at[1])
    rows_t = (rows_t.at[0], rows_t.at[1])
    sums = (sums.at[0], sums.at[1])
    pieces = [
        moves(
            i,
            up,
            down,
            gathered.at[i],
            base,
            up_sem.at[i],
            down_sem.at[i],
            True,
        )
        for i in range(PIECES)
    ]
    arriving = [row_copies(r, (second, dfeed), rows_in, row_sem) for r in range(tiles)]
    turned = [
        pltpu.make_async_copy(a, b, turned_sem.at[i])
        for i, (a, b) in enumerate(zip((second_t, dfeed_t), rows_t))
    ]
    partial = [] if first else [row_copies(r, carried, sums, sum_sem) for r in range(tiles)]
    later = arriving[1:] + partial + [turned]
    for copies in pieces:
        run(copies[:1])
    run(arriving[0])
    for copies in pieces:
        run(copies[1:])
    for copies in pieces:
        copies[0].wait()
    add = bias[part : part + 1, :]
    total = jnp.zeros((1, up.shape[-1]), F32)
    for r in range(tiles):
        rows = slice(r * tile, (r + 1) * tile)
        for copy in arriving[r]:
            copy.wait()
        ahead = -(-len(later) // (tiles - r))
        for copies in later[:ahead]:
            run(copies)
        later = later[ahead:]
        pre = dot(rows_in[0][rows, :], up[...]) + add
        if r == 0:
            for copies in pieces:
                for copy in copies[1:]:
                    copy.wait()
        back = dot(rows_in[1][rows, :], down[...])
        value, slope = gelu_pair(pre)
        hidden[rows, :] = value.astype(BF)
        back = (back * slope).astype(BF)
        dpre[rows, :] = back
        total = total + row_sum(back.astype(F32))
    bias_grad[...] = total
    leaving = []
    for r in range(tiles):
        rows = slice(r * tile, (r + 1) * tile)
        forward = dot_general(hidden[rows, :], down[...], NT)
        back = dot_general(dpre[rows, :], up[...], NT)
        if not first:
            for copy in partial[r]:
                copy.wait()
            forward = forward + sums[0][rows, :].astype(F32)
            back = back + sums[1][rows, :].astype(F32)
        sums[0][rows, :] = forward.astype(BF)
        sums[1][rows, :] = back.astype(BF)
        leaving += run(row_copies(r, sums, (feed, dsecond), sum_sem))
    for copy in turned:
        copy.wait()
    up_grad[...] = dot(rows_t[0][...], dpre[...]).astype(BF)
    outs = [
        moves(
            dest[i] if split else i,
            up_grad,
            down_grad,
            (keep if i < HALF else send).at[i % HALF] if split else grads.at[i],
            top,
            out_sem.at[i],
            out_sem.at[i],
            False,
        )
        for i in range(PIECES)
    ]
    for copies in outs:
        leaving += run(copies[:1])
    down_grad[...] = dot(rows_t[1][...], hidden[...]).astype(BF)
    for copies in outs:
        leaving += run(copies[1:])
    for copy in leaving:
        copy.wait()


def middle_kernel(
    counts,
    cotangent,
    feed,
    dsecond,
    resid,
    branch,
    attended,
    out_full,
    table,
    block_out,
    dresid_out,
    dattended,
    out_grad,
    sums,
    total,
):
    length = cotangent.shape[1]
    step = pl.program_id(0)

    @pl.when(step == 0)
    def _():
        total[...] = jnp.zeros(total.shape, F32)
        sums[...] = jnp.zeros(sums.shape, F32)

    rows = lax.broadcasted_iota(jnp.int32, (length, 1), 0)
    mask = (rows < counts[step]).astype(F32)
    feed_out = feed[...].astype(F32) + table[8:9]
    grad = cotangent[0].astype(F32) * mask
    value = resid[...]
    block_out[0] = ((value + table[9:10] * feed_out) * mask).astype(BF)
    normed, inverse = normalize(value)
    upstream = dsecond[...].astype(F32)
    dresid = grad + norm_back(upstream, normed, inverse, table[6:7])
    dresid_out[...] = dresid
    dbranch = (dresid * table[5:6]).astype(BF)
    dfeed = (grad * table[9:10]).astype(BF)
    sums[0:1] += row_sum(dbranch.astype(F32))
    sums[1:2] += row_sum(dresid * branch[...].astype(F32))
    sums[2:3] += row_sum(upstream * normed)
    sums[3:4] += row_sum(upstream)
    sums[4:5] += row_sum(dfeed.astype(F32))
    sums[5:6] += row_sum(grad * feed_out)
    total[...] += dot(attended[...], dbranch)
    dattended[...] = dot_general(out_full[...], dbranch, NT).astype(BF)

    @pl.when(step == pl.num_programs(0) - 1)
    def _():
        out_grad[...] = total[...].astype(BF)


def attention_back_kernel(mixed, probs, attended, dattended, dmixed, sums, dquery_sum, dvalue_sum):
    width = attended.shape[0]
    length = mixed.shape[1]
    factor = 1.0 / math.sqrt(HD)
    step = pl.program_id(0)

    @pl.when(step == 0)
    def _():
        dquery_sum[...] = jnp.zeros(dquery_sum.shape, F32)
        dvalue_sum[...] = jnp.zeros(dvalue_sum.shape, F32)

    def fold(values):
        values = values.astype(F32)
        return sum(values[:, a : a + 128] for a in range(0, length, 128))

    for h in range(width // HD):
        at = slice(h * HD, (h + 1) * HD)
        query = mixed[h * HD : (h + 1) * HD, :]
        key = mixed[width + h * HD : width + (h + 1) * HD, :]
        value = mixed[2 * width + h * HD : 2 * width + (h + 1) * HD, :]
        upstream = dattended[at, :]
        low = probs[0, h]
        delta = row_sum(upstream.astype(F32) * attended[at, :].astype(F32))
        dprobs = dot_general(value, upstream, TN)
        dscores = (low.astype(F32) * (dprobs - delta)).astype(BF)
        dvalue = dot_general(upstream, low, NT).astype(BF)
        dkey = (dot_general(query, dscores, NT) * factor).astype(BF)
        dquery = (dot(key, dscores) * factor).astype(BF)
        dmixed[at, :] = dquery
        dmixed[width + h * HD : width + (h + 1) * HD, :] = dkey
        dmixed[2 * width + h * HD : 2 * width + (h + 1) * HD, :] = dvalue
        dquery_sum[at, :] += fold(dquery)
        dvalue_sum[at, :] += fold(dvalue)

    @pl.when(step == pl.num_programs(0) - 1)
    def _():
        sums[...] = jnp.zeros(sums.shape, F32)
        sums[0:1] = row_sum(dquery_sum[...].T)
        sums[1:2] = row_sum(dvalue_sum[...].T)


def joint_grad_kernel(offset, dest, first_t, dmixed, out_grad, out, grads, sems):
    width = first_t.shape[0]
    depth = width // ROW_TILES
    span = dmixed.shape[0]
    piece = width // COL_TILES
    step = pl.program_id(0)
    low = out_grad[:, 0:piece]
    high = out_grad[:, piece : 2 * piece]
    odd = lax.rem(dest[0] + offset, 2) == 1
    grads[step, :, span:] = jnp.where(odd, high, low)
    grads[step, :, 0:span] = dot_general(first_t[...], dmixed[...], NT).astype(BF)

    @pl.when(step == pl.num_programs(0) - 1)
    def _():
        copies = []
        for i in range(HALF):
            place = dest[offset * HALF + i]
            m = lax.div(place, COL_TILES)
            near = grads.at[
                lax.div(lax.rem(place, COL_TILES), 2),
                pl.ds(pl.multiple_of(m * depth, 16), depth),
                :,
            ]
            copies.append(pltpu.make_async_copy(near, out.at[i], sems.at[i]))
        for copy in copies:
            copy.start()
        for copy in copies:
            copy.wait()


def collect_kernel(input_sums, attention_sums, middle_sums, *refs):
    *bias_sums, out = refs
    lane = bias_sums[0].shape[1] // ROW_TILES
    out[0:2] = input_sums[0:2]
    out[2:4] = attention_sums[0:2]
    out[4:VECTORS] = middle_sums[0 : VECTORS - 4]
    out[VECTORS:] = jnp.zeros((16 - VECTORS, out.shape[1]), F32)
    for j, sums in enumerate(bias_sums):
        for m in range(ROW_TILES):
            at = (m * PARTS + j) * lane
            row, column = divmod(at, out.shape[1])
            out[VECTORS + row : VECTORS + row + 1, column : column + lane] = sums[
                :, m * lane : (m + 1) * lane
            ]


def input_grad_kernel(dest, normed, inverse, dresid, dmixed, table, *refs):
    *sources, image_grad, sums, weights, sems = refs
    width = normed.shape[-1]
    span = 3 * width // COL_TILES

    @pl.when(pl.program_id(0) == 0)
    def _():
        stage_pieces(*grouped(dest, sources), weights, sems)
        sums[...] = jnp.zeros(sums.shape, F32)

    back = None
    for s in range(COL_TILES):
        part = dot(
            columns_of(weights, s)[:, :span], dmixed[s * span : (s + 1) * span, :]
        )
        back = part if back is None else back + part
    upstream = back.T
    sums[0:1] += row_sum(upstream * normed[...])
    sums[1:2] += row_sum(upstream)
    image_grad[0] = dresid[...] + norm_back(upstream, normed[...], inverse[:, 0:1], table[0:1])


def flat_pairs(fsdp, sub, there):
    return [(f * sub + s, there(f, s)) for f in range(fsdp) for s in range(sub)]


class Cube:
    def __init__(self):
        def along_z(k):
            return flat_pairs(8, 4, lambda f, s: (f ^ (2 * k)) * 4 + s)

        def y_or_x(order):
            def there(f, s):
                turn = (s % 2) ^ order
                return (f * 4 + (s ^ 2)) if turn else ((f ^ 1) * 4 + s)

            return flat_pairs(8, 4, there)

        self.z = [along_z(k) for k in (1, 2, 3)]
        self.plane = [y_or_x(0), y_or_x(1)]
        self.core = flat_pairs(8, 4, lambda f, s: f * 4 + (s ^ 1))
        self.y = flat_pairs(8, 4, lambda f, s: (f ^ 1) * 4 + s)
        self.x = flat_pairs(8, 4, lambda f, s: f * 4 + (s ^ 2))

    def swap(self, value, pairs):
        return lax.ppermute(value, BOTH, pairs)

    def places(self):
        f = lax.axis_index("fsdp")
        s = lax.axis_index("sub")
        z, y, x, c = f // 2, f % 2, s // 2, s % 2

        def slot_to_place(i):
            core = c ^ (i // 16)
            far, near, dz = (i // 8) % 2, (i // 4) % 2, i % 4
            dy = jnp.where(core == 0, near, far)
            dx = jnp.where(core == 0, far, near)
            return ((z ^ dz) * 2 + (y ^ dy)) * 4 + (x ^ dx) * 2 + core

        index = jnp.arange(PIECES, dtype=jnp.int32)
        return slot_to_place(index)

    def near(self, value):
        return self.swap(value, self.plane[0])

    def far(self, value):
        return self.swap(value, self.plane[1])

    def over(self, value):
        return self.swap(value, self.core)

    def gather_z(self, piece):
        return (piece,) + tuple(self.swap(piece, pairs) for pairs in self.z)

    def reduce_z(self, four):
        return (four[0],) + tuple(self.swap(four[k], self.z[k - 1]) for k in (1, 2, 3))

    def total(self, value, stages):
        for pairs in stages:
            value = value + self.swap(value, pairs)
        return value


def join(pieces, after=()):
    shape = (len(pieces),) + pieces[0].shape
    return launch(
        join_kernel,
        "join",
        1,
        (),
        list(pieces),
        [whole(piece.shape) for piece in pieces],
        [(shape, BF)],
        [whole_out(shape)],
        (),
        (0, 4 * math.prod(shape)),
        after,
    )[0]


def gate_kernel(value, out):
    del value, out


def gate(value, after, covers=False):
    return launch(
        gate_kernel,
        "gate",
        1,
        (),
        [value],
        [ANY],
        [(value.shape, value.dtype)],
        [ANY],
        (),
        (10**8, 0),
        after,
        {0: 0},
        covers,
    )[0]


def add_halves(low, high, got, after=()):
    count = got.shape[0] // 2
    shift = count if high is None else 0
    steps = 2
    block = (count // steps,) + got.shape[1:]
    here = pl.BlockSpec(block, lambda i, *_: (i, 0, 0))
    there = pl.BlockSpec(block, lambda i, *_: (i + steps, 0, 0))
    shape = (count,) + got.shape[1:]
    return launch(
        add_kernel,
        "add",
        steps,
        (),
        [low, low if high is None else high, got, got],
        [here, there if shift else here, here, there],
        [(shape, BF), (shape, BF)],
        [here, here],
        (),
        (0, 12 * math.prod(shape)),
        after,
    )


def add_four(keep, got, after=(), held=()):
    shape = got.shape[1:]
    return launch(
        add_four_kernel,
        "add",
        1,
        (),
        [keep, got, *held],
        [whole(got.shape)] * 2 + [ANY] * len(held),
        [(v.shape, v.dtype) for v in held] + [(shape, BF)] * 4,
        [ANY] * len(held) + [whole_out(shape)] * 4,
        (),
        (0, 24 * math.prod(shape)),
        after,
        {2 + i: i for i in range(len(held))},
    )


def totals(kernel, name, terms, shapes, after=()):
    return launch(
        kernel,
        name,
        1,
        (),
        list(terms),
        [whole(term.shape) for term in terms],
        [(shape, F32) for shape in shapes],
        [whole_out(shape) for shape in shapes],
        (),
        (0, sum(2 * math.prod(term.shape) for term in terms)),
        after,
    )


def shards(
    images,
    counts,
    joint_weight,
    out_weight,
    up_weight,
    down_weight,
    first_gain,
    first_shift,
    query_bias,
    value_bias,
    out_bias,
    first_scale,
    second_gain,
    second_shift,
    up_bias,
    down_bias,
    second_scale,
    cotangent,
    sizes,
):
    fsdp, sub = sizes
    cube = Cube() if (fsdp, sub) == (8, 4) else None
    images_here, length, width = images.shape
    heads = width // HD
    rows = images_here * length
    hidden_units = up_weight.shape[1] * sub
    depth = width // ROW_TILES
    span = 3 * width // COL_TILES
    piece = width // COL_TILES
    part = hidden_units // PARTS
    lane = part // ROW_TILES
    steps = COL_TILES

    image_block = pl.BlockSpec((1, length, width), lambda i, *_: (i, 0, 0))
    row_block = pl.BlockSpec((length, width), lambda i, *_: (i, 0))
    column_block = pl.BlockSpec((width, length), lambda i, *_: (0, i))
    mixed_block = pl.BlockSpec((3 * width, length), lambda i, *_: (0, i))
    probs_block = pl.BlockSpec((1, heads, length, length), lambda i, *_: (i, 0, 0, 0))
    tall, wide = (rows, width), (width, rows)
    area = rows * width

    def input_norm(after):
        return launch(
            normalize_kernel,
            "first_norm",
            images_here,
            (),
            [images],
            [image_block],
            [(tall, F32), ((rows, 128), F32)],
            [row_block, pl.BlockSpec((length, 128), lambda i, *_: (i, 0))],
            (),
            (area * width, 8 * area),
            after,
            covers=False,
        )

    vectors = (first_gain, first_shift, query_bias, value_bias, out_bias, first_scale)
    vectors += (second_gain, second_shift, down_bias, second_scale)
    wide_span = span + 64

    if cube is not None:
        dest = cube.places()
        ins = [joint_weight, *vectors, up_bias]
        first_piece = launch(
            pack_first_kernel,
            "pack_first",
            1,
            (),
            ins,
            [whole(v.shape) for v in ins],
            [((depth, wide_span), BF)],
            [whole_out((depth, wide_span))],
            (),
            (0, 4 * depth * wide_span),
        )[0]

        def pack(which, after=(), held=()):
            height = (2 * len(which) + (which[0] == 0)) * depth
            ins = [up_weight, down_weight.T, out_weight]
            return launch(
                functools.partial(pack_kernel, which),
                "pack",
                1,
                (),
                [*ins, *held],
                [whole(v.shape) for v in ins] + [ANY] * len(held),
                [(v.shape, v.dtype) for v in held] + [((height, 2 * lane), BF)],
                [ANY] * len(held) + [whole_out((height, 2 * lane))],
                (),
                (0, 4 * height * lane),
                after,
                {len(ins) + i: i for i in range(len(held))},
            )

        four = join(cube.gather_z(first_piece))
        feed_piece = pack(tuple(range(PARTS)), ())[0]
        feed_pieces = lax.all_gather(feed_piece, BOTH, axis=0)
        near, far = cube.near(four), cube.far(four)
        normed_one, inverse_one = input_norm((four,))
        near = gate(near, (inverse_one,))
        far_near = cube.far(near)
        first = [four, near, far, far_near]
        first += [cube.over(v) for v in first]
        after_first = ()
    else:
        order = [p for p in range(PIECES) if p % 2 == 0] + [p for p in range(PIECES) if p % 2]
        back_order = [order.index(p) for p in range(PIECES)]
        dest = jnp.array(order, dtype=jnp.int32)
        normed_one, inverse_one = input_norm(())
        after_first = ()

        def fetch(value):
            return lax.all_gather(
                lax.all_gather(value, "sub", axis=1, tiled=True), "fsdp", axis=0, tiled=True
            )

        def cut(value, columns):
            value = value.reshape(ROW_TILES, depth, COL_TILES, columns)
            return value.transpose(0, 2, 1, 3).reshape(PIECES, depth, columns)

        def groups(value):
            value = jnp.stack([value[p] for p in order])
            return [value[i : i + GROUP] for i in range(0, PIECES, GROUP)]

        short = width // PIECES
        lines = [lax.all_gather(v, BOTH, axis=0, tiled=True) for v in vectors]
        lines = jnp.stack(lines).reshape(VECTORS, PIECES, short).transpose(1, 0, 2)
        lines = jnp.pad(lines, ((0, 0), (0, 0), (0, 64 - short)))
        long = lax.all_gather(up_bias, BOTH, axis=0, tiled=True).reshape(PIECES, 2, 2 * short)
        long = jnp.pad(long, ((0, 0), (0, 0), (0, 64 - 2 * short)))
        lines = jnp.concatenate([lines, long], axis=1)
        lines = jnp.pad(lines, ((0, 0), (0, depth - VECTORS - 2), (0, 0)))
        first = groups(jnp.concatenate([cut(fetch(joint_weight), span), lines], axis=2))
        out_pieces = jnp.pad(cut(fetch(out_weight), piece), ((0, 0), (0, 0), (0, 2 * lane - piece)))
        up_parts = fetch(up_weight).reshape(ROW_TILES, depth, COL_TILES, 2, PARTS, lane)
        up_parts = up_parts.transpose(0, 2, 4, 1, 3, 5)
        down_parts = fetch(down_weight).reshape(ROW_TILES, PARTS, lane, COL_TILES, 2, depth)
        down_parts = down_parts.transpose(0, 3, 1, 5, 4, 2)
        shape = (PIECES, PARTS, depth, 2 * lane)
        feed_pieces = jnp.concatenate([up_parts.reshape(shape), down_parts.reshape(shape)], axis=2)
        feed_pieces = [feed_pieces[:, 0], out_pieces, *(feed_pieces[:, j] for j in range(1, PARTS))]
        feed_pieces = jnp.concatenate(feed_pieces, axis=1)

    table_spec = whole((16, width))
    joint_scratch = [
        pltpu.VMEM((COL_TILES, ROW_TILES, depth, wide_span), BF),
        pltpu.SemaphoreType.DMA((PIECES,)),
    ]

    mixed, first_t, table, up_rows = launch(
        qkv_kernel,
        "qkv",
        images_here,
        (dest,),
        [normed_one, *first],
        [row_block] + [ANY] * GROUPS,
        [((3 * width, rows), BF), (wide, BF), ((16, width), F32), ((PARTS, part), F32)],
        [mixed_block, column_block, whole_out((16, width)), whole_out((PARTS, part))],
        joint_scratch,
        (6 * area * width, 14 * area),
        after_first,
        covers=False,
    )

    def attend(start, stop, into, after, covers):
        return launch(
            functools.partial(attention_kernel, start),
            "attention",
            stop - start,
            (counts,),
            [mixed, *into],
            [pl.BlockSpec((3 * width, length), lambda i, *_: (0, i + start))] + [ANY] * len(into),
            [(wide, BF), ((images_here, heads, length, length), BF)],
            [
                pl.BlockSpec((width, length), lambda i, *_: (0, i + start)),
                pl.BlockSpec((1, heads, length, length), lambda i, *_: (i + start, 0, 0, 0)),
            ],
            (),
            (16 * area * length // 2, 16 * area // 2),
            after,
            {2: 0, 3: 1} if into else None,
            covers,
        )

    attended, probs = attend(0, images_here, (), (), False)

    resid, branch, second, second_t, dfeed, dfeed_t, out_full = launch(
        second_kernel,
        "second_norm",
        images_here,
        (counts,),
        [images, cotangent, attended, table, feed_pieces],
        [image_block, image_block, column_block, table_spec, ANY],
        [(tall, F32), (tall, BF), (tall, BF), (wide, BF), (tall, BF), (wide, BF)]
        + [((width, width), BF)],
        [row_block, row_block, row_block, column_block, row_block, column_block]
        + [whole_out((width, width))],
        [
            pltpu.VMEM((COL_TILES, ROW_TILES, depth, 2 * lane), BF),
            pltpu.SemaphoreType.DMA((PIECES,)),
        ],
        (2 * area * width, 20 * area),
        covers=False,
    )

    def feed_forward(j, height, top, carried, adopted, split, after=()):
        base = 2 * j + (j > 0)
        ins = [up_rows, second, second_t, dfeed, dfeed_t, feed_pieces, *carried, *adopted]
        slots = (HALF if split else PIECES, height * 2 * depth, 2 * lane)
        both = pltpu.VMEM((width, part), BF)
        across = pltpu.VMEM((rows, part), BF)
        tiles = rows // 256
        return launch(
            functools.partial(
                mlp_kernel, not carried, j, base * depth, top * 2 * depth, bool(adopted), split
            ),
            "feed_forward",
            1,
            (dest,),
            ins,
            [whole(up_rows.shape)] + [ANY] * (len(ins) - 1),
            [(tall, BF), (tall, BF), ((1, part), F32)] + [(slots, BF)] * (1 + split),
            [ANY, ANY, whole_out((1, part))] + [ANY] * (1 + split),
            [
                pltpu.VMEM((2, rows, width), BF),
                pltpu.VMEM((2, width, rows), BF),
                pltpu.VMEM((2, rows, width), BF),
                both,
                both,
                across,
                across,
                both,
                both,
                pltpu.SemaphoreType.DMA((PIECES,)),
                pltpu.SemaphoreType.DMA((PIECES,)),
                pltpu.SemaphoreType.DMA((2, tiles)),
                pltpu.SemaphoreType.DMA((2,)),
                pltpu.SemaphoreType.DMA((2, tiles)),
                pltpu.SemaphoreType.DMA((PIECES,)),
            ],
            (12 * area * part, 20 * area),
            after,
            {len(ins): 3} if adopted else None,
        )

    bias_sums = []
    early = PARTS - 1
    early_grads = ()
    feed = dsecond = None
    for j in range(early):
        carried = (feed, dsecond) if j else ()
        feed, dsecond, bias_sum, *early_grads = feed_forward(
            j, early, j, carried, early_grads, False
        )
        bias_sums.append(bias_sum)
    feed, dsecond, bias_sum, *late_grads = feed_forward(
        early, 1, 0, (feed, dsecond), (), True, tuple(early_grads)
    )
    bias_sums.append(bias_sum)

    waits = {}
    if cube is not None:
        early_total = lax.psum_scatter(early_grads[0], BOTH, scatter_dimension=0)
        late_got = cube.over(late_grads[1])

    block_out, dresid, dattended, out_grad, middle_sums = launch(
        middle_kernel,
        "middle",
        images_here,
        (counts,),
        [cotangent, feed, dsecond, resid, branch, attended, out_full, table],
        [image_block, row_block, row_block, row_block, row_block, column_block]
        + [whole((width, width)), table_spec],
        [(images.shape, BF), (tall, F32), (wide, BF), ((width, width), BF), ((8, width), F32)],
        [image_block, row_block, column_block, whole_out((width, width)), whole_out((8, width))],
        [pltpu.VMEM((width, width), F32)],
        (4 * area * width, 30 * area),
        waits.get("middle", ()),
    )

    if cube is not None:
        late_low, late_high = add_halves(late_grads[0], None, late_got, (dresid,))
        late_got = cube.far(late_high)
        waits["attention_back"] = (late_high,)

    dmixed, attention_sums = launch(
        attention_back_kernel,
        "attention_back",
        images_here,
        (),
        [mixed, probs, attended, dattended],
        [mixed_block, probs_block, column_block, column_block],
        [((3 * width, rows), BF), ((8, width), F32)],
        [mixed_block, whole_out((8, width))],
        [pltpu.VMEM((width, 128), F32)] * 2,
        (32 * area * length, 24 * area),
        waits.get("attention_back", ()),
    )

    if cube is not None:
        late_low, late_high = add_halves(late_low, None, late_got, (dmixed,))
        late_got = cube.near(late_high)
        waits["joint_grad"] = (late_high,)

    def joint_grads(offset, after):
        def column_tile(g, dest):
            return (2 * g + lax.rem(dest[0] + offset, 2), 0)

        return launch(
            functools.partial(joint_grad_kernel, offset),
            "joint_grad",
            2,
            (dest,),
            [first_t, dmixed, out_grad],
            [
                whole(wide),
                pl.BlockSpec((span, rows), column_tile),
                pl.BlockSpec((width, width // 2), lambda g, *_: (0, g)),
            ],
            [((HALF, depth, width), BF)],
            [ANY],
            [pltpu.VMEM((2, width, width), BF), pltpu.SemaphoreType.DMA((HALF,))],
            (3 * area * width, 10 * area),
            after,
        )[0]

    send_first = joint_grads(1, waits.get("joint_grad", ()))
    if cube is not None:
        first_got = cube.over(send_first)
    keep_first = joint_grads(0, (send_first,))

    after_input = ()
    if cube is not None:
        late_last = add_four(late_low, late_got, (keep_first,))
        late_terms = cube.reduce_z(late_last)
        first_low, first_high = add_halves(keep_first, None, first_got, (late_last[0],))
        first_got = cube.far(first_high)
        after_input = (first_high,)

    image_grad, input_sums = launch(
        input_grad_kernel,
        "input_grad",
        images_here,
        (dest,),
        [normed_one, inverse_one, dresid, dmixed, table, *first],
        [row_block, pl.BlockSpec((length, 128), lambda i, *_: (i, 0)), row_block, mixed_block]
        + [table_spec]
        + [ANY] * GROUPS,
        [(images.shape, F32), ((8, width), F32)],
        [image_block, whole_out((8, width))],
        joint_scratch,
        (6 * area * width, 20 * area),
        after_input,
    )

    ins = [input_sums, attention_sums, middle_sums, *bias_sums]
    sums = launch(
        collect_kernel,
        "collect",
        1,
        (),
        ins,
        [whole(v.shape) for v in ins],
        [((16, width), F32)],
        [whole_out((16, width))],
        (),
        (0, 0),
    )[0]
    short = first_gain.shape[0]
    if cube is not None:
        late_total = totals(
            late_total_kernel, "late_total", late_terms, (late_terms[0].shape,), (image_grad,)
        )
        first_low, first_high = add_halves(first_low, None, first_got, (image_grad, *late_total))
        first_got = cube.near(first_high)
        sums = gate(sums, (first_high,), True)
        first_last = add_four(first_low, first_got, (sums,))
        first_terms = cube.reduce_z(first_last)
        sums = cube.total(sums, cube.z[:2])
        sums = gate(sums, first_last[:1], True)
        sums = cube.total(sums, (cube.core, cube.x, cube.y))
        up_grad, down_grad = totals(
            feed_total_kernel,
            "feed_total",
            (early_total, *late_total),
            (up_weight.shape, down_weight.shape[::-1]),
            (sums,),
        )
        down_grad = down_grad.T
        joint_grad, out_weight_grad = totals(
            first_total_kernel,
            "first_total",
            first_terms,
            (joint_weight.shape, out_weight.shape),
            (sums,),
        )
        device = lax.axis_index("fsdp") * sub + lax.axis_index("sub")
        vectors = lax.dynamic_slice(sums[:10], (0, device * short), (10, short))
        up_bias_grad = lax.dynamic_slice(
            sums[VECTORS : VECTORS + 4].reshape(-1), (device * up_bias.shape[0],), up_bias.shape
        )
    else:

        def hand_out(value):
            value = lax.psum_scatter(value.astype(BF), "fsdp", scatter_dimension=0, tiled=True)
            value = lax.psum_scatter(value, "sub", scatter_dimension=1, tiled=True)
            return value.astype(F32)

        def uncut(value, columns):
            value = value.reshape(ROW_TILES, COL_TILES, depth, columns)
            return value.transpose(0, 2, 1, 3).reshape(width, COL_TILES * columns)

        def in_order(value):
            return jnp.stack([value[i] for i in back_order])

        grads = in_order(jnp.concatenate([keep_first, send_first]))
        joint_grad = hand_out(uncut(grads[:, :, :span], span))
        out_weight_grad = hand_out(uncut(grads[:, :, span:], piece))
        late_grads = in_order(jnp.concatenate(late_grads))
        grads = jnp.concatenate([early_grads[0], late_grads], axis=1)
        grads = grads.reshape(ROW_TILES, COL_TILES, PARTS, 2, depth, 2, lane)
        up_grad = grads[:, :, :, 0].transpose(0, 3, 1, 4, 2, 5).reshape(width, hidden_units)
        down_grad = grads[:, :, :, 1].transpose(0, 2, 5, 1, 4, 3).reshape(hidden_units, width)
        up_grad, down_grad = hand_out(up_grad), hand_out(down_grad)

        def hand_vector(value):
            return lax.psum_scatter(value, BOTH, scatter_dimension=0, tiled=True)

        vectors = [hand_vector(sums[v]) for v in range(10)]
        up_bias_grad = hand_vector(sums[VECTORS : VECTORS + 4].reshape(-1))
    return (
        block_out,
        image_grad,
        joint_grad,
        out_weight_grad,
        up_grad,
        down_grad,
        vectors[0],
        vectors[1],
        vectors[2],
        vectors[3],
        vectors[4],
        vectors[5],
        vectors[6],
        vectors[7],
        up_bias_grad,
        vectors[8],
        vectors[9],
    )


def solution(mesh):
    rows = P(BOTH, None, None)
    matrix = P("fsdp", "sub")
    vector = P(BOTH)
    sizes = (mesh.shape["fsdp"], mesh.shape["sub"])
    return jax.shard_map(
        functools.partial(shards, sizes=sizes),
        mesh=mesh,
        in_specs=(rows, vector) + (matrix,) * 4 + (vector,) * 11 + (rows,),
        out_specs=(rows, rows) + (matrix,) * 4 + (vector,) * 11,
        check_vma=False,
    )
```

```python
import functools
import math

import jax
import jax.numpy as jnp
from jax import lax
from jax.experimental import pallas as pl
from jax.experimental.pallas import tpu as pltpu
from jax.sharding import PartitionSpec as P

HD = 64
EPS = 1e-06
NEGATIVE = -1e30
ROW_TILES = 8
COL_TILES = 4
PIECES = ROW_TILES * COL_TILES
HALF = PIECES // 2
GROUP = 4
GROUPS = PIECES // GROUP
VECTORS = 10
PARTS = 3
BOTH = ("fsdp", "sub")
LIGHT = 0.08
SLACK = 100
VMEM_LIMIT = 56 * 1024 * 1024
BF = jnp.bfloat16
F32 = jnp.float32
NT = (((1,), (1,)), ((), ()))
TN = (((0,), (0,)), ((), ()))


def dot(left, right):
    return jnp.dot(left, right, preferred_element_type=F32)


def dot_general(left, right, dims):
    return lax.dot_general(left, right, dims, preferred_element_type=F32)


def launch(
    kernel, name, grid, scalars, ins, specs, outs, out_specs, scratch, price, after=(), aliases=None, covers=1.0
):
    known = len(scalars) + len(ins)

    def body(*refs):
        kernel(*refs[:known], *refs[known + len(after) :])

    return pl.pallas_call(
        body,
        grid_spec=pltpu.PrefetchScalarGridSpec(
            num_scalar_prefetch=len(scalars),
            grid=(grid,),
            in_specs=list(specs) + [ANY] * len(after),
            out_specs=list(out_specs),
            scratch_shapes=list(scratch),
        ),
        out_shape=[jax.ShapeDtypeStruct(shape, dtype) for shape, dtype in outs],
        input_output_aliases=aliases or {},
        compiler_params=pltpu.CompilerParams(
            dimension_semantics=("arbitrary",), vmem_limit_bytes=VMEM_LIMIT
        ),
        cost_estimate=pl.CostEstimate(
            flops=int(SLACK * covers * price[0]), bytes_accessed=price[1], transcendentals=0
        ),
        name=name,
    )(*scalars, *ins, *after)


def normalize(rows):
    centre = rows - jnp.mean(rows, axis=-1, keepdims=True)
    spread = jnp.mean(centre * centre, axis=-1, keepdims=True)
    inverse = lax.rsqrt(spread + EPS)
    return (centre * inverse, inverse)


def norm_back(upstream, normed, inverse, gain):
    scaled = upstream * gain
    return inverse * (
        scaled
        - jnp.mean(scaled, axis=-1, keepdims=True)
        - normed * jnp.mean(scaled * normed, axis=-1, keepdims=True)
    )


def row_sum(values):
    return jnp.sum(values, axis=0, keepdims=True)


def whole(shape):
    zeros = (0,) * len(shape)
    return pl.BlockSpec(shape, lambda *_: zeros, pipeline_mode=pl.Buffered(1))


def whole_out(shape):
    zeros = (0,) * len(shape)
    return pl.BlockSpec(shape, lambda *_: zeros)


ANY = pl.BlockSpec(memory_space=pl.ANY)


def stage_pieces(places, sources, weights, sems, low=0):
    wide = weights.shape[-1]
    copies = []
    for i, place in enumerate(places):
        copies.append(
            pltpu.make_async_copy(
                sources(i).at[:, pl.ds(low, wide)],
                weights.at[lax.rem(place, COL_TILES), lax.div(place, COL_TILES)],
                sems.at[i],
            )
        )
    for copy in copies:
        copy.start()
    for copy in copies:
        copy.wait()


def grouped(dest, refs):
    return [dest[i] for i in range(PIECES)], lambda i: refs[i // GROUP].at[i % GROUP]


def columns_of(weights, s):
    _, tiles, depth, wide = weights.shape
    return weights[s].reshape(tiles * depth, wide)


def join_kernel(*refs):
    *pieces, out = refs
    for i, piece in enumerate(pieces):
        out[i] = piece[...]


def pack_first_kernel(joint_weight, out_weight, *refs):
    *vectors, long, packed = refs
    depth, span = joint_weight.shape
    rest = 64
    packed[:, :span] = joint_weight[...]
    packed[:, span + rest :] = jnp.zeros((depth, packed.shape[1] - span - rest), BF)
    packed[:, span + rest : span + rest + out_weight.shape[1]] = out_weight[...]
    half = long.shape[0] // 2
    lines = [vector[...].astype(F32).reshape(1, -1) for vector in vectors]
    both = long[...].astype(F32).reshape(1, -1)
    lines += [both[:, :half], both[:, half:]]
    lines = [jnp.pad(line, ((0, 0), (0, rest - line.shape[1]))) for line in lines]
    lines.append(jnp.zeros((16 - len(lines), rest), F32))
    packed[:, span : span + rest] = jnp.zeros((depth, rest), BF)
    packed[0:16, span : span + rest] = jnp.concatenate(lines).astype(BF)


def pack_kernel(up_weight, down_t, packed):
    depth, units = up_weight.shape
    lane = units // PARTS // 2
    for j in range(PARTS):
        at = 2 * j * depth
        low = j * lane
        for h in range(2):
            lanes = slice(h * lane, (h + 1) * lane)
            packed[at : at + depth, lanes] = up_weight[
                :, h * units // 2 + low : h * units // 2 + low + lane
            ]
            packed[at + depth : at + 2 * depth, lanes] = down_t[
                h * depth : (h + 1) * depth, low : low + lane
            ]


def add_kernel(low, high, got_low, got_high, low_out, high_out):
    low_out[...] = (low[...].astype(F32) + got_low[...].astype(F32)).astype(BF)
    high_out[...] = (high[...].astype(F32) + got_high[...].astype(F32)).astype(BF)


def add_four_kernel(keep, got, *outs):
    for k, out in enumerate(outs[-4:]):
        out[...] = (keep[k].astype(F32) + got[k].astype(F32)).astype(BF)


def sum_of(refs):
    return sum(ref[...].astype(F32) for ref in refs)


def late_total_kernel(*refs):
    refs[-1][...] = sum_of(refs[:-1])


def first_total_kernel(a, b, c, d, joint_grad, out_grad):
    total = sum_of((a, b, c, d))
    span = joint_grad.shape[1]
    joint_grad[...] = total[:, :span]
    out_grad[...] = total[:, span:]


def feed_total_kernel(*refs):
    *terms, up_grad, down_grad = refs
    depth, units = up_grad.shape
    lane = units // PARTS // 2
    total = jnp.concatenate([term[...].astype(F32) for term in terms])
    tall = []
    for j in range(PARTS):
        at = 2 * j * depth
        for h in range(2):
            lanes = slice(h * lane, (h + 1) * lane)
            low = h * units // 2 + j * lane
            up_grad[:, low : low + lane] = total[at : at + depth, lanes]
        at += depth
        tall.append(
            jnp.concatenate([total[at : at + depth, :lane], total[at : at + depth, lane:]])
        )
    wide = jnp.concatenate(tall, axis=1)
    down_grad[...] = wide


def normalize_kernel(images, normed_out, inverse_out):
    normed, inverse = normalize(images[0].astype(F32))
    normed_out[...] = normed
    inverse_out[...] = jnp.broadcast_to(inverse, inverse_out.shape)


def qkv_kernel(dest, normed, *refs):
    *sources, mixed, first_t, table, up_rows, weights, sems = refs
    width = normed.shape[-1]
    span = 3 * width // COL_TILES
    short = width // PIECES
    lane = 128

    @pl.when(pl.program_id(0) == 0)
    def _():
        stage_pieces(*grouped(dest, sources), weights, sems)
        lines = []
        long = []
        for place in range(PIECES):
            block = weights[place % COL_TILES, place // COL_TILES, 0:16, span:].astype(F32)
            lines.append(block[:, :short])
            long += [block[VECTORS : VECTORS + 1, : 2 * short]]
            long += [block[VECTORS + 1 : VECTORS + 2, : 2 * short]]
        table[...] = jnp.concatenate(lines, axis=1)
        long = jnp.concatenate(long, axis=1)
        for j in range(PARTS):
            for m in range(ROW_TILES):
                up_rows[j : j + 1, m * lane : (m + 1) * lane] = long[:, (m * PARTS + j) * lane : (m * PARTS + j + 1) * lane]

    bias = jnp.concatenate([table[2:3], jnp.zeros((1, width), F32), table[3:4]], axis=1)
    first = (normed[...] * table[0:1] + table[1:2]).astype(BF)
    first_t[...] = first.T
    for s in range(COL_TILES):
        out = dot(first, columns_of(weights, s)[:, :span])
        out = (out + bias[:, s * span : (s + 1) * span]).astype(BF)
        mixed[s * span : (s + 1) * span, :] = out.T


def attention_kernel(start, counts, mixed, *refs):
    attended, probs = refs[-2:]
    width = attended.shape[0]
    length = mixed.shape[1]
    scale = math.log2(math.e) / math.sqrt(HD)
    count = counts[pl.program_id(0) + start]
    valid = lax.broadcasted_iota(jnp.int32, (length, length), 0) < count
    for h in range(width // HD):
        query = mixed[h * HD : (h + 1) * HD, :]
        key = mixed[width + h * HD : width + (h + 1) * HD, :]
        scores = jnp.where(valid, dot_general(key, query, TN), NEGATIVE)
        largest = jnp.max(scores, axis=0, keepdims=True)
        expon = jnp.exp2((scores - largest) * scale)
        probs[0, h] = (expon * (1.0 / jnp.sum(expon, axis=0, keepdims=True))).astype(BF)
    for h in range(width // HD):
        value = mixed[2 * width + h * HD : 2 * width + (h + 1) * HD, :]
        attended[h * HD : (h + 1) * HD, :] = dot(value, probs[0, h]).astype(BF)


def second_kernel(dest, counts, images, cotangent, attended, table, *refs):
    sources, refs = refs[:GROUPS], refs[GROUPS:]
    resid_out, branch_out, second, second_t, dfeed_out, dfeed_t, out_full, weights, sems = refs
    width = images.shape[-1]
    length = images.shape[1]
    piece = width // COL_TILES

    @pl.when(pl.program_id(0) == 0)
    def _():
        low = 3 * width // COL_TILES + 64
        stage_pieces(*grouped(dest, sources), weights, sems, low)
        for s in range(COL_TILES):
            out_full[:, s * piece : (s + 1) * piece] = columns_of(weights, s)[:, :piece]

    branch = dot_general(attended[...], out_full[...], TN) + table[4:5]
    branch_out[...] = branch.astype(BF)
    resid = images[0].astype(F32) + table[5:6] * branch
    resid_out[...] = resid
    normed, _ = normalize(resid)
    second_in = (normed * table[6:7] + table[7:8]).astype(BF)
    second[...] = second_in
    second_t[...] = second_in.T
    rows = lax.broadcasted_iota(jnp.int32, (length, 1), 0)
    mask = (rows < counts[pl.program_id(0)]).astype(F32)
    dfeed = (cotangent[0].astype(F32) * mask * table[9:10]).astype(BF)
    dfeed_out[...] = dfeed
    dfeed_t[...] = dfeed.T


def gelu_pair(value):
    size = jnp.abs(value)
    t = 1.0 / (1.0 + (0.3275911 / math.sqrt(2.0)) * size)
    bell = jnp.exp2(value * value * (-0.5 * math.log2(math.e)))
    poly = 0.5 * 1.061405429
    for c in (-1.453152027, 1.421413741, -0.284496736, 0.254829592):
        poly = poly * t + 0.5 * c
    tail = poly * t * bell
    cumul = jnp.where(value >= 0, 1.0 - tail, tail)
    return value * cumul, cumul + value * bell * (1.0 / math.sqrt(2.0 * math.pi))


def mlp_kernel(parts, split, dest, bias, second, second_t, dfeed, dfeed_t, gathered, *rest):
    first = parts[0] == 0
    if not first:
        carried, rest = rest[:2], rest[2:]
    feed, dsecond, bias_grad, *rest = rest
    if split:
        keep, send, *rest = rest
    else:
        grads, *rest = rest
    rows_in, rows_t, sums, weights, hidden, dpre, weight_grads, *sems = rest
    piece_sem, row_sem, turned_sem, sum_sem, out_sem = sems
    count, width = second.shape
    depth = width // ROW_TILES
    span = width // COL_TILES
    wide = weights.shape[-1]
    lane = wide // ROW_TILES
    tile = 256
    tiles = count // tile

    def moves(place, buffer, outside, origin, sem, inward):
        m = lax.div(place, COL_TILES)
        s = lax.rem(place, COL_TILES)
        copies = [
            (
                outside.at[pl.ds(origin, depth), :],
                buffer.at[
                    0,
                    pl.ds(pl.multiple_of(m * depth, 16), depth),
                    pl.ds(pl.multiple_of(s * 2 * lane, 128), 2 * lane),
                ],
                sem.at[0],
            )
        ]
        for h in range(2):
            copies.append(
                (
                    outside.at[pl.ds(origin + depth, depth), pl.ds(h * lane, lane)],
                    buffer.at[
                        1,
                        pl.ds(pl.multiple_of(s * span + h * depth, 16), depth),
                        pl.ds(pl.multiple_of(m * lane, 128), lane),
                    ],
                    sem.at[1],
                )
            )
        return [
            pltpu.make_async_copy(*((a, b) if inward else (b, a)), sem) for a, b, sem in copies
        ]

    def run(copies):
        for copy in copies:
            copy.start()
        return copies

    def wait(copies):
        for copy in copies:
            copy.wait()

    def row_copies(r, sources, targets, sem):
        rows = pl.ds(r * tile, tile)
        return [
            pltpu.make_async_copy(a.at[rows, :], b.at[rows, :], sem.at[i, r])
            for i, (a, b) in enumerate(zip(sources, targets))
        ]

    rows_in = (rows_in.at[0], rows_in.at[1])
    rows_t = (rows_t.at[0], rows_t.at[1])
    sums = (sums.at[0], sums.at[1])

    def arrivals(n):
        every = [
            moves(
                i,
                weights.at[n],
                gathered.at[i],
                2 * depth * parts[n],
                piece_sem.at[n, i],
                True,
            )
            for i in range(PIECES)
        ]
        return [c[0] for c in every], [c for copies in every for c in copies[1:]]

    coming = [arrivals(n) for n in range(len(parts))]
    arriving = [row_copies(r, (second, dfeed), rows_in, row_sem) for r in range(tiles)]
    turned = [
        pltpu.make_async_copy(a, b, turned_sem.at[i])
        for i, (a, b) in enumerate(zip((second_t, dfeed_t), rows_t))
    ]
    partial = [] if first else [row_copies(r, carried, sums, sum_sem) for r in range(tiles)]
    later = arriving[1:] + partial + [turned] + [c for two in coming[1:] for c in two]
    run(coming[0][0])
    run(arriving[0])
    run(coming[0][1])
    leaving = []
    for n, part in enumerate(parts):
        up, down = weights.at[n, 0], weights.at[n, 1]
        up_grad, down_grad = weight_grads.at[n, 0], weight_grads.at[n, 1]
        wait(coming[n][0])
        add = bias[part : part + 1, :]
        total = jnp.zeros((1, wide), F32)
        for r in range(tiles):
            rows = slice(r * tile, (r + 1) * tile)
            if n == 0:
                wait(arriving[r])
                ahead = -(-len(later) // (tiles - r))
                for copies in later[:ahead]:
                    run(copies)
                later = later[ahead:]
            pre = dot(rows_in[0][rows, :], up[...]) + add
            if r == 0:
                wait(coming[n][1])
            back = dot(rows_in[1][rows, :], down[...])
            value, slope = gelu_pair(pre)
            hidden[rows, :] = value.astype(BF)
            back = (back * slope).astype(BF)
            dpre[rows, :] = back
            total = total + row_sum(back.astype(F32))
        bias_grad[n : n + 1, :] = total
        for r in range(tiles):
            rows = slice(r * tile, (r + 1) * tile)
            forward = dot_general(hidden[rows, :], down[...], NT)
            back = dot_general(dpre[rows, :], up[...], NT)
            if not first and n == 0:
                wait(partial[r])
            if not first or n > 0:
                forward = forward + sums[0][rows, :].astype(F32)
                back = back + sums[1][rows, :].astype(F32)
            sums[0][rows, :] = forward.astype(BF)
            sums[1][rows, :] = back.astype(BF)
            if n == len(parts) - 1:
                leaving += run(row_copies(r, sums, (feed, dsecond), sum_sem))
        if n == 0:
            wait(turned)
        up_grad[...] = dot(rows_t[0][...], dpre[...]).astype(BF)
        outs = [
            moves(
                dest[i] if split else i,
                weight_grads.at[n],
                (keep if i < HALF else send).at[i % HALF] if split else grads.at[i],
                2 * depth * n,
                out_sem.at[n, i],
                False,
            )
            for i in range(PIECES)
        ]
        for copies in outs:
            leaving += run(copies[:1])
        down_grad[...] = dot(rows_t[1][...], hidden[...]).astype(BF)
        for copies in outs:
            leaving += run(copies[1:])
    wait(leaving)


def middle_kernel(
    counts,
    cotangent,
    feed,
    dsecond,
    resid,
    branch,
    attended,
    out_full,
    table,
    block_out,
    dresid_out,
    dattended,
    out_grad,
    sums,
    total,
):
    length = cotangent.shape[1]
    step = pl.program_id(0)

    @pl.when(step == 0)
    def _():
        total[...] = jnp.zeros(total.shape, F32)
        sums[...] = jnp.zeros(sums.shape, F32)

    rows = lax.broadcasted_iota(jnp.int32, (length, 1), 0)
    mask = (rows < counts[step]).astype(F32)
    feed_out = feed[...].astype(F32) + table[8:9]
    grad = cotangent[0].astype(F32) * mask
    value = resid[...]
    block_out[0] = ((value + table[9:10] * feed_out) * mask).astype(BF)
    normed, inverse = normalize(value)
    upstream = dsecond[...].astype(F32)
    dresid = grad + norm_back(upstream, normed, inverse, table[6:7])
    dresid_out[...] = dresid
    dbranch = (dresid * table[5:6]).astype(BF)
    dfeed = (grad * table[9:10]).astype(BF)
    sums[0:1] += row_sum(dbranch.astype(F32))
    sums[1:2] += row_sum(dresid * branch[...].astype(F32))
    sums[2:3] += row_sum(upstream * normed)
    sums[3:4] += row_sum(upstream)
    sums[4:5] += row_sum(dfeed.astype(F32))
    sums[5:6] += row_sum(grad * feed_out)
    total[...] += dot(attended[...], dbranch)
    dattended[...] = dot_general(out_full[...], dbranch, NT).astype(BF)

    @pl.when(step == pl.num_programs(0) - 1)
    def _():
        out_grad[...] = total[...].astype(BF)


def attention_back_kernel(
    mixed, probs, attended, dattended, dmixed, sums, dquery_sum, dvalue_sum, dscores
):
    width = attended.shape[0]
    length = mixed.shape[1]
    heads = width // HD
    factor = 1.0 / math.sqrt(HD)
    step = pl.program_id(0)

    @pl.when(step == 0)
    def _():
        dquery_sum[...] = jnp.zeros(dquery_sum.shape, F32)
        dvalue_sum[...] = jnp.zeros(dvalue_sum.shape, F32)

    def part(block, h):
        return slice(block * width + h * HD, block * width + (h + 1) * HD)

    def fold(values):
        return sum(values[:, a : a + 128].astype(F32) for a in range(0, length, 128))

    def score_grads(h):
        upstream = dattended[part(0, h), :]
        delta = row_sum(upstream.astype(F32) * attended[part(0, h), :].astype(F32))
        dprobs = dot_general(mixed[part(2, h), :], upstream, TN)
        dscores[h] = (probs[0, h].astype(F32) * (dprobs - delta)).astype(BF)

    score_grads(0)
    for h in range(heads):
        if h + 1 < heads:
            score_grads(h + 1)
        dvalue = dot_general(dattended[part(0, h), :], probs[0, h], NT)
        dkey = dot_general(mixed[part(0, h), :], dscores[h], NT) * factor
        dquery = dot(mixed[part(1, h), :], dscores[h]) * factor
        dmixed[part(2, h), :] = dvalue.astype(BF)
        dmixed[part(1, h), :] = dkey.astype(BF)
        dmixed[part(0, h), :] = dquery.astype(BF)
    dquery_sum[...] += fold(dmixed[0:width, :])
    dvalue_sum[...] += fold(dmixed[2 * width :, :])

    @pl.when(step == pl.num_programs(0) - 1)
    def _():
        sums[...] = jnp.zeros(sums.shape, F32)
        sums[0:1] = row_sum(dquery_sum[...].T)
        sums[1:2] = row_sum(dvalue_sum[...].T)


def joint_grad_kernel(offset, dest, first_t, dmixed, out_grad, out, grads, sems):
    width = first_t.shape[0]
    depth = width // ROW_TILES
    span = dmixed.shape[0]
    piece = width // COL_TILES
    step = pl.program_id(0)
    low = out_grad[:, 0:piece]
    high = out_grad[:, piece : 2 * piece]
    odd = lax.rem(dest[0] + offset, 2) == 1
    grads[step, :, span:] = jnp.where(odd, high, low)
    grads[step, :, 0:span] = dot_general(first_t[...], dmixed[...], NT).astype(BF)

    @pl.when(step == pl.num_programs(0) - 1)
    def _():
        copies = []
        for i in range(HALF):
            place = dest[offset * HALF + i]
            m = lax.div(place, COL_TILES)
            near = grads.at[
                lax.div(lax.rem(place, COL_TILES), 2),
                pl.ds(pl.multiple_of(m * depth, 16), depth),
                :,
            ]
            copies.append(pltpu.make_async_copy(near, out.at[i], sems.at[i]))
        for copy in copies:
            copy.start()
        for copy in copies:
            copy.wait()


def collect_kernel(input_sums, attention_sums, middle_sums, *refs):
    *bias_sums, out = refs
    lane = bias_sums[0].shape[1] // ROW_TILES
    out[0:2] = input_sums[0:2]
    out[2:4] = attention_sums[0:2]
    out[4:VECTORS] = middle_sums[0 : VECTORS - 4]
    out[VECTORS:] = jnp.zeros((16 - VECTORS, out.shape[1]), F32)
    bias_rows = [sums[n : n + 1, :] for sums in bias_sums for n in range(sums.shape[0])]
    for j, sums in enumerate(bias_rows):
        for m in range(ROW_TILES):
            at = (m * PARTS + j) * lane
            row, column = divmod(at, out.shape[1])
            out[VECTORS + row : VECTORS + row + 1, column : column + lane] = sums[
                :, m * lane : (m + 1) * lane
            ]


def input_grad_kernel(dest, normed, inverse, dresid, dmixed, table, *refs):
    *sources, image_grad, sums, weights, sems = refs
    width = normed.shape[-1]
    span = 3 * width // COL_TILES

    @pl.when(pl.program_id(0) == 0)
    def _():
        stage_pieces(*grouped(dest, sources), weights, sems)
        sums[...] = jnp.zeros(sums.shape, F32)

    back = None
    for s in range(COL_TILES):
        part = dot(
            columns_of(weights, s)[:, :span], dmixed[s * span : (s + 1) * span, :]
        )
        back = part if back is None else back + part
    upstream = back.T
    sums[0:1] += row_sum(upstream * normed[...])
    sums[1:2] += row_sum(upstream)
    image_grad[0] = dresid[...] + norm_back(upstream, normed[...], inverse[:, 0:1], table[0:1])


def flat_pairs(fsdp, sub, there):
    return [(f * sub + s, there(f, s)) for f in range(fsdp) for s in range(sub)]


class Cube:
    def __init__(self):
        def along_z(k):
            return flat_pairs(8, 4, lambda f, s: (f ^ (2 * k)) * 4 + s)

        def y_or_x(order):
            def there(f, s):
                turn = (s % 2) ^ order
                return (f * 4 + (s ^ 2)) if turn else ((f ^ 1) * 4 + s)

            return flat_pairs(8, 4, there)

        self.z = [along_z(k) for k in (1, 2, 3)]
        self.plane = [y_or_x(0), y_or_x(1)]
        self.core = flat_pairs(8, 4, lambda f, s: f * 4 + (s ^ 1))
        self.y = flat_pairs(8, 4, lambda f, s: (f ^ 1) * 4 + s)
        self.x = flat_pairs(8, 4, lambda f, s: f * 4 + (s ^ 2))

    def swap(self, value, pairs):
        return lax.ppermute(value, BOTH, pairs)

    def places(self):
        f = lax.axis_index("fsdp")
        s = lax.axis_index("sub")
        z, y, x, c = f // 2, f % 2, s // 2, s % 2

        def slot_to_place(i):
            core = c ^ (i // 16)
            far, near, dz = (i // 8) % 2, (i // 4) % 2, i % 4
            dy = jnp.where(core == 0, near, far)
            dx = jnp.where(core == 0, far, near)
            return ((z ^ dz) * 2 + (y ^ dy)) * 4 + (x ^ dx) * 2 + core

        index = jnp.arange(PIECES, dtype=jnp.int32)
        return slot_to_place(index)

    def near(self, value):
        return self.swap(value, self.plane[0])

    def far(self, value):
        return self.swap(value, self.plane[1])

    def over(self, value):
        return self.swap(value, self.core)

    def gather_z(self, piece):
        return (piece,) + tuple(self.swap(piece, pairs) for pairs in self.z)

    def reduce_z(self, four):
        return (four[0],) + tuple(self.swap(four[k], self.z[k - 1]) for k in (1, 2, 3))

    def total(self, value, stages):
        for pairs in stages:
            value = value + self.swap(value, pairs)
        return value


def join(pieces, after=()):
    shape = (len(pieces),) + pieces[0].shape
    return launch(
        join_kernel,
        "join",
        1,
        (),
        list(pieces),
        [whole(piece.shape) for piece in pieces],
        [(shape, BF)],
        [whole_out(shape)],
        (),
        (0, 4 * math.prod(shape)),
        after,
    )[0]


def gate_kernel(value, out):
    del value, out


def gate(value, after, covers=0.0):
    return launch(
        gate_kernel,
        "gate",
        1,
        (),
        [value],
        [ANY],
        [(value.shape, value.dtype)],
        [ANY],
        (),
        (10**8, 0),
        after,
        {0: 0},
        covers,
    )[0]


def add_halves(low, high, got, after=()):
    count = got.shape[0] // 2
    shift = count if high is None else 0
    steps = 2
    block = (count // steps,) + got.shape[1:]
    here = pl.BlockSpec(block, lambda i, *_: (i, 0, 0))
    there = pl.BlockSpec(block, lambda i, *_: (i + steps, 0, 0))
    shape = (count,) + got.shape[1:]
    return launch(
        add_kernel,
        "add",
        steps,
        (),
        [low, low if high is None else high, got, got],
        [here, there if shift else here, here, there],
        [(shape, BF), (shape, BF)],
        [here, here],
        (),
        (0, 12 * math.prod(shape)),
        after,
    )


def add_four(keep, got, after=(), held=()):
    shape = got.shape[1:]
    return launch(
        add_four_kernel,
        "add",
        1,
        (),
        [keep, got, *held],
        [whole(got.shape)] * 2 + [ANY] * len(held),
        [(v.shape, v.dtype) for v in held] + [(shape, BF)] * 4,
        [ANY] * len(held) + [whole_out(shape)] * 4,
        (),
        (0, 24 * math.prod(shape)),
        after,
        {2 + i: i for i in range(len(held))},
    )


def totals(kernel, name, terms, shapes, after=()):
    return launch(
        kernel,
        name,
        1,
        (),
        list(terms),
        [whole(term.shape) for term in terms],
        [(shape, F32) for shape in shapes],
        [whole_out(shape) for shape in shapes],
        (),
        (0, sum(2 * math.prod(term.shape) for term in terms)),
        after,
    )


def shards(
    images,
    counts,
    joint_weight,
    out_weight,
    up_weight,
    down_weight,
    first_gain,
    first_shift,
    query_bias,
    value_bias,
    out_bias,
    first_scale,
    second_gain,
    second_shift,
    up_bias,
    down_bias,
    second_scale,
    cotangent,
    sizes,
):
    fsdp, sub = sizes
    cube = Cube() if (fsdp, sub) == (8, 4) else None
    images_here, length, width = images.shape
    heads = width // HD
    rows = images_here * length
    hidden_units = up_weight.shape[1] * sub
    depth = width // ROW_TILES
    span = 3 * width // COL_TILES
    piece = width // COL_TILES
    part = hidden_units // PARTS
    lane = part // ROW_TILES
    steps = COL_TILES

    image_block = pl.BlockSpec((1, length, width), lambda i, *_: (i, 0, 0))
    row_block = pl.BlockSpec((length, width), lambda i, *_: (i, 0))
    column_block = pl.BlockSpec((width, length), lambda i, *_: (0, i))
    mixed_block = pl.BlockSpec((3 * width, length), lambda i, *_: (0, i))
    probs_block = pl.BlockSpec((1, heads, length, length), lambda i, *_: (i, 0, 0, 0))
    tall, wide = (rows, width), (width, rows)
    area = rows * width

    def input_norm(after):
        return launch(
            normalize_kernel,
            "first_norm",
            images_here,
            (),
            [images],
            [image_block],
            [(tall, F32), ((rows, 128), F32)],
            [row_block, pl.BlockSpec((length, 128), lambda i, *_: (i, 0))],
            (),
            (area * width, 8 * area),
            after,
            covers=LIGHT,
        )

    vectors = (first_gain, first_shift, query_bias, value_bias, out_bias, first_scale)
    vectors += (second_gain, second_shift, down_bias, second_scale)
    wide_span = span + 64

    if cube is not None:
        dest = cube.places()
        ins = [joint_weight, out_weight, *vectors, up_bias]
        first_piece = launch(
            pack_first_kernel,
            "pack_first",
            1,
            (),
            ins,
            [whole(v.shape) for v in ins],
            [((depth, wide_span + 2 * lane), BF)],
            [whole_out((depth, wide_span + 2 * lane))],
            (),
            (0, 4 * depth * wide_span),
        )[0]

        ins = [up_weight, down_weight.T]
        shape = (PARTS * 2 * depth, 2 * lane)
        feed_piece = launch(
            pack_kernel,
            "pack",
            1,
            (),
            ins,
            [whole(v.shape) for v in ins],
            [(shape, BF)],
            [whole_out(shape)],
            (),
            (0, 4 * math.prod(shape)),
        )[0]
        feed_pieces = lax.all_gather(feed_piece, BOTH, axis=0)

        four = join(cube.gather_z(first_piece))
        near, far = cube.near(four), cube.far(four)
        normed_one, inverse_one = input_norm((four,))
        near = gate(near, (inverse_one,), 1.0)
        far_near = cube.far(near)
        first = [four, near, far, far_near]
        first += [cube.over(v) for v in first]
        after_first = ()
    else:
        order = [p for p in range(PIECES) if p % 2 == 0] + [p for p in range(PIECES) if p % 2]
        back_order = [order.index(p) for p in range(PIECES)]
        dest = jnp.array(order, dtype=jnp.int32)
        normed_one, inverse_one = input_norm(())
        after_first = ()

        def fetch(value):
            return lax.all_gather(
                lax.all_gather(value, "sub", axis=1, tiled=True), "fsdp", axis=0, tiled=True
            )

        def cut(value, columns):
            value = value.reshape(ROW_TILES, depth, COL_TILES, columns)
            return value.transpose(0, 2, 1, 3).reshape(PIECES, depth, columns)

        def groups(value):
            value = jnp.stack([value[p] for p in order])
            return [value[i : i + GROUP] for i in range(0, PIECES, GROUP)]

        short = width // PIECES
        lines = [lax.all_gather(v, BOTH, axis=0, tiled=True) for v in vectors]
        lines = jnp.stack(lines).reshape(VECTORS, PIECES, short).transpose(1, 0, 2)
        lines = jnp.pad(lines, ((0, 0), (0, 0), (0, 64 - short)))
        long = lax.all_gather(up_bias, BOTH, axis=0, tiled=True).reshape(PIECES, 2, 2 * short)
        long = jnp.pad(long, ((0, 0), (0, 0), (0, 64 - 2 * short)))
        lines = jnp.concatenate([lines, long], axis=1)
        lines = jnp.pad(lines, ((0, 0), (0, depth - VECTORS - 2), (0, 0)))
        out_pieces = jnp.pad(cut(fetch(out_weight), piece), ((0, 0), (0, 0), (0, 2 * lane - piece)))
        first = [cut(fetch(joint_weight), span), lines, out_pieces]
        first = groups(jnp.concatenate(first, axis=2))
        up_parts = fetch(up_weight).reshape(ROW_TILES, depth, COL_TILES, 2, PARTS, lane)
        up_parts = up_parts.transpose(0, 2, 4, 1, 3, 5)
        down_parts = fetch(down_weight).reshape(ROW_TILES, PARTS, lane, COL_TILES, 2, depth)
        down_parts = down_parts.transpose(0, 3, 1, 5, 4, 2)
        shape = (PIECES, PARTS, depth, 2 * lane)
        feed_pieces = jnp.concatenate([up_parts.reshape(shape), down_parts.reshape(shape)], axis=2)
        feed_pieces = feed_pieces.reshape(PIECES, -1, 2 * lane)

    table_spec = whole((16, width))
    joint_scratch = [
        pltpu.VMEM((COL_TILES, ROW_TILES, depth, wide_span), BF),
        pltpu.SemaphoreType.DMA((PIECES,)),
    ]

    mixed, first_t, table, up_rows = launch(
        qkv_kernel,
        "qkv",
        images_here,
        (dest,),
        [normed_one, *first],
        [row_block] + [ANY] * GROUPS,
        [((3 * width, rows), BF), (wide, BF), ((16, width), F32), ((PARTS, part), F32)],
        [mixed_block, column_block, whole_out((16, width)), whole_out((PARTS, part))],
        joint_scratch,
        (6 * area * width, 14 * area),
        after_first,
        covers=LIGHT,
    )

    def attend(start, stop, into, after, covers):
        return launch(
            functools.partial(attention_kernel, start),
            "attention",
            stop - start,
            (counts,),
            [mixed, *into],
            [pl.BlockSpec((3 * width, length), lambda i, *_: (0, i + start))] + [ANY] * len(into),
            [(wide, BF), ((images_here, heads, length, length), BF)],
            [
                pl.BlockSpec((width, length), lambda i, *_: (0, i + start)),
                pl.BlockSpec((1, heads, length, length), lambda i, *_: (i + start, 0, 0, 0)),
            ],
            (),
            (16 * area * length // 2, 16 * area // 2),
            after,
            {2: 0, 3: 1} if into else None,
            covers,
        )

    attended, probs = attend(0, images_here, (), (), LIGHT)

    resid, branch, second, second_t, dfeed, dfeed_t, out_full = launch(
        second_kernel,
        "second_norm",
        images_here,
        (dest, counts),
        [images, cotangent, attended, table, *first],
        [image_block, image_block, column_block, table_spec] + [ANY] * GROUPS,
        [(tall, F32), (tall, BF), (tall, BF), (wide, BF), (tall, BF), (wide, BF)]
        + [((width, width), BF)],
        [row_block, row_block, row_block, column_block, row_block, column_block]
        + [whole_out((width, width))],
        [
            pltpu.VMEM((COL_TILES, ROW_TILES, depth, 2 * lane), BF),
            pltpu.SemaphoreType.DMA((PIECES,)),
        ],
        (2 * area * width, 20 * area),
        covers=0.0,
    )

    def feed_forward(parts, carried, split, after=(), covers=1.0):
        ins = [up_rows, second, second_t, dfeed, dfeed_t, feed_pieces, *carried]
        count = len(parts)
        slots = (HALF if split else PIECES, count * 2 * depth, 2 * lane)
        tiles = rows // 256
        dma = pltpu.SemaphoreType.DMA
        return launch(
            functools.partial(mlp_kernel, parts, split),
            "feed_forward",
            1,
            (dest,),
            ins,
            [whole(up_rows.shape)] + [ANY] * (len(ins) - 1),
            [(tall, BF), (tall, BF), ((count, part), F32)] + [(slots, BF)] * (1 + split),
            [ANY, ANY, whole_out((count, part))] + [ANY] * (1 + split),
            [
                pltpu.VMEM((2, rows, width), BF),
                pltpu.VMEM((2, width, rows), BF),
                pltpu.VMEM((2, rows, width), BF),
                pltpu.VMEM((count, 2, width, part), BF),
                pltpu.VMEM((rows, part), BF),
                pltpu.VMEM((rows, part), BF),
                pltpu.VMEM((count, 2, width, part), BF),
                dma((count, PIECES, 2)),
                dma((2, tiles)),
                dma((2,)),
                dma((2, tiles)),
                dma((count, PIECES, 2)),
            ],
            (12 * area * part * count, 20 * area),
            after,
            covers=covers,
        )

    early = tuple(range(PARTS - 1))
    feed, dsecond, early_bias, early_grads = feed_forward(early, (), False, (), 0.0)
    feed, dsecond, late_bias, *late_grads = feed_forward(
        (PARTS - 1,), (feed, dsecond), True, (early_grads,)
    )

    waits = {}
    if cube is not None:
        early_total = lax.psum_scatter(early_grads, BOTH, scatter_dimension=0)
        late_got = cube.over(late_grads[1])

    block_out, dresid, dattended, out_grad, middle_sums = launch(
        middle_kernel,
        "middle",
        images_here,
        (counts,),
        [cotangent, feed, dsecond, resid, branch, attended, out_full, table],
        [image_block, row_block, row_block, row_block, row_block, column_block]
        + [whole((width, width)), table_spec],
        [(images.shape, BF), (tall, F32), (wide, BF), ((width, width), BF), ((8, width), F32)],
        [image_block, row_block, column_block, whole_out((width, width)), whole_out((8, width))],
        [pltpu.VMEM((width, width), F32)],
        (4 * area * width, 30 * area),
        waits.get("middle", ()),
    )

    if cube is not None:
        late_low, late_high = add_halves(late_grads[0], None, late_got, (dresid,))
        late_got = cube.far(late_high)
        waits["attention_back"] = (late_high,)

    dmixed, attention_sums = launch(
        attention_back_kernel,
        "attention_back",
        images_here,
        (),
        [mixed, probs, attended, dattended],
        [mixed_block, probs_block, column_block, column_block],
        [((3 * width, rows), BF), ((8, width), F32)],
        [mixed_block, whole_out((8, width))],
        [pltpu.VMEM((width, 128), F32)] * 2 + [pltpu.VMEM((heads, length, length), BF)],
        (32 * area * length, 24 * area),
        waits.get("attention_back", ()),
    )

    if cube is not None:
        late_low, late_high = add_halves(late_low, None, late_got, (dmixed,))
        late_got = cube.near(late_high)
        waits["joint_grad"] = (late_high,)

    def joint_grads(offset, after):
        def column_tile(g, dest):
            return (2 * g + lax.rem(dest[0] + offset, 2), 0)

        return launch(
            functools.partial(joint_grad_kernel, offset),
            "joint_grad",
            2,
            (dest,),
            [first_t, dmixed, out_grad],
            [
                whole(wide),
                pl.BlockSpec((span, rows), column_tile),
                pl.BlockSpec((width, width // 2), lambda g, *_: (0, g)),
            ],
            [((HALF, depth, width), BF)],
            [ANY],
            [pltpu.VMEM((2, width, width), BF), pltpu.SemaphoreType.DMA((HALF,))],
            (3 * area * width, 10 * area),
            after,
        )[0]

    send_first = joint_grads(1, waits.get("joint_grad", ()))
    if cube is not None:
        first_got = cube.over(send_first)
    keep_first = joint_grads(0, (send_first,))

    after_input = ()
    if cube is not None:
        late_last = add_four(late_low, late_got, (keep_first,))
        late_terms = cube.reduce_z(late_last)
        first_low, first_high = add_halves(keep_first, None, first_got, (late_last[0],))
        first_got = cube.far(first_high)
        after_input = (first_high,)

    image_grad, input_sums = launch(
        input_grad_kernel,
        "input_grad",
        images_here,
        (dest,),
        [normed_one, inverse_one, dresid, dmixed, table, *first],
        [row_block, pl.BlockSpec((length, 128), lambda i, *_: (i, 0)), row_block, mixed_block]
        + [table_spec]
        + [ANY] * GROUPS,
        [(images.shape, F32), ((8, width), F32)],
        [image_block, whole_out((8, width))],
        joint_scratch,
        (6 * area * width, 20 * area),
        after_input,
    )

    ins = [input_sums, attention_sums, middle_sums, early_bias, late_bias]
    sums = launch(
        collect_kernel,
        "collect",
        1,
        (),
        ins,
        [whole(v.shape) for v in ins],
        [((16, width), F32)],
        [whole_out((16, width))],
        (),
        (0, 0),
    )[0]
    short = first_gain.shape[0]
    if cube is not None:
        late_total = totals(
            late_total_kernel, "late_total", late_terms, (late_terms[0].shape,), (image_grad,)
        )
        first_low, first_high = add_halves(first_low, None, first_got, (image_grad, *late_total))
        first_got = cube.near(first_high)
        sums = gate(sums, (first_high,), 1.0)
        first_last = add_four(first_low, first_got, (sums,))
        first_terms = cube.reduce_z(first_last)
        sums = cube.total(sums, cube.z[:2])
        sums = gate(sums, first_last[:1], 1.0)
        sums = cube.total(sums, (cube.core, cube.x, cube.y))
        up_grad, down_grad = totals(
            feed_total_kernel,
            "feed_total",
            (early_total, *late_total),
            (up_weight.shape, down_weight.shape[::-1]),
            (sums,),
        )
        down_grad = down_grad.T
        joint_grad, out_weight_grad = totals(
            first_total_kernel,
            "first_total",
            first_terms,
            (joint_weight.shape, out_weight.shape),
            (sums,),
        )
        device = lax.axis_index("fsdp") * sub + lax.axis_index("sub")
        vectors = lax.dynamic_slice(sums[:10], (0, device * short), (10, short))
        up_bias_grad = lax.dynamic_slice(
            sums[VECTORS : VECTORS + 4].reshape(-1), (device * up_bias.shape[0],), up_bias.shape
        )
    else:

        def hand_out(value):
            value = lax.psum_scatter(value.astype(BF), "fsdp", scatter_dimension=0, tiled=True)
            value = lax.psum_scatter(value, "sub", scatter_dimension=1, tiled=True)
            return value.astype(F32)

        def uncut(value, columns):
            value = value.reshape(ROW_TILES, COL_TILES, depth, columns)
            return value.transpose(0, 2, 1, 3).reshape(width, COL_TILES * columns)

        def in_order(value):
            return jnp.stack([value[i] for i in back_order])

        grads = in_order(jnp.concatenate([keep_first, send_first]))
        joint_grad = hand_out(uncut(grads[:, :, :span], span))
        out_weight_grad = hand_out(uncut(grads[:, :, span:], piece))
        late_grads = in_order(jnp.concatenate(late_grads))
        grads = jnp.concatenate([early_grads, late_grads], axis=1)
        grads = grads.reshape(ROW_TILES, COL_TILES, PARTS, 2, depth, 2, lane)
        up_grad = grads[:, :, :, 0].transpose(0, 3, 1, 4, 2, 5).reshape(width, hidden_units)
        down_grad = grads[:, :, :, 1].transpose(0, 2, 5, 1, 4, 3).reshape(hidden_units, width)
        up_grad, down_grad = hand_out(up_grad), hand_out(down_grad)

        def hand_vector(value):
            return lax.psum_scatter(value, BOTH, scatter_dimension=0, tiled=True)

        vectors = [hand_vector(sums[v]) for v in range(10)]
        up_bias_grad = hand_vector(sums[VECTORS : VECTORS + 4].reshape(-1))
    return (
        block_out,
        image_grad,
        joint_grad,
        out_weight_grad,
        up_grad,
        down_grad,
        vectors[0],
        vectors[1],
        vectors[2],
        vectors[3],
        vectors[4],
        vectors[5],
        vectors[6],
        vectors[7],
        up_bias_grad,
        vectors[8],
        vectors[9],
    )


def solution(mesh):
    rows = P(BOTH, None, None)
    matrix = P("fsdp", "sub")
    vector = P(BOTH)
    sizes = (mesh.shape["fsdp"], mesh.shape["sub"])
    return jax.shard_map(
        functools.partial(shards, sizes=sizes),
        mesh=mesh,
        in_specs=(rows, vector) + (matrix,) * 4 + (vector,) * 11 + (rows,),
        out_specs=(rows, rows) + (matrix,) * 4 + (vector,) * 11,
        check_vma=False,
    )
```

```python
import functools
import math

import jax
import jax.numpy as jnp
from jax import lax
from jax.experimental import pallas as pl
from jax.experimental.pallas import tpu as pltpu
from jax.sharding import PartitionSpec as P

HD = 64
EPS = 1e-06
NEGATIVE = -1e30
ROW_TILES = 8
COL_TILES = 4
PIECES = ROW_TILES * COL_TILES
HALF = PIECES // 2
ROWS = 512
CHUNK = 64
GROUP = 4
GROUPS = PIECES // GROUP
VECTORS = 10
PARTS = 3
BOTH = ("fsdp", "sub")
LIGHT = 0.08
SLACK = 100
VMEM_LIMIT = 56 * 1024 * 1024
BF = jnp.bfloat16
F32 = jnp.float32
NT = (((1,), (1,)), ((), ()))
TN = (((0,), (0,)), ((), ()))


def dot(left, right):
    return jnp.dot(left, right, preferred_element_type=F32)


def dot_general(left, right, dims):
    return lax.dot_general(left, right, dims, preferred_element_type=F32)


def launch(
    kernel, name, grid, scalars, ins, specs, outs, out_specs, scratch, price, after=(), aliases=None, covers=1.0
):
    known = len(scalars) + len(ins)

    def body(*refs):
        kernel(*refs[:known], *refs[known + len(after) :])

    return pl.pallas_call(
        body,
        grid_spec=pltpu.PrefetchScalarGridSpec(
            num_scalar_prefetch=len(scalars),
            grid=(grid,),
            in_specs=list(specs) + [ANY] * len(after),
            out_specs=list(out_specs),
            scratch_shapes=list(scratch),
        ),
        out_shape=[jax.ShapeDtypeStruct(shape, dtype) for shape, dtype in outs],
        input_output_aliases=aliases or {},
        compiler_params=pltpu.CompilerParams(
            dimension_semantics=("arbitrary",), vmem_limit_bytes=VMEM_LIMIT
        ),
        cost_estimate=pl.CostEstimate(
            flops=int(SLACK * covers * price[0]), bytes_accessed=price[1], transcendentals=0
        ),
        name=name,
    )(*scalars, *ins, *after)


def normalize(rows):
    centre = rows - jnp.mean(rows, axis=-1, keepdims=True)
    spread = jnp.mean(centre * centre, axis=-1, keepdims=True)
    inverse = lax.rsqrt(spread + EPS)
    return (centre * inverse, inverse)


def norm_back(upstream, normed, inverse, gain):
    scaled = upstream * gain
    return inverse * (
        scaled
        - jnp.mean(scaled, axis=-1, keepdims=True)
        - normed * jnp.mean(scaled * normed, axis=-1, keepdims=True)
    )


def eight_sum(values):
    return jnp.sum(values.reshape(-1, 8, values.shape[-1]), axis=0)


def row_sum(values):
    return jnp.sum(values, axis=0, keepdims=True)


def whole(shape):
    zeros = (0,) * len(shape)
    return pl.BlockSpec(shape, lambda *_: zeros, pipeline_mode=pl.Buffered(1))


def whole_out(shape):
    zeros = (0,) * len(shape)
    return pl.BlockSpec(shape, lambda *_: zeros)


ANY = pl.BlockSpec(memory_space=pl.ANY)


def stage_pieces(places, sources, weights, sems, low=0):
    wide = weights.shape[-1]
    copies = []
    for i, place in enumerate(places):
        copies.append(
            pltpu.make_async_copy(
                sources(i).at[:, pl.ds(low, wide)],
                weights.at[lax.rem(place, COL_TILES), lax.div(place, COL_TILES)],
                sems.at[i],
            )
        )
    for copy in copies:
        copy.start()
    for copy in copies:
        copy.wait()


def grouped(dest, refs):
    return [dest[i] for i in range(PIECES)], lambda i: refs[i // GROUP].at[i % GROUP]


def columns_of(weights, s):
    _, tiles, depth, wide = weights.shape
    return weights[s].reshape(tiles * depth, wide)


def join_kernel(*refs):
    *pieces, out = refs
    for i, piece in enumerate(pieces):
        out[i] = piece[...]


def pack_first_kernel(joint_weight, out_weight, *refs):
    *vectors, long, packed = refs
    depth, span = joint_weight.shape
    rest = 64
    packed[:, :span] = joint_weight[...]
    packed[:, span + rest :] = jnp.zeros((depth, packed.shape[1] - span - rest), BF)
    packed[:, span + rest : span + rest + out_weight.shape[1]] = out_weight[...]
    half = long.shape[0] // 2
    lines = [vector[...].astype(F32).reshape(1, -1) for vector in vectors]
    both = long[...].astype(F32).reshape(1, -1)
    lines += [both[:, :half], both[:, half:]]
    lines = [jnp.pad(line, ((0, 0), (0, rest - line.shape[1]))) for line in lines]
    lines.append(jnp.zeros((16 - len(lines), rest), F32))
    packed[:, span : span + rest] = jnp.zeros((depth, rest), BF)
    packed[0:16, span : span + rest] = jnp.concatenate(lines).astype(BF)


def pack_kernel(up_weight, down_t, packed):
    depth, units = up_weight.shape
    lane = units // PARTS // 2
    for j in range(PARTS):
        at = 2 * j * depth
        low = j * lane
        for h in range(2):
            lanes = slice(h * lane, (h + 1) * lane)
            packed[at : at + depth, lanes] = up_weight[
                :, h * units // 2 + low : h * units // 2 + low + lane
            ]
            packed[at + depth : at + 2 * depth, lanes] = down_t[
                h * depth : (h + 1) * depth, low : low + lane
            ]


def add_kernel(low, high, got_low, got_high, low_out, high_out):
    low_out[...] = (low[...].astype(F32) + got_low[...].astype(F32)).astype(BF)
    high_out[...] = (high[...].astype(F32) + got_high[...].astype(F32)).astype(BF)


def add_four_kernel(keep, got, *outs):
    for k, out in enumerate(outs[-4:]):
        out[...] = (keep[k].astype(F32) + got[k].astype(F32)).astype(BF)


def sum_of(refs):
    return sum(ref[...].astype(F32) for ref in refs)


def late_total_kernel(*refs):
    refs[-1][...] = sum_of(refs[:-1])


def first_total_kernel(a, b, c, d, joint_grad, out_grad):
    total = sum_of((a, b, c, d))
    span = joint_grad.shape[1]
    joint_grad[...] = total[:, :span]
    out_grad[...] = total[:, span:]


def feed_total_kernel(*refs):
    *terms, up_grad, down_grad = refs
    depth, units = up_grad.shape
    lane = units // PARTS // 2
    total = jnp.concatenate([term[...].astype(F32) for term in terms])
    tall = []
    for j in range(PARTS):
        at = 2 * j * depth
        for h in range(2):
            lanes = slice(h * lane, (h + 1) * lane)
            low = h * units // 2 + j * lane
            up_grad[:, low : low + lane] = total[at : at + depth, lanes]
        at += depth
        tall.append(
            jnp.concatenate([total[at : at + depth, :lane], total[at : at + depth, lane:]])
        )
    wide = jnp.concatenate(tall, axis=1)
    down_grad[...] = wide


def normalize_kernel(images, normed_out, inverse_out):
    normed, inverse = normalize(images[0].astype(F32))
    normed_out[...] = normed
    inverse_out[...] = jnp.broadcast_to(inverse, inverse_out.shape)


def qkv_kernel(dest, normed, *refs):
    *sources, mixed, first_t, table, up_rows, weights, sems = refs
    width = normed.shape[-1]
    span = 3 * width // COL_TILES
    short = width // PIECES
    lane = 128

    @pl.when(pl.program_id(0) == 0)
    def _():
        stage_pieces(*grouped(dest, sources), weights, sems)
        lines = []
        long = []
        for place in range(PIECES):
            block = weights[place % COL_TILES, place // COL_TILES, 0:16, span:].astype(F32)
            lines.append(block[:, :short])
            long += [block[VECTORS : VECTORS + 1, : 2 * short]]
            long += [block[VECTORS + 1 : VECTORS + 2, : 2 * short]]
        table[...] = jnp.concatenate(lines, axis=1)
        long = jnp.concatenate(long, axis=1)
        for j in range(PARTS):
            for m in range(ROW_TILES):
                up_rows[j : j + 1, m * lane : (m + 1) * lane] = long[:, (m * PARTS + j) * lane : (m * PARTS + j + 1) * lane]

    bias = jnp.concatenate([table[2:3], jnp.zeros((1, width), F32), table[3:4]], axis=1)
    first = (normed[...] * table[0:1] + table[1:2]).astype(BF)
    first_t[...] = first.T
    for s in range(COL_TILES):
        out = dot(first, columns_of(weights, s)[:, :span])
        out = (out + bias[:, s * span : (s + 1) * span]).astype(BF)
        mixed[s * span : (s + 1) * span, :] = out.T


def attention_kernel(start, counts, mixed, *refs):
    attended, probs = refs[-2:]
    width = attended.shape[0]
    length = mixed.shape[1]
    scale = math.log2(math.e) / math.sqrt(HD)
    count = counts[pl.program_id(0) + start]
    valid = lax.broadcasted_iota(jnp.int32, (length, length), 0) < count
    for h in range(width // HD):
        query = mixed[h * HD : (h + 1) * HD, :]
        key = mixed[width + h * HD : width + (h + 1) * HD, :]
        scores = jnp.where(valid, dot_general(key, query, TN), NEGATIVE)
        largest = jnp.max(scores, axis=0, keepdims=True)
        expon = jnp.exp2((scores - largest) * scale)
        probs[0, h] = (expon * (1.0 / jnp.sum(expon, axis=0, keepdims=True))).astype(BF)
    for h in range(width // HD):
        value = mixed[2 * width + h * HD : 2 * width + (h + 1) * HD, :]
        attended[h * HD : (h + 1) * HD, :] = dot(value, probs[0, h]).astype(BF)


def second_kernel(dest, counts, images, cotangent, attended, table, *refs):
    sources, refs = refs[:GROUPS], refs[GROUPS:]
    resid_out, branch_out, second, second_t, dfeed_out, dfeed_t, out_full, *refs = refs
    weights, sems, branch_all = refs
    width = images.shape[-1]
    length = images.shape[1]
    piece = width // COL_TILES

    @pl.when(pl.program_id(0) == 0)
    def _():
        low = 3 * width // COL_TILES + 64
        stage_pieces(*grouped(dest, sources), weights, sems, low)
        for s in range(COL_TILES):
            out_full[:, s * piece : (s + 1) * piece] = columns_of(weights, s)[:, :piece]

    branch_all[...] = dot_general(attended[...], out_full[...], TN)
    for low in range(0, length, CHUNK):
        rows = slice(low, low + CHUNK)
        branch = branch_all[rows, :] + table[4:5]
        branch_out[rows, :] = branch.astype(BF)
        resid = images[0, rows, :].astype(F32) + table[5:6] * branch
        resid_out[rows, :] = resid.astype(BF)
        normed, _ = normalize(resid)
        second[rows, :] = (normed * table[6:7] + table[7:8]).astype(BF)
        places = low + lax.broadcasted_iota(jnp.int32, (CHUNK, 1), 0)
        mask = (places < counts[pl.program_id(0)]).astype(F32)
        dfeed_out[rows, :] = (cotangent[0, rows, :].astype(F32) * mask * table[9:10]).astype(BF)
    second_t[...] = second[...].T
    dfeed_t[...] = dfeed_out[...].T


def gelu_pair(value):
    size = jnp.abs(value)
    t = 1.0 / (1.0 + (0.3275911 / math.sqrt(2.0)) * size)
    bell = jnp.exp2(value * value * (-0.5 * math.log2(math.e)))
    poly = 0.5 * 1.061405429
    for c in (-1.453152027, 1.421413741, -0.284496736, 0.254829592):
        poly = poly * t + 0.5 * c
    tail = poly * t * bell
    cumul = jnp.where(value >= 0, 1.0 - tail, tail)
    return value * cumul, cumul + value * bell * (1.0 / math.sqrt(2.0 * math.pi))


def mlp_kernel(parts, split, dest, bias, second, second_t, dfeed, dfeed_t, gathered, *rest):
    first = parts[0] == 0
    if not first:
        carried, rest = rest[:2], rest[2:]
    feed, dsecond, bias_grad, *rest = rest
    if split:
        keep, send, *rest = rest
    else:
        grads, *rest = rest
    rows_in, rows_t, sums, weights, hidden, dpre, weight_grads, *sems = rest
    piece_sem, row_sem, turned_sem, sum_sem, out_sem = sems
    count, width = second.shape
    depth = width // ROW_TILES
    span = width // COL_TILES
    wide = weights.shape[-1]
    lane = wide // ROW_TILES
    tile = ROWS
    tiles = count // tile

    def moves(place, buffer, outside, origin, sem, inward):
        m = lax.div(place, COL_TILES)
        s = lax.rem(place, COL_TILES)
        copies = [
            (
                outside.at[pl.ds(origin, depth), :],
                buffer.at[
                    0,
                    pl.ds(pl.multiple_of(m * depth, 16), depth),
                    pl.ds(pl.multiple_of(s * 2 * lane, 128), 2 * lane),
                ],
                sem.at[0],
            )
        ]
        for h in range(2):
            copies.append(
                (
                    outside.at[pl.ds(origin + depth, depth), pl.ds(h * lane, lane)],
                    buffer.at[
                        1,
                        pl.ds(pl.multiple_of(s * span + h * depth, 16), depth),
                        pl.ds(pl.multiple_of(m * lane, 128), lane),
                    ],
                    sem.at[1],
                )
            )
        return [
            pltpu.make_async_copy(*((a, b) if inward else (b, a)), sem) for a, b, sem in copies
        ]

    def run(copies):
        for copy in copies:
            copy.start()
        return copies

    def wait(copies):
        for copy in copies:
            copy.wait()

    def row_copies(r, sources, targets, sem):
        rows = pl.ds(r * tile, tile)
        return [
            pltpu.make_async_copy(a.at[rows, :], b.at[rows, :], sem.at[i, r])
            for i, (a, b) in enumerate(zip(sources, targets))
        ]

    rows_in = (rows_in.at[0], rows_in.at[1])
    rows_t = (rows_t.at[0], rows_t.at[1])
    sums = (sums.at[0], sums.at[1])

    def arrivals(n):
        every = [
            moves(
                i,
                weights.at[n],
                gathered.at[i],
                2 * depth * parts[n],
                piece_sem.at[n, i],
                True,
            )
            for i in range(PIECES)
        ]
        return [c[0] for c in every], [c for copies in every for c in copies[1:]]

    coming = [arrivals(n) for n in range(len(parts))]
    arriving = [row_copies(r, (second, dfeed), rows_in, row_sem) for r in range(tiles)]
    turned = [
        pltpu.make_async_copy(a, b, turned_sem.at[i])
        for i, (a, b) in enumerate(zip((second_t, dfeed_t), rows_t))
    ]
    partial = [] if first else [row_copies(r, carried, sums, sum_sem) for r in range(tiles)]
    later = arriving[1:] + partial + [turned] + [c for two in coming[1:] for c in two]
    run(coming[0][0])
    run(arriving[0])
    run(coming[0][1])
    leaving = []
    for n, part in enumerate(parts):
        up, down = weights.at[n, 0], weights.at[n, 1]
        up_grad, down_grad = weight_grads.at[n, 0], weight_grads.at[n, 1]
        wait(coming[n][0])
        add = bias[part : part + 1, :]
        total = jnp.zeros((1, wide), F32)
        for r in range(tiles):
            rows = slice(r * tile, (r + 1) * tile)
            if n == 0:
                wait(arriving[r])
                ahead = -(-len(later) // (tiles - r))
                for copies in later[:ahead]:
                    run(copies)
                later = later[ahead:]
            pre = dot(rows_in[0][rows, :], up[...]) + add
            if r == 0:
                wait(coming[n][1])
            back = dot(rows_in[1][rows, :], down[...])
            value, slope = gelu_pair(pre)
            hidden[rows, :] = value.astype(BF)
            back = (back * slope).astype(BF)
            dpre[rows, :] = back
            total = total + row_sum(back.astype(F32))
        bias_grad[n : n + 1, :] = total
        for r in range(tiles):
            rows = slice(r * tile, (r + 1) * tile)
            forward = dot_general(hidden[rows, :], down[...], NT)
            back = dot_general(dpre[rows, :], up[...], NT)
            if not first and n == 0:
                wait(partial[r])
            if not first or n > 0:
                forward = forward + sums[0][rows, :].astype(F32)
                back = back + sums[1][rows, :].astype(F32)
            sums[0][rows, :] = forward.astype(BF)
            sums[1][rows, :] = back.astype(BF)
            if n == len(parts) - 1:
                leaving += run(row_copies(r, sums, (feed, dsecond), sum_sem))
        if n == 0:
            wait(turned)
        up_grad[...] = dot(rows_t[0][...], dpre[...]).astype(BF)
        outs = [
            moves(
                dest[i] if split else i,
                weight_grads.at[n],
                (keep if i < HALF else send).at[i % HALF] if split else grads.at[i],
                2 * depth * n,
                out_sem.at[n, i],
                False,
            )
            for i in range(PIECES)
        ]
        for copies in outs:
            leaving += run(copies[:1])
        down_grad[...] = dot(rows_t[1][...], hidden[...]).astype(BF)
        for copies in outs:
            leaving += run(copies[1:])
    wait(leaving)


def middle_kernel(
    counts,
    cotangent,
    feed,
    dsecond,
    resid,
    branch,
    attended,
    out_full,
    table,
    block_out,
    dresid_out,
    dattended,
    out_grad,
    sums,
    total,
    partial,
    dbranch_all,
):
    length = cotangent.shape[1]
    step = pl.program_id(0)

    @pl.when(step == 0)
    def _():
        total[...] = jnp.zeros(total.shape, F32)
        partial[...] = jnp.zeros(partial.shape, F32)

    for low in range(0, length, CHUNK):
        rows = slice(low, low + CHUNK)
        places = low + lax.broadcasted_iota(jnp.int32, (CHUNK, 1), 0)
        mask = (places < counts[step]).astype(F32)
        feed_out = feed[rows, :].astype(F32) + table[8:9]
        grad = cotangent[0, rows, :].astype(F32) * mask
        value = resid[rows, :].astype(F32)
        block_out[0, rows, :] = ((value + table[9:10] * feed_out) * mask).astype(BF)
        normed, inverse = normalize(value)
        upstream = dsecond[rows, :].astype(F32)
        dresid = grad + norm_back(upstream, normed, inverse, table[6:7])
        dresid_out[rows, :] = dresid.astype(BF)
        dbranch = (dresid * table[5:6]).astype(BF)
        dbranch_all[rows, :] = dbranch
        dfeed = (grad * table[9:10]).astype(BF)
        partial[0] += eight_sum(dbranch.astype(F32))
        partial[1] += eight_sum(dresid * branch[rows, :].astype(F32))
        partial[2] += eight_sum(upstream * normed)
        partial[3] += eight_sum(upstream)
        partial[4] += eight_sum(dfeed.astype(F32))
        partial[5] += eight_sum(grad * feed_out)
    dbranch = dbranch_all[...]
    total[...] += dot(attended[...], dbranch)
    dattended[...] = dot_general(out_full[...], dbranch, NT).astype(BF)

    @pl.when(step == pl.num_programs(0) - 1)
    def _():
        out_grad[...] = total[...].astype(BF)
        sums[...] = jnp.zeros(sums.shape, F32)
        for n in range(6):
            sums[n : n + 1] = row_sum(partial[n])


def attention_back_kernel(
    dest,
    mixed,
    probs,
    attended,
    dattended,
    first_t,
    out_grad,
    dmixed,
    sums,
    send,
    dquery_sum,
    dvalue_sum,
    dscores,
    every,
    first_here,
    out_here,
    grads,
    sems,
):
    width = attended.shape[0]
    length = mixed.shape[1]
    heads = width // HD
    factor = 1.0 / math.sqrt(HD)
    step = pl.program_id(0)
    wanted = [
        pltpu.make_async_copy(first_t, first_here, sems.at[0]),
        pltpu.make_async_copy(out_grad, out_here, sems.at[1]),
    ]

    @pl.when(step == 0)
    def _():
        for copy in wanted:
            copy.start()
        dquery_sum[...] = jnp.zeros(dquery_sum.shape, F32)
        dvalue_sum[...] = jnp.zeros(dvalue_sum.shape, F32)

    def part(block, h):
        return slice(block * width + h * HD, block * width + (h + 1) * HD)

    def fold(values):
        return sum(values[:, a : a + 128].astype(F32) for a in range(0, length, 128))

    def score_grads(h):
        upstream = dattended[part(0, h), :]
        delta = row_sum(upstream.astype(F32) * attended[part(0, h), :].astype(F32))
        dprobs = dot_general(mixed[part(2, h), :], upstream, TN)
        dscores[h] = (probs[0, h].astype(F32) * (dprobs - delta)).astype(BF)

    score_grads(0)
    for h in range(heads):
        if h + 1 < heads:
            score_grads(h + 1)
        dvalue = dot_general(dattended[part(0, h), :], probs[0, h], NT)
        dkey = dot_general(mixed[part(0, h), :], dscores[h], NT) * factor
        dquery = dot(mixed[part(1, h), :], dscores[h]) * factor
        dmixed[part(2, h), :] = dvalue.astype(BF)
        dmixed[part(1, h), :] = dkey.astype(BF)
        dmixed[part(0, h), :] = dquery.astype(BF)
    dquery_sum[...] += fold(dmixed[0:width, :])
    dvalue_sum[...] += fold(dmixed[2 * width :, :])
    every[step] = dmixed[...]

    @pl.when(step == pl.num_programs(0) - 1)
    def _():
        sums[...] = jnp.zeros(sums.shape, F32)
        sums[0:1] = row_sum(dquery_sum[...].T)
        sums[1:2] = row_sum(dvalue_sum[...].T)
        for copy in wanted:
            copy.wait()
        span = 3 * width // COL_TILES
        for g in range(2):
            low = (2 * g + lax.rem(dest[0] + 1, 2)) * span
            rows = pl.ds(pl.multiple_of(low, 16), span)
            part = jnp.concatenate([every[i, rows, :] for i in range(every.shape[0])], axis=1)
            put_joint_grad(1, g, dest, first_here[...], part, out_here, grads)
        leave(1, dest, grads, send, sems, 2)


def put_joint_grad(offset, g, dest, first_t, dmixed, out_grad, grads):
    width = grads.shape[1]
    span = dmixed.shape[0]
    piece = width - span
    low = 2 * g * piece
    odd = lax.rem(dest[0] + offset, 2) == 1
    grads[g, :, span:] = jnp.where(
        odd, out_grad[:, low + piece : low + 2 * piece], out_grad[:, low : low + piece]
    )
    grads[g, :, 0:span] = dot_general(first_t, dmixed, NT).astype(BF)


def leave(offset, dest, grads, out, sems, first_sem):
    depth = grads.shape[1] // ROW_TILES
    copies = []
    for i in range(HALF):
        place = dest[offset * HALF + i]
        m = lax.div(place, COL_TILES)
        near = grads.at[
            lax.div(lax.rem(place, COL_TILES), 2),
            pl.ds(pl.multiple_of(m * depth, 16), depth),
            :,
        ]
        copies.append(pltpu.make_async_copy(near, out.at[i], sems.at[first_sem + i]))
    for copy in copies:
        copy.start()
    for copy in copies:
        copy.wait()


def joint_grad_kernel(dest, first_t, low_tile, high_tile, out_grad, out, grads, sems):
    for g, dmixed in enumerate((low_tile, high_tile)):
        put_joint_grad(0, g, dest, first_t[...], dmixed[...], out_grad, grads)
    leave(0, dest, grads, out, sems, 0)


def collect_kernel(input_sums, attention_sums, middle_sums, *refs):
    *bias_sums, out = refs
    lane = bias_sums[0].shape[1] // ROW_TILES
    out[0:2] = input_sums[0:2]
    out[2:4] = attention_sums[0:2]
    out[4:VECTORS] = middle_sums[0 : VECTORS - 4]
    out[VECTORS:] = jnp.zeros((16 - VECTORS, out.shape[1]), F32)
    bias_rows = [sums[n : n + 1, :] for sums in bias_sums for n in range(sums.shape[0])]
    for j, sums in enumerate(bias_rows):
        for m in range(ROW_TILES):
            at = (m * PARTS + j) * lane
            row, column = divmod(at, out.shape[1])
            out[VECTORS + row : VECTORS + row + 1, column : column + lane] = sums[
                :, m * lane : (m + 1) * lane
            ]


def input_grad_kernel(dest, normed, inverse, dresid, dmixed, table, *refs):
    *sources, image_grad, sums, weights, sems, partial, back_all = refs
    width = normed.shape[-1]
    span = 3 * width // COL_TILES

    @pl.when(pl.program_id(0) == 0)
    def _():
        stage_pieces(*grouped(dest, sources), weights, sems)
        partial[...] = jnp.zeros(partial.shape, F32)

    back = None
    for s in range(COL_TILES):
        part = dot(
            columns_of(weights, s)[:, :span], dmixed[s * span : (s + 1) * span, :]
        )
        back = part if back is None else back + part
    back_all[...] = back.T
    for low in range(0, back_all.shape[0], CHUNK):
        rows = slice(low, low + CHUNK)
        upstream = back_all[rows, :]
        value = normed[rows, :]
        partial[0] += eight_sum(upstream * value)
        partial[1] += eight_sum(upstream)
        image_grad[0, rows, :] = dresid[rows, :].astype(F32) + norm_back(
            upstream, value, inverse[rows, 0:1], table[0:1]
        )

    @pl.when(pl.program_id(0) == pl.num_programs(0) - 1)
    def _():
        sums[...] = jnp.zeros(sums.shape, F32)
        for n in range(2):
            sums[n : n + 1] = row_sum(partial[n])


def flat_pairs(fsdp, sub, there):
    return [(f * sub + s, there(f, s)) for f in range(fsdp) for s in range(sub)]


class Cube:
    def __init__(self):
        def along_z(k):
            return flat_pairs(8, 4, lambda f, s: (f ^ (2 * k)) * 4 + s)

        def y_or_x(order):
            def there(f, s):
                turn = (s % 2) ^ order
                return (f * 4 + (s ^ 2)) if turn else ((f ^ 1) * 4 + s)

            return flat_pairs(8, 4, there)

        self.z = [along_z(k) for k in (1, 2, 3)]
        self.plane = [y_or_x(0), y_or_x(1)]
        self.core = flat_pairs(8, 4, lambda f, s: f * 4 + (s ^ 1))
        self.y = flat_pairs(8, 4, lambda f, s: (f ^ 1) * 4 + s)
        self.x = flat_pairs(8, 4, lambda f, s: f * 4 + (s ^ 2))

    def swap(self, value, pairs):
        return lax.ppermute(value, BOTH, pairs)

    def places(self):
        f = lax.axis_index("fsdp")
        s = lax.axis_index("sub")
        z, y, x, c = f // 2, f % 2, s // 2, s % 2

        def slot_to_place(i):
            core = c ^ (i // 16)
            far, near, dz = (i // 8) % 2, (i // 4) % 2, i % 4
            dy = jnp.where(core == 0, near, far)
            dx = jnp.where(core == 0, far, near)
            return ((z ^ dz) * 2 + (y ^ dy)) * 4 + (x ^ dx) * 2 + core

        index = jnp.arange(PIECES, dtype=jnp.int32)
        return slot_to_place(index)

    def near(self, value):
        return self.swap(value, self.plane[0])

    def far(self, value):
        return self.swap(value, self.plane[1])

    def over(self, value):
        return self.swap(value, self.core)

    def gather_z(self, piece):
        return (piece,) + tuple(self.swap(piece, pairs) for pairs in self.z)

    def reduce_z(self, four):
        return (four[0],) + tuple(self.swap(four[k], self.z[k - 1]) for k in (1, 2, 3))

    def total(self, value, stages):
        for pairs in stages:
            value = value + self.swap(value, pairs)
        return value


def join(pieces, after=()):
    shape = (len(pieces),) + pieces[0].shape
    return launch(
        join_kernel,
        "join",
        1,
        (),
        list(pieces),
        [whole(piece.shape) for piece in pieces],
        [(shape, BF)],
        [whole_out(shape)],
        (),
        (0, 4 * math.prod(shape)),
        after,
    )[0]


def gate_kernel(value, out):
    del value, out


def gate(value, after, covers=0.0):
    return launch(
        gate_kernel,
        "gate",
        1,
        (),
        [value],
        [ANY],
        [(value.shape, value.dtype)],
        [ANY],
        (),
        (10**8, 0),
        after,
        {0: 0},
        covers,
    )[0]


def add_halves(low, high, got, after=()):
    count = got.shape[0] // 2
    shift = count if high is None else 0
    steps = 2
    block = (count // steps,) + got.shape[1:]
    here = pl.BlockSpec(block, lambda i, *_: (i, 0, 0))
    there = pl.BlockSpec(block, lambda i, *_: (i + steps, 0, 0))
    shape = (count,) + got.shape[1:]
    return launch(
        add_kernel,
        "add",
        steps,
        (),
        [low, low if high is None else high, got, got],
        [here, there if shift else here, here, there],
        [(shape, BF), (shape, BF)],
        [here, here],
        (),
        (0, 12 * math.prod(shape)),
        after,
    )


def add_four(keep, got, after=(), held=()):
    shape = got.shape[1:]
    return launch(
        add_four_kernel,
        "add",
        1,
        (),
        [keep, got, *held],
        [whole(got.shape)] * 2 + [ANY] * len(held),
        [(v.shape, v.dtype) for v in held] + [(shape, BF)] * 4,
        [ANY] * len(held) + [whole_out(shape)] * 4,
        (),
        (0, 24 * math.prod(shape)),
        after,
        {2 + i: i for i in range(len(held))},
    )


def totals(kernel, name, terms, shapes, after=()):
    return launch(
        kernel,
        name,
        1,
        (),
        list(terms),
        [whole(term.shape) for term in terms],
        [(shape, F32) for shape in shapes],
        [whole_out(shape) for shape in shapes],
        (),
        (0, sum(2 * math.prod(term.shape) for term in terms)),
        after,
    )


def shards(
    images,
    counts,
    joint_weight,
    out_weight,
    up_weight,
    down_weight,
    first_gain,
    first_shift,
    query_bias,
    value_bias,
    out_bias,
    first_scale,
    second_gain,
    second_shift,
    up_bias,
    down_bias,
    second_scale,
    cotangent,
    sizes,
):
    fsdp, sub = sizes
    cube = Cube() if (fsdp, sub) == (8, 4) else None
    images_here, length, width = images.shape
    heads = width // HD
    rows = images_here * length
    hidden_units = up_weight.shape[1] * sub
    depth = width // ROW_TILES
    span = 3 * width // COL_TILES
    piece = width // COL_TILES
    part = hidden_units // PARTS
    lane = part // ROW_TILES
    steps = COL_TILES

    image_block = pl.BlockSpec((1, length, width), lambda i, *_: (i, 0, 0))
    row_block = pl.BlockSpec((length, width), lambda i, *_: (i, 0))
    column_block = pl.BlockSpec((width, length), lambda i, *_: (0, i))
    mixed_block = pl.BlockSpec((3 * width, length), lambda i, *_: (0, i))
    probs_block = pl.BlockSpec((1, heads, length, length), lambda i, *_: (i, 0, 0, 0))
    tall, wide = (rows, width), (width, rows)
    area = rows * width

    def input_norm(after):
        return launch(
            normalize_kernel,
            "first_norm",
            images_here,
            (),
            [images],
            [image_block],
            [(tall, F32), ((rows, 128), F32)],
            [row_block, pl.BlockSpec((length, 128), lambda i, *_: (i, 0))],
            (),
            (area * width, 8 * area),
            after,
            covers=LIGHT,
        )

    vectors = (first_gain, first_shift, query_bias, value_bias, out_bias, first_scale)
    vectors += (second_gain, second_shift, down_bias, second_scale)
    wide_span = span + 64

    if cube is not None:
        dest = cube.places()
        ins = [joint_weight, out_weight, *vectors, up_bias]
        first_piece = launch(
            pack_first_kernel,
            "pack_first",
            1,
            (),
            ins,
            [whole(v.shape) for v in ins],
            [((depth, wide_span + 2 * lane), BF)],
            [whole_out((depth, wide_span + 2 * lane))],
            (),
            (0, 4 * depth * wide_span),
        )[0]

        ins = [up_weight, down_weight.T]
        shape = (PARTS * 2 * depth, 2 * lane)
        feed_piece = launch(
            pack_kernel,
            "pack",
            1,
            (),
            ins,
            [whole(v.shape) for v in ins],
            [(shape, BF)],
            [whole_out(shape)],
            (),
            (0, 4 * math.prod(shape)),
        )[0]
        feed_pieces = lax.all_gather(feed_piece, BOTH, axis=0)

        normed_one, inverse_one = input_norm(())
        four = join(cube.gather_z(first_piece), (inverse_one,))
        near, far = cube.near(four), cube.far(four)
        far_near = cube.far(near)
        first = [four, near, far, far_near]
        first += [cube.over(v) for v in first]
        after_first = ()
    else:
        order = [p for p in range(PIECES) if p % 2 == 0] + [p for p in range(PIECES) if p % 2]
        back_order = [order.index(p) for p in range(PIECES)]
        dest = jnp.array(order, dtype=jnp.int32)
        normed_one, inverse_one = input_norm(())
        after_first = ()

        def fetch(value):
            return lax.all_gather(
                lax.all_gather(value, "sub", axis=1, tiled=True), "fsdp", axis=0, tiled=True
            )

        def cut(value, columns):
            value = value.reshape(ROW_TILES, depth, COL_TILES, columns)
            return value.transpose(0, 2, 1, 3).reshape(PIECES, depth, columns)

        def groups(value):
            value = jnp.stack([value[p] for p in order])
            return [value[i : i + GROUP] for i in range(0, PIECES, GROUP)]

        short = width // PIECES
        lines = [lax.all_gather(v, BOTH, axis=0, tiled=True) for v in vectors]
        lines = jnp.stack(lines).reshape(VECTORS, PIECES, short).transpose(1, 0, 2)
        lines = jnp.pad(lines, ((0, 0), (0, 0), (0, 64 - short)))
        long = lax.all_gather(up_bias, BOTH, axis=0, tiled=True).reshape(PIECES, 2, 2 * short)
        long = jnp.pad(long, ((0, 0), (0, 0), (0, 64 - 2 * short)))
        lines = jnp.concatenate([lines, long], axis=1)
        lines = jnp.pad(lines, ((0, 0), (0, depth - VECTORS - 2), (0, 0)))
        out_pieces = jnp.pad(cut(fetch(out_weight), piece), ((0, 0), (0, 0), (0, 2 * lane - piece)))
        first = [cut(fetch(joint_weight), span), lines, out_pieces]
        first = groups(jnp.concatenate(first, axis=2))
        up_parts = fetch(up_weight).reshape(ROW_TILES, depth, COL_TILES, 2, PARTS, lane)
        up_parts = up_parts.transpose(0, 2, 4, 1, 3, 5)
        down_parts = fetch(down_weight).reshape(ROW_TILES, PARTS, lane, COL_TILES, 2, depth)
        down_parts = down_parts.transpose(0, 3, 1, 5, 4, 2)
        shape = (PIECES, PARTS, depth, 2 * lane)
        feed_pieces = jnp.concatenate([up_parts.reshape(shape), down_parts.reshape(shape)], axis=2)
        feed_pieces = feed_pieces.reshape(PIECES, -1, 2 * lane)

    table_spec = whole((16, width))
    joint_scratch = [
        pltpu.VMEM((COL_TILES, ROW_TILES, depth, wide_span), BF),
        pltpu.SemaphoreType.DMA((PIECES,)),
    ]

    mixed, first_t, table, up_rows = launch(
        qkv_kernel,
        "qkv",
        images_here,
        (dest,),
        [normed_one, *first],
        [row_block] + [ANY] * GROUPS,
        [((3 * width, rows), BF), (wide, BF), ((16, width), F32), ((PARTS, part), F32)],
        [mixed_block, column_block, whole_out((16, width)), whole_out((PARTS, part))],
        joint_scratch,
        (6 * area * width, 14 * area),
        after_first,
        covers=LIGHT,
    )

    def attend(start, stop, into, after, covers):
        return launch(
            functools.partial(attention_kernel, start),
            "attention",
            stop - start,
            (counts,),
            [mixed, *into],
            [pl.BlockSpec((3 * width, length), lambda i, *_: (0, i + start))] + [ANY] * len(into),
            [(wide, BF), ((images_here, heads, length, length), BF)],
            [
                pl.BlockSpec((width, length), lambda i, *_: (0, i + start)),
                pl.BlockSpec((1, heads, length, length), lambda i, *_: (i + start, 0, 0, 0)),
            ],
            (),
            (16 * area * length // 2, 16 * area // 2),
            after,
            {2: 0, 3: 1} if into else None,
            covers,
        )

    attended, probs = attend(0, images_here, (), (), LIGHT)

    resid, branch, second, second_t, dfeed, dfeed_t, out_full = launch(
        second_kernel,
        "second_norm",
        images_here,
        (dest, counts),
        [images, cotangent, attended, table, *first],
        [image_block, image_block, column_block, table_spec] + [ANY] * GROUPS,
        [(tall, BF), (tall, BF), (tall, BF), (wide, BF), (tall, BF), (wide, BF)]
        + [((width, width), BF)],
        [row_block, row_block, row_block, column_block, row_block, column_block]
        + [whole_out((width, width))],
        [
            pltpu.VMEM((COL_TILES, ROW_TILES, depth, 2 * lane), BF),
            pltpu.SemaphoreType.DMA((PIECES,)),
            pltpu.VMEM((length, width), F32),
        ],
        (2 * area * width, 20 * area),
        covers=0.0,
    )

    def feed_forward(parts, carried, split, after=(), covers=1.0):
        ins = [up_rows, second, second_t, dfeed, dfeed_t, feed_pieces, *carried]
        count = len(parts)
        slots = (HALF if split else PIECES, count * 2 * depth, 2 * lane)
        tiles = rows // ROWS
        dma = pltpu.SemaphoreType.DMA
        return launch(
            functools.partial(mlp_kernel, parts, split),
            "feed_forward",
            1,
            (dest,),
            ins,
            [whole(up_rows.shape)] + [ANY] * (len(ins) - 1),
            [(tall, BF), (tall, BF), ((count, part), F32)] + [(slots, BF)] * (1 + split),
            [ANY, ANY, whole_out((count, part))] + [ANY] * (1 + split),
            [
                pltpu.VMEM((2, rows, width), BF),
                pltpu.VMEM((2, width, rows), BF),
                pltpu.VMEM((2, rows, width), BF),
                pltpu.VMEM((count, 2, width, part), BF),
                pltpu.VMEM((rows, part), BF),
                pltpu.VMEM((rows, part), BF),
                pltpu.VMEM((count, 2, width, part), BF),
                dma((count, PIECES, 2)),
                dma((2, tiles)),
                dma((2,)),
                dma((2, tiles)),
                dma((count, PIECES, 2)),
            ],
            (12 * area * part * count, 20 * area),
            after,
            covers=covers,
        )

    early = tuple(range(PARTS - 1))
    feed, dsecond, early_bias, early_grads = feed_forward(early, (), False, (), 0.0)
    feed, dsecond, late_bias, *late_grads = feed_forward(
        (PARTS - 1,), (feed, dsecond), True, (early_grads,)
    )

    waits = {}
    if cube is not None:
        early_total = lax.psum_scatter(early_grads, BOTH, scatter_dimension=0)
        late_got = cube.over(late_grads[1])

    block_out, dresid, dattended, out_grad, middle_sums = launch(
        middle_kernel,
        "middle",
        images_here,
        (counts,),
        [cotangent, feed, dsecond, resid, branch, attended, out_full, table],
        [image_block, row_block, row_block, row_block, row_block, column_block]
        + [whole((width, width)), table_spec],
        [(images.shape, BF), (tall, BF), (wide, BF), ((width, width), BF), ((8, width), F32)],
        [image_block, row_block, column_block, whole_out((width, width)), whole_out((8, width))],
        [
            pltpu.VMEM((width, width), F32),
            pltpu.VMEM((6, 8, width), F32),
            pltpu.VMEM((length, width), BF),
        ],
        (4 * area * width, 30 * area),
        waits.get("middle", ()),
    )

    if cube is not None:
        late_low, late_high = add_halves(late_grads[0], None, late_got, (dresid,))
        late_got = cube.far(late_high)
        waits["attention_back"] = (late_high,)

    dmixed, attention_sums, send_first = launch(
        attention_back_kernel,
        "attention_back",
        images_here,
        (dest,),
        [mixed, probs, attended, dattended, first_t, out_grad],
        [mixed_block, probs_block, column_block, column_block, ANY, ANY],
        [((3 * width, rows), BF), ((8, width), F32), ((HALF, depth, width), BF)],
        [mixed_block, whole_out((8, width)), ANY],
        [
            pltpu.VMEM((width, 128), F32),
            pltpu.VMEM((width, 128), F32),
            pltpu.VMEM((heads, length, length), BF),
            pltpu.VMEM((images_here, 3 * width, length), BF),
            pltpu.VMEM((width, rows), BF),
            pltpu.VMEM((width, width), BF),
            pltpu.VMEM((2, width, width), BF),
            pltpu.SemaphoreType.DMA((2 + HALF,)),
        ],
        (32 * area * length, 24 * area),
        waits.get("attention_back", ()),
    )

    if cube is not None:
        late_low, late_high = add_halves(late_low, None, late_got, (dmixed,))
        late_got = cube.near(late_high)
        waits["joint_grad"] = (late_high,)

    if cube is not None:
        first_got = cube.over(send_first)

    def column_tile(g):
        return pl.BlockSpec((span, rows), lambda _, dest: (2 * g + lax.rem(dest[0], 2), 0))

    keep_first = launch(
        joint_grad_kernel,
        "joint_grad",
        1,
        (dest,),
        [first_t, dmixed, dmixed, out_grad],
        [whole(wide), column_tile(0), column_tile(1), whole((width, width))],
        [((HALF, depth, width), BF)],
        [ANY],
        [pltpu.VMEM((2, width, width), BF), pltpu.SemaphoreType.DMA((HALF,))],
        (3 * area * width, 10 * area),
        waits.get("joint_grad", ()),
    )[0]

    after_input = ()
    if cube is not None:
        first_low, first_high = add_halves(keep_first, None, first_got)
        first_got = cube.far(first_high)
        late_last = add_four(late_low, late_got, (first_high,))
        late_terms = cube.reduce_z(late_last)
        after_input = (late_last[0],)

    image_grad, input_sums = launch(
        input_grad_kernel,
        "input_grad",
        images_here,
        (dest,),
        [normed_one, inverse_one, dresid, dmixed, table, *first],
        [row_block, pl.BlockSpec((length, 128), lambda i, *_: (i, 0)), row_block, mixed_block]
        + [table_spec]
        + [ANY] * GROUPS,
        [(images.shape, F32), ((8, width), F32)],
        [image_block, whole_out((8, width))],
        joint_scratch
        + [pltpu.VMEM((2, 8, width), F32), pltpu.VMEM((length, width), F32)],
        (6 * area * width, 20 * area),
        after_input,
    )

    after = ()
    if cube is not None:
        first_low, first_high = add_halves(first_low, None, first_got, (image_grad,))
        first_got = cube.near(first_high)
        after = (first_high,)
    ins = [input_sums, attention_sums, middle_sums, early_bias, late_bias]
    sums = launch(
        collect_kernel,
        "collect",
        1,
        (),
        ins,
        [whole(v.shape) for v in ins],
        [((16, width), F32)],
        [whole_out((16, width))],
        (),
        (10**8, 0),
        after,
    )[0]
    short = first_gain.shape[0]
    if cube is not None:
        late_total = totals(
            late_total_kernel, "late_total", late_terms, (late_terms[0].shape,), (image_grad,)
        )
        first_last = add_four(first_low, first_got, (sums, *late_total))
        first_terms = cube.reduce_z(first_last)
        sums = cube.total(sums, cube.z[:2])
        sums = gate(sums, first_last[:1], 5.0)
        sums = cube.total(sums, (cube.core, cube.x, cube.y))
        joint_grad, out_weight_grad = totals(
            first_total_kernel,
            "first_total",
            first_terms,
            (joint_weight.shape, out_weight.shape),
        )
        device = lax.axis_index("fsdp") * sub + lax.axis_index("sub")
        vectors = lax.dynamic_slice(sums[:10], (0, device * short), (10, short))
        up_bias_grad = lax.dynamic_slice(
            sums[VECTORS : VECTORS + 4].reshape(-1), (device * up_bias.shape[0],), up_bias.shape
        )
        up_grad, down_grad = totals(
            feed_total_kernel,
            "feed_total",
            (early_total, *late_total),
            (up_weight.shape, down_weight.shape[::-1]),
            first_last[:1],
        )
        down_grad = down_grad.T
    else:

        def hand_out(value):
            value = lax.psum_scatter(value.astype(BF), "fsdp", scatter_dimension=0, tiled=True)
            value = lax.psum_scatter(value, "sub", scatter_dimension=1, tiled=True)
            return value.astype(F32)

        def uncut(value, columns):
            value = value.reshape(ROW_TILES, COL_TILES, depth, columns)
            return value.transpose(0, 2, 1, 3).reshape(width, COL_TILES * columns)

        def in_order(value):
            return jnp.stack([value[i] for i in back_order])

        grads = in_order(jnp.concatenate([keep_first, send_first]))
        joint_grad = hand_out(uncut(grads[:, :, :span], span))
        out_weight_grad = hand_out(uncut(grads[:, :, span:], piece))
        late_grads = in_order(jnp.concatenate(late_grads))
        grads = jnp.concatenate([early_grads, late_grads], axis=1)
        grads = grads.reshape(ROW_TILES, COL_TILES, PARTS, 2, depth, 2, lane)
        up_grad = grads[:, :, :, 0].transpose(0, 3, 1, 4, 2, 5).reshape(width, hidden_units)
        down_grad = grads[:, :, :, 1].transpose(0, 2, 5, 1, 4, 3).reshape(hidden_units, width)
        up_grad, down_grad = hand_out(up_grad), hand_out(down_grad)

        def hand_vector(value):
            return lax.psum_scatter(value, BOTH, scatter_dimension=0, tiled=True)

        vectors = [hand_vector(sums[v]) for v in range(10)]
        up_bias_grad = hand_vector(sums[VECTORS : VECTORS + 4].reshape(-1))
    return (
        block_out,
        image_grad,
        joint_grad,
        out_weight_grad,
        up_grad,
        down_grad,
        vectors[0],
        vectors[1],
        vectors[2],
        vectors[3],
        vectors[4],
        vectors[5],
        vectors[6],
        vectors[7],
        up_bias_grad,
        vectors[8],
        vectors[9],
    )


def solution(mesh):
    rows = P(BOTH, None, None)
    matrix = P("fsdp", "sub")
    vector = P(BOTH)
    sizes = (mesh.shape["fsdp"], mesh.shape["sub"])
    return jax.shard_map(
        functools.partial(shards, sizes=sizes),
        mesh=mesh,
        in_specs=(rows, vector) + (matrix,) * 4 + (vector,) * 11 + (rows,),
        out_specs=(rows, rows) + (matrix,) * 4 + (vector,) * 11,
        check_vma=False,
    )
```

```python
import functools
import math

import jax
import jax.numpy as jnp
from jax import lax
from jax.experimental import pallas as pl
from jax.experimental.pallas import tpu as pltpu
from jax.sharding import PartitionSpec as P

HD = 64
EPS = 1e-06
NEGATIVE = -1e30
ROW_TILES = 8
COL_TILES = 4
PIECES = ROW_TILES * COL_TILES
HALF = PIECES // 2
ROWS = 512
CHUNK = 64
GROUP = 4
GROUPS = PIECES // GROUP
VECTORS = 10
PARTS = 3
BOTH = ("fsdp", "sub")
LIGHT = 0.08
SLACK = 100
VMEM_LIMIT = 56 * 1024 * 1024
BF = jnp.bfloat16
F32 = jnp.float32
NT = (((1,), (1,)), ((), ()))
TN = (((0,), (0,)), ((), ()))


def dot(left, right):
    return jnp.dot(left, right, preferred_element_type=F32)


def dot_general(left, right, dims):
    return lax.dot_general(left, right, dims, preferred_element_type=F32)


def launch(
    kernel, name, grid, scalars, ins, specs, outs, out_specs, scratch, price, after=(), aliases=None, covers=1.0
):
    known = len(scalars) + len(ins)

    def body(*refs):
        kernel(*refs[:known], *refs[known + len(after) :])

    return pl.pallas_call(
        body,
        grid_spec=pltpu.PrefetchScalarGridSpec(
            num_scalar_prefetch=len(scalars),
            grid=(grid,),
            in_specs=list(specs) + [ANY] * len(after),
            out_specs=list(out_specs),
            scratch_shapes=list(scratch),
        ),
        out_shape=[jax.ShapeDtypeStruct(shape, dtype) for shape, dtype in outs],
        input_output_aliases=aliases or {},
        compiler_params=pltpu.CompilerParams(
            dimension_semantics=("arbitrary",), vmem_limit_bytes=VMEM_LIMIT
        ),
        cost_estimate=pl.CostEstimate(
            flops=int(SLACK * covers * price[0]), bytes_accessed=price[1], transcendentals=0
        ),
        name=name,
    )(*scalars, *ins, *after)


def normalize(rows):
    centre = rows - jnp.mean(rows, axis=-1, keepdims=True)
    spread = jnp.mean(centre * centre, axis=-1, keepdims=True)
    inverse = lax.rsqrt(spread + EPS)
    return (centre * inverse, inverse)


def norm_back(upstream, normed, inverse, gain):
    scaled = upstream * gain
    return inverse * (
        scaled
        - jnp.mean(scaled, axis=-1, keepdims=True)
        - normed * jnp.mean(scaled * normed, axis=-1, keepdims=True)
    )


def eight_sum(values):
    return jnp.sum(values.reshape(-1, 8, values.shape[-1]), axis=0)


def row_sum(values):
    return jnp.sum(values, axis=0, keepdims=True)


def whole(shape):
    zeros = (0,) * len(shape)
    return pl.BlockSpec(shape, lambda *_: zeros, pipeline_mode=pl.Buffered(1))


def whole_out(shape):
    zeros = (0,) * len(shape)
    return pl.BlockSpec(shape, lambda *_: zeros)


ANY = pl.BlockSpec(memory_space=pl.ANY)


def stage_pieces(places, sources, weights, sems, low=0):
    wide = weights.shape[-1]
    copies = []
    for i, place in enumerate(places):
        copies.append(
            pltpu.make_async_copy(
                sources(i).at[:, pl.ds(low, wide)],
                weights.at[lax.rem(place, COL_TILES), lax.div(place, COL_TILES)],
                sems.at[i],
            )
        )
    for copy in copies:
        copy.start()
    for copy in copies:
        copy.wait()


def grouped(dest, refs):
    return [dest[i] for i in range(PIECES)], lambda i: refs[i // GROUP].at[i % GROUP]


def columns_of(weights, s):
    _, tiles, depth, wide = weights.shape
    return weights[s].reshape(tiles * depth, wide)


def join_kernel(*refs):
    *pieces, out = refs
    for i, piece in enumerate(pieces):
        out[i] = piece[...]


def pack_first_kernel(joint_weight, out_weight, *refs):
    *vectors, long, packed = refs
    depth, span = joint_weight.shape
    rest = 64
    packed[:, :span] = joint_weight[...]
    packed[:, span + rest :] = jnp.zeros((depth, packed.shape[1] - span - rest), BF)
    packed[:, span + rest : span + rest + out_weight.shape[1]] = out_weight[...]
    half = long.shape[0] // 2
    lines = [vector[...].astype(F32).reshape(1, -1) for vector in vectors]
    both = long[...].astype(F32).reshape(1, -1)
    lines += [both[:, :half], both[:, half:]]
    lines = [jnp.pad(line, ((0, 0), (0, rest - line.shape[1]))) for line in lines]
    lines.append(jnp.zeros((16 - len(lines), rest), F32))
    packed[:, span : span + rest] = jnp.zeros((depth, rest), BF)
    packed[0:16, span : span + rest] = jnp.concatenate(lines).astype(BF)


def pack_kernel(up_weight, down_t, packed):
    depth, units = up_weight.shape
    lane = units // PARTS // 2
    for j in range(PARTS):
        at = 2 * j * depth
        low = j * lane
        for h in range(2):
            lanes = slice(h * lane, (h + 1) * lane)
            packed[at : at + depth, lanes] = up_weight[
                :, h * units // 2 + low : h * units // 2 + low + lane
            ]
            packed[at + depth : at + 2 * depth, lanes] = down_t[
                h * depth : (h + 1) * depth, low : low + lane
            ]


def add_kernel(low, high, got_low, got_high, low_out, high_out):
    low_out[...] = (low[...].astype(F32) + got_low[...].astype(F32)).astype(BF)
    high_out[...] = (high[...].astype(F32) + got_high[...].astype(F32)).astype(BF)


def add_four_kernel(keep, got, *outs):
    for k, out in enumerate(outs[-4:]):
        out[...] = (keep[k].astype(F32) + got[k].astype(F32)).astype(BF)


def sum_of(refs):
    return sum(ref[...].astype(F32) for ref in refs)


def late_total_kernel(*refs):
    refs[-1][...] = sum_of(refs[:-1])


def first_total_kernel(a, b, c, d, joint_grad, out_grad):
    total = sum_of((a, b, c, d))
    span = joint_grad.shape[1]
    joint_grad[...] = total[:, :span]
    out_grad[...] = total[:, span:]


def feed_total_kernel(*refs):
    *terms, up_grad, down_grad = refs
    depth, units = up_grad.shape
    lane = units // PARTS // 2
    total = jnp.concatenate([term[...].astype(F32) for term in terms])
    tall = []
    for j in range(PARTS):
        at = 2 * j * depth
        for h in range(2):
            lanes = slice(h * lane, (h + 1) * lane)
            low = h * units // 2 + j * lane
            up_grad[:, low : low + lane] = total[at : at + depth, lanes]
        at += depth
        tall.append(
            jnp.concatenate([total[at : at + depth, :lane], total[at : at + depth, lane:]])
        )
    wide = jnp.concatenate(tall, axis=1)
    down_grad[...] = wide


def normalize_kernel(images, normed_out, inverse_out):
    normed, inverse = normalize(images[0].astype(F32))
    normed_out[...] = normed
    inverse_out[...] = jnp.broadcast_to(inverse, inverse_out.shape)


def qkv_kernel(dest, normed, *refs):
    *sources, mixed, first_t, table, up_rows, weights, sems = refs
    width = normed.shape[-1]
    span = 3 * width // COL_TILES
    short = width // PIECES
    lane = 128

    @pl.when(pl.program_id(0) == 0)
    def _():
        stage_pieces(*grouped(dest, sources), weights, sems)
        lines = []
        long = []
        for place in range(PIECES):
            block = weights[place % COL_TILES, place // COL_TILES, 0:16, span:].astype(F32)
            lines.append(block[:, :short])
            long += [block[VECTORS : VECTORS + 1, : 2 * short]]
            long += [block[VECTORS + 1 : VECTORS + 2, : 2 * short]]
        table[...] = jnp.concatenate(lines, axis=1)
        long = jnp.concatenate(long, axis=1)
        for j in range(PARTS):
            for m in range(ROW_TILES):
                up_rows[j : j + 1, m * lane : (m + 1) * lane] = long[:, (m * PARTS + j) * lane : (m * PARTS + j + 1) * lane]

    bias = jnp.concatenate([table[2:3], jnp.zeros((1, width), F32), table[3:4]], axis=1)
    first = (normed[...] * table[0:1] + table[1:2]).astype(BF)
    first_t[...] = first.T
    for s in range(COL_TILES):
        out = dot(first, columns_of(weights, s)[:, :span])
        out = (out + bias[:, s * span : (s + 1) * span]).astype(BF)
        mixed[s * span : (s + 1) * span, :] = out.T


def attention_kernel(start, counts, mixed, *refs):
    attended, probs = refs[-2:]
    width = attended.shape[0]
    length = mixed.shape[1]
    scale = math.log2(math.e) / math.sqrt(HD)
    count = counts[pl.program_id(0) + start]
    valid = lax.broadcasted_iota(jnp.int32, (length, length), 0) < count
    for h in range(width // HD):
        query = mixed[h * HD : (h + 1) * HD, :]
        key = mixed[width + h * HD : width + (h + 1) * HD, :]
        scores = jnp.where(valid, dot_general(key, query, TN), NEGATIVE)
        largest = jnp.max(scores, axis=0, keepdims=True)
        expon = jnp.exp2((scores - largest) * scale)
        probs[0, h] = (expon * (1.0 / jnp.sum(expon, axis=0, keepdims=True))).astype(BF)
    for h in range(width // HD):
        value = mixed[2 * width + h * HD : 2 * width + (h + 1) * HD, :]
        attended[h * HD : (h + 1) * HD, :] = dot(value, probs[0, h]).astype(BF)


def second_kernel(dest, counts, images, cotangent, attended, table, *refs):
    sources, refs = refs[:GROUPS], refs[GROUPS:]
    resid_out, branch_out, second, second_t, dfeed_out, dfeed_t, out_full, *refs = refs
    weights, sems, branch_all = refs
    width = images.shape[-1]
    length = images.shape[1]
    piece = width // COL_TILES

    @pl.when(pl.program_id(0) == 0)
    def _():
        low = 3 * width // COL_TILES + 64
        stage_pieces(*grouped(dest, sources), weights, sems, low)
        for s in range(COL_TILES):
            out_full[:, s * piece : (s + 1) * piece] = columns_of(weights, s)[:, :piece]

    branch_all[...] = dot_general(attended[...], out_full[...], TN)
    for low in range(0, length, CHUNK):
        rows = slice(low, low + CHUNK)
        branch = branch_all[rows, :] + table[4:5]
        branch_out[rows, :] = branch.astype(BF)
        resid = images[0, rows, :].astype(F32) + table[5:6] * branch
        resid_out[rows, :] = resid.astype(BF)
        normed, _ = normalize(resid)
        second[rows, :] = (normed * table[6:7] + table[7:8]).astype(BF)
        places = low + lax.broadcasted_iota(jnp.int32, (CHUNK, 1), 0)
        mask = (places < counts[pl.program_id(0)]).astype(F32)
        dfeed_out[rows, :] = (cotangent[0, rows, :].astype(F32) * mask * table[9:10]).astype(BF)
    second_t[...] = second[...].T
    dfeed_t[...] = dfeed_out[...].T


def gelu_pair(value):
    size = jnp.abs(value)
    t = 1.0 / (1.0 + (0.3275911 / math.sqrt(2.0)) * size)
    bell = jnp.exp2(value * value * (-0.5 * math.log2(math.e)))
    poly = 0.5 * 1.061405429
    for c in (-1.453152027, 1.421413741, -0.284496736, 0.254829592):
        poly = poly * t + 0.5 * c
    tail = poly * t * bell
    cumul = jnp.where(value >= 0, 1.0 - tail, tail)
    return value * cumul, cumul + value * bell * (1.0 / math.sqrt(2.0 * math.pi))


def mlp_kernel(parts, split, dest, bias, second, second_t, dfeed, dfeed_t, gathered, *rest):
    first = parts[0] == 0
    if not first:
        carried, rest = rest[:2], rest[2:]
    feed, dsecond, bias_grad, *rest = rest
    if split:
        keep, send, *rest = rest
    else:
        grads, *rest = rest
    rows_in, rows_t, sums, weights, hidden, dpre, weight_grads, *sems = rest
    piece_sem, row_sem, turned_sem, sum_sem, out_sem = sems
    count, width = second.shape
    depth = width // ROW_TILES
    span = width // COL_TILES
    wide = weights.shape[-1]
    lane = wide // ROW_TILES
    tile = ROWS
    tiles = count // tile

    def moves(place, buffer, outside, origin, sem, inward):
        m = lax.div(place, COL_TILES)
        s = lax.rem(place, COL_TILES)
        copies = [
            (
                outside.at[pl.ds(origin, depth), :],
                buffer.at[
                    0,
                    pl.ds(pl.multiple_of(m * depth, 16), depth),
                    pl.ds(pl.multiple_of(s * 2 * lane, 128), 2 * lane),
                ],
                sem.at[0],
            )
        ]
        for h in range(2):
            copies.append(
                (
                    outside.at[pl.ds(origin + depth, depth), pl.ds(h * lane, lane)],
                    buffer.at[
                        1,
                        pl.ds(pl.multiple_of(s * span + h * depth, 16), depth),
                        pl.ds(pl.multiple_of(m * lane, 128), lane),
                    ],
                    sem.at[1],
                )
            )
        return [
            pltpu.make_async_copy(*((a, b) if inward else (b, a)), sem) for a, b, sem in copies
        ]

    def run(copies):
        for copy in copies:
            copy.start()
        return copies

    def wait(copies):
        for copy in copies:
            copy.wait()

    def row_copies(r, sources, targets, sem):
        rows = pl.ds(r * tile, tile)
        return [
            pltpu.make_async_copy(a.at[rows, :], b.at[rows, :], sem.at[i, r])
            for i, (a, b) in enumerate(zip(sources, targets))
        ]

    rows_in = (rows_in.at[0], rows_in.at[1])
    rows_t = (rows_t.at[0], rows_t.at[1])
    sums = (sums.at[0], sums.at[1])

    def arrivals(n):
        every = [
            moves(
                i,
                weights.at[n],
                gathered.at[i],
                2 * depth * parts[n],
                piece_sem.at[n, i],
                True,
            )
            for i in range(PIECES)
        ]
        return [c[0] for c in every], [c for copies in every for c in copies[1:]]

    coming = [arrivals(n) for n in range(len(parts))]
    arriving = [row_copies(r, (second, dfeed), rows_in, row_sem) for r in range(tiles)]
    turned = [
        pltpu.make_async_copy(a, b, turned_sem.at[i])
        for i, (a, b) in enumerate(zip((second_t, dfeed_t), rows_t))
    ]
    partial = [] if first else [row_copies(r, carried, sums, sum_sem) for r in range(tiles)]
    later = arriving[1:] + partial + [turned] + [c for two in coming[1:] for c in two]
    run(coming[0][0])
    run(arriving[0])
    run(coming[0][1])
    leaving = []
    for n, part in enumerate(parts):
        up, down = weights.at[n, 0], weights.at[n, 1]
        up_grad, down_grad = weight_grads.at[n, 0], weight_grads.at[n, 1]
        wait(coming[n][0])
        add = bias[part : part + 1, :]
        total = jnp.zeros((1, wide), F32)
        for r in range(tiles):
            rows = slice(r * tile, (r + 1) * tile)
            if n == 0:
                wait(arriving[r])
                ahead = -(-len(later) // (tiles - r))
                for copies in later[:ahead]:
                    run(copies)
                later = later[ahead:]
            pre = dot(rows_in[0][rows, :], up[...]) + add
            if r == 0:
                wait(coming[n][1])
            back = dot(rows_in[1][rows, :], down[...])
            value, slope = gelu_pair(pre)
            hidden[rows, :] = value.astype(BF)
            back = (back * slope).astype(BF)
            dpre[rows, :] = back
            total = total + row_sum(back.astype(F32))
        bias_grad[n : n + 1, :] = total
        for r in range(tiles):
            rows = slice(r * tile, (r + 1) * tile)
            forward = dot_general(hidden[rows, :], down[...], NT)
            back = dot_general(dpre[rows, :], up[...], NT)
            if not first and n == 0:
                wait(partial[r])
            if not first or n > 0:
                forward = forward + sums[0][rows, :].astype(F32)
                back = back + sums[1][rows, :].astype(F32)
            sums[0][rows, :] = forward.astype(BF)
            sums[1][rows, :] = back.astype(BF)
            if n == len(parts) - 1:
                leaving += run(row_copies(r, sums, (feed, dsecond), sum_sem))
        if n == 0:
            wait(turned)
        up_grad[...] = dot(rows_t[0][...], dpre[...]).astype(BF)
        outs = [
            moves(
                dest[i] if split else i,
                weight_grads.at[n],
                (keep if i < HALF else send).at[i % HALF] if split else grads.at[i],
                2 * depth * n,
                out_sem.at[n, i],
                False,
            )
            for i in range(PIECES)
        ]
        for copies in outs:
            leaving += run(copies[:1])
        down_grad[...] = dot(rows_t[1][...], hidden[...]).astype(BF)
        for copies in outs:
            leaving += run(copies[1:])
    wait(leaving)


def middle_kernel(
    counts,
    cotangent,
    feed,
    dsecond,
    resid,
    branch,
    attended,
    out_full,
    table,
    block_out,
    dresid_out,
    dattended,
    out_grad,
    sums,
    total,
    partial,
    dbranch_all,
):
    length = cotangent.shape[1]
    step = pl.program_id(0)

    @pl.when(step == 0)
    def _():
        total[...] = jnp.zeros(total.shape, F32)
        partial[...] = jnp.zeros(partial.shape, F32)

    for low in range(0, length, CHUNK):
        rows = slice(low, low + CHUNK)
        places = low + lax.broadcasted_iota(jnp.int32, (CHUNK, 1), 0)
        mask = (places < counts[step]).astype(F32)
        feed_out = feed[rows, :].astype(F32) + table[8:9]
        grad = cotangent[0, rows, :].astype(F32) * mask
        value = resid[rows, :].astype(F32)
        block_out[0, rows, :] = ((value + table[9:10] * feed_out) * mask).astype(BF)
        normed, inverse = normalize(value)
        upstream = dsecond[rows, :].astype(F32)
        dresid = grad + norm_back(upstream, normed, inverse, table[6:7])
        dresid_out[rows, :] = dresid.astype(BF)
        dbranch = (dresid * table[5:6]).astype(BF)
        dbranch_all[rows, :] = dbranch
        dfeed = (grad * table[9:10]).astype(BF)
        partial[0] += eight_sum(dbranch.astype(F32))
        partial[1] += eight_sum(dresid * branch[rows, :].astype(F32))
        partial[2] += eight_sum(upstream * normed)
        partial[3] += eight_sum(upstream)
        partial[4] += eight_sum(dfeed.astype(F32))
        partial[5] += eight_sum(grad * feed_out)
    dbranch = dbranch_all[...]
    total[...] += dot(attended[...], dbranch)
    dattended[...] = dot_general(out_full[...], dbranch, NT).astype(BF)

    @pl.when(step == pl.num_programs(0) - 1)
    def _():
        out_grad[...] = total[...].astype(BF)
        sums[...] = jnp.zeros(sums.shape, F32)
        for n in range(6):
            sums[n : n + 1] = row_sum(partial[n])


def attention_back_kernel(
    dest,
    mixed,
    probs,
    attended,
    dattended,
    first_t,
    out_grad,
    dmixed,
    sums,
    send,
    dquery_sum,
    dvalue_sum,
    dscores,
    every,
    first_here,
    out_here,
    grads,
    sems,
):
    width = attended.shape[0]
    length = mixed.shape[1]
    heads = width // HD
    factor = 1.0 / math.sqrt(HD)
    step = pl.program_id(0)
    wanted = [
        pltpu.make_async_copy(first_t, first_here, sems.at[0]),
        pltpu.make_async_copy(out_grad, out_here, sems.at[1]),
    ]

    @pl.when(step == 0)
    def _():
        for copy in wanted:
            copy.start()
        dquery_sum[...] = jnp.zeros(dquery_sum.shape, F32)
        dvalue_sum[...] = jnp.zeros(dvalue_sum.shape, F32)

    def part(block, h):
        return slice(block * width + h * HD, block * width + (h + 1) * HD)

    def fold(values):
        return sum(values[:, a : a + 128].astype(F32) for a in range(0, length, 128))

    def score_grads(h):
        upstream = dattended[part(0, h), :]
        delta = row_sum(upstream.astype(F32) * attended[part(0, h), :].astype(F32))
        dprobs = dot_general(mixed[part(2, h), :], upstream, TN)
        dscores[h] = (probs[0, h].astype(F32) * (dprobs - delta)).astype(BF)

    score_grads(0)
    for h in range(heads):
        if h + 1 < heads:
            score_grads(h + 1)
        dvalue = dot_general(dattended[part(0, h), :], probs[0, h], NT)
        dkey = dot_general(mixed[part(0, h), :], dscores[h], NT) * factor
        dquery = dot(mixed[part(1, h), :], dscores[h]) * factor
        dmixed[part(2, h), :] = dvalue.astype(BF)
        dmixed[part(1, h), :] = dkey.astype(BF)
        dmixed[part(0, h), :] = dquery.astype(BF)
    dquery_sum[...] += fold(dmixed[0:width, :])
    dvalue_sum[...] += fold(dmixed[2 * width :, :])
    every[step] = dmixed[...]

    @pl.when(step == pl.num_programs(0) - 1)
    def _():
        sums[...] = jnp.zeros(sums.shape, F32)
        sums[0:1] = row_sum(dquery_sum[...].T)
        sums[1:2] = row_sum(dvalue_sum[...].T)
        for copy in wanted:
            copy.wait()
        span = 3 * width // COL_TILES
        for g in range(2):
            low = (2 * g + lax.rem(dest[0] + 1, 2)) * span
            rows = pl.ds(pl.multiple_of(low, 16), span)
            part = jnp.concatenate([every[i, rows, :] for i in range(every.shape[0])], axis=1)
            put_joint_grad(1, g, dest, first_here[...], part, out_here, grads)
        leave(1, dest, grads, send, sems, 2)


def put_joint_grad(offset, g, dest, first_t, dmixed, out_grad, grads):
    width = grads.shape[1]
    span = dmixed.shape[0]
    piece = width - span
    low = 2 * g * piece
    odd = lax.rem(dest[0] + offset, 2) == 1
    grads[g, :, span:] = jnp.where(
        odd, out_grad[:, low + piece : low + 2 * piece], out_grad[:, low : low + piece]
    )
    grads[g, :, 0:span] = dot_general(first_t, dmixed, NT).astype(BF)


def leave(offset, dest, grads, out, sems, first_sem):
    depth = grads.shape[1] // ROW_TILES
    copies = []
    for i in range(HALF):
        place = dest[offset * HALF + i]
        m = lax.div(place, COL_TILES)
        near = grads.at[
            lax.div(lax.rem(place, COL_TILES), 2),
            pl.ds(pl.multiple_of(m * depth, 16), depth),
            :,
        ]
        copies.append(pltpu.make_async_copy(near, out.at[i], sems.at[first_sem + i]))
    for copy in copies:
        copy.start()
    for copy in copies:
        copy.wait()


def joint_grad_kernel(dest, first_t, low_tile, high_tile, out_grad, out, grads, sems):
    for g, dmixed in enumerate((low_tile, high_tile)):
        put_joint_grad(0, g, dest, first_t[...], dmixed[...], out_grad, grads)
    leave(0, dest, grads, out, sems, 0)


def collect_kernel(input_sums, attention_sums, middle_sums, *refs):
    *bias_sums, out = refs
    lane = bias_sums[0].shape[1] // ROW_TILES
    out[0:2] = input_sums[0:2]
    out[2:4] = attention_sums[0:2]
    out[4:VECTORS] = middle_sums[0 : VECTORS - 4]
    out[VECTORS:] = jnp.zeros((16 - VECTORS, out.shape[1]), F32)
    bias_rows = [sums[n : n + 1, :] for sums in bias_sums for n in range(sums.shape[0])]
    for j, sums in enumerate(bias_rows):
        for m in range(ROW_TILES):
            at = (m * PARTS + j) * lane
            row, column = divmod(at, out.shape[1])
            out[VECTORS + row : VECTORS + row + 1, column : column + lane] = sums[
                :, m * lane : (m + 1) * lane
            ]


def input_grad_kernel(dest, normed, inverse, dresid, dmixed, table, *refs):
    *sources, image_grad, sums, weights, sems, partial, back_all = refs
    width = normed.shape[-1]
    span = 3 * width // COL_TILES

    @pl.when(pl.program_id(0) == 0)
    def _():
        stage_pieces(*grouped(dest, sources), weights, sems)
        partial[...] = jnp.zeros(partial.shape, F32)

    back = None
    for s in range(COL_TILES):
        part = dot(
            columns_of(weights, s)[:, :span], dmixed[s * span : (s + 1) * span, :]
        )
        back = part if back is None else back + part
    back_all[...] = back.T
    for low in range(0, back_all.shape[0], CHUNK):
        rows = slice(low, low + CHUNK)
        upstream = back_all[rows, :]
        value = normed[rows, :]
        partial[0] += eight_sum(upstream * value)
        partial[1] += eight_sum(upstream)
        image_grad[0, rows, :] = dresid[rows, :].astype(F32) + norm_back(
            upstream, value, inverse[rows, 0:1], table[0:1]
        )

    @pl.when(pl.program_id(0) == pl.num_programs(0) - 1)
    def _():
        sums[...] = jnp.zeros(sums.shape, F32)
        for n in range(2):
            sums[n : n + 1] = row_sum(partial[n])


def flat_pairs(fsdp, sub, there):
    return [(f * sub + s, there(f, s)) for f in range(fsdp) for s in range(sub)]


class Cube:
    def __init__(self):
        def along_z(k):
            return flat_pairs(8, 4, lambda f, s: (f ^ (2 * k)) * 4 + s)

        def y_or_x(order):
            def there(f, s):
                turn = (s % 2) ^ order
                return (f * 4 + (s ^ 2)) if turn else ((f ^ 1) * 4 + s)

            return flat_pairs(8, 4, there)

        self.z = [along_z(k) for k in (1, 2, 3)]
        self.plane = [y_or_x(0), y_or_x(1)]
        self.core = flat_pairs(8, 4, lambda f, s: f * 4 + (s ^ 1))
        self.y = flat_pairs(8, 4, lambda f, s: (f ^ 1) * 4 + s)
        self.x = flat_pairs(8, 4, lambda f, s: f * 4 + (s ^ 2))

    def swap(self, value, pairs):
        return lax.ppermute(value, BOTH, pairs)

    def places(self):
        f = lax.axis_index("fsdp")
        s = lax.axis_index("sub")
        z, y, x, c = f // 2, f % 2, s // 2, s % 2

        def slot_to_place(i):
            core = c ^ (i // 16)
            far, near, dz = (i // 8) % 2, (i // 4) % 2, i % 4
            dy = jnp.where(core == 0, near, far)
            dx = jnp.where(core == 0, far, near)
            return ((z ^ dz) * 2 + (y ^ dy)) * 4 + (x ^ dx) * 2 + core

        index = jnp.arange(PIECES, dtype=jnp.int32)
        return slot_to_place(index)

    def near(self, value):
        return self.swap(value, self.plane[0])

    def far(self, value):
        return self.swap(value, self.plane[1])

    def over(self, value):
        return self.swap(value, self.core)

    def gather_z(self, piece):
        return (piece,) + tuple(self.swap(piece, pairs) for pairs in self.z)

    def reduce_z(self, four):
        return (four[0],) + tuple(self.swap(four[k], self.z[k - 1]) for k in (1, 2, 3))

    def total(self, value, stages):
        for pairs in stages:
            value = value + self.swap(value, pairs)
        return value


def join(pieces, after=()):
    shape = (len(pieces),) + pieces[0].shape
    return launch(
        join_kernel,
        "join",
        1,
        (),
        list(pieces),
        [whole(piece.shape) for piece in pieces],
        [(shape, BF)],
        [whole_out(shape)],
        (),
        (0, 4 * math.prod(shape)),
        after,
    )[0]


def gate_kernel(value, out):
    del value, out


def gate(value, after, covers=0.0):
    return launch(
        gate_kernel,
        "gate",
        1,
        (),
        [value],
        [ANY],
        [(value.shape, value.dtype)],
        [ANY],
        (),
        (10**8, 0),
        after,
        {0: 0},
        covers,
    )[0]


def add_halves(low, high, got, after=()):
    count = got.shape[0] // 2
    shift = count if high is None else 0
    steps = 1
    block = (count // steps,) + got.shape[1:]
    here = pl.BlockSpec(block, lambda i, *_: (i, 0, 0))
    there = pl.BlockSpec(block, lambda i, *_: (i + steps, 0, 0))
    shape = (count,) + got.shape[1:]
    return launch(
        add_kernel,
        "add",
        steps,
        (),
        [low, low if high is None else high, got, got],
        [here, there if shift else here, here, there],
        [(shape, BF), (shape, BF)],
        [here, here],
        (),
        (0, 12 * math.prod(shape)),
        after,
    )


def add_four(keep, got, after=(), held=()):
    shape = got.shape[1:]
    return launch(
        add_four_kernel,
        "add",
        1,
        (),
        [keep, got, *held],
        [whole(got.shape)] * 2 + [ANY] * len(held),
        [(v.shape, v.dtype) for v in held] + [(shape, BF)] * 4,
        [ANY] * len(held) + [whole_out(shape)] * 4,
        (),
        (0, 24 * math.prod(shape)),
        after,
        {2 + i: i for i in range(len(held))},
    )


def totals(kernel, name, terms, shapes, after=()):
    return launch(
        kernel,
        name,
        1,
        (),
        list(terms),
        [whole(term.shape) for term in terms],
        [(shape, F32) for shape in shapes],
        [whole_out(shape) for shape in shapes],
        (),
        (0, sum(2 * math.prod(term.shape) for term in terms)),
        after,
    )


def shards(
    images,
    counts,
    joint_weight,
    out_weight,
    up_weight,
    down_weight,
    first_gain,
    first_shift,
    query_bias,
    value_bias,
    out_bias,
    first_scale,
    second_gain,
    second_shift,
    up_bias,
    down_bias,
    second_scale,
    cotangent,
    sizes,
):
    fsdp, sub = sizes
    cube = Cube() if (fsdp, sub) == (8, 4) else None
    images_here, length, width = images.shape
    heads = width // HD
    rows = images_here * length
    hidden_units = up_weight.shape[1] * sub
    depth = width // ROW_TILES
    span = 3 * width // COL_TILES
    piece = width // COL_TILES
    part = hidden_units // PARTS
    lane = part // ROW_TILES
    steps = COL_TILES

    image_block = pl.BlockSpec((1, length, width), lambda i, *_: (i, 0, 0))
    row_block = pl.BlockSpec((length, width), lambda i, *_: (i, 0))
    column_block = pl.BlockSpec((width, length), lambda i, *_: (0, i))
    mixed_block = pl.BlockSpec((3 * width, length), lambda i, *_: (0, i))
    probs_block = pl.BlockSpec((1, heads, length, length), lambda i, *_: (i, 0, 0, 0))
    tall, wide = (rows, width), (width, rows)
    area = rows * width

    def input_norm(after):
        return launch(
            normalize_kernel,
            "first_norm",
            images_here,
            (),
            [images],
            [image_block],
            [(tall, F32), ((rows, 128), F32)],
            [row_block, pl.BlockSpec((length, 128), lambda i, *_: (i, 0))],
            (),
            (area * width, 8 * area),
            after,
            covers=LIGHT,
        )

    vectors = (first_gain, first_shift, query_bias, value_bias, out_bias, first_scale)
    vectors += (second_gain, second_shift, down_bias, second_scale)
    wide_span = span + 64

    if cube is not None:
        dest = cube.places()
        ins = [joint_weight, out_weight, *vectors, up_bias]
        first_piece = launch(
            pack_first_kernel,
            "pack_first",
            1,
            (),
            ins,
            [whole(v.shape) for v in ins],
            [((depth, wide_span + 2 * lane), BF)],
            [whole_out((depth, wide_span + 2 * lane))],
            (),
            (0, 4 * depth * wide_span),
        )[0]

        ins = [up_weight, down_weight.T]
        shape = (PARTS * 2 * depth, 2 * lane)
        feed_piece = launch(
            pack_kernel,
            "pack",
            1,
            (),
            ins,
            [whole(v.shape) for v in ins],
            [(shape, BF)],
            [whole_out(shape)],
            (),
            (0, 4 * math.prod(shape)),
        )[0]
        feed_pieces = lax.all_gather(feed_piece, BOTH, axis=0)

        normed_one, inverse_one = input_norm(())
        four = join(cube.gather_z(first_piece), (inverse_one,))
        near, far = cube.near(four), cube.far(four)
        far_near = cube.far(near)
        first = [four, near, far, far_near]
        first += [cube.over(v) for v in first]
        after_first = ()
    else:
        order = [p for p in range(PIECES) if p % 2 == 0] + [p for p in range(PIECES) if p % 2]
        back_order = [order.index(p) for p in range(PIECES)]
        dest = jnp.array(order, dtype=jnp.int32)
        normed_one, inverse_one = input_norm(())
        after_first = ()

        def fetch(value):
            return lax.all_gather(
                lax.all_gather(value, "sub", axis=1, tiled=True), "fsdp", axis=0, tiled=True
            )

        def cut(value, columns):
            value = value.reshape(ROW_TILES, depth, COL_TILES, columns)
            return value.transpose(0, 2, 1, 3).reshape(PIECES, depth, columns)

        def groups(value):
            value = jnp.stack([value[p] for p in order])
            return [value[i : i + GROUP] for i in range(0, PIECES, GROUP)]

        short = width // PIECES
        lines = [lax.all_gather(v, BOTH, axis=0, tiled=True) for v in vectors]
        lines = jnp.stack(lines).reshape(VECTORS, PIECES, short).transpose(1, 0, 2)
        lines = jnp.pad(lines, ((0, 0), (0, 0), (0, 64 - short)))
        long = lax.all_gather(up_bias, BOTH, axis=0, tiled=True).reshape(PIECES, 2, 2 * short)
        long = jnp.pad(long, ((0, 0), (0, 0), (0, 64 - 2 * short)))
        lines = jnp.concatenate([lines, long], axis=1)
        lines = jnp.pad(lines, ((0, 0), (0, depth - VECTORS - 2), (0, 0)))
        out_pieces = jnp.pad(cut(fetch(out_weight), piece), ((0, 0), (0, 0), (0, 2 * lane - piece)))
        first = [cut(fetch(joint_weight), span), lines, out_pieces]
        first = groups(jnp.concatenate(first, axis=2))
        up_parts = fetch(up_weight).reshape(ROW_TILES, depth, COL_TILES, 2, PARTS, lane)
        up_parts = up_parts.transpose(0, 2, 4, 1, 3, 5)
        down_parts = fetch(down_weight).reshape(ROW_TILES, PARTS, lane, COL_TILES, 2, depth)
        down_parts = down_parts.transpose(0, 3, 1, 5, 4, 2)
        shape = (PIECES, PARTS, depth, 2 * lane)
        feed_pieces = jnp.concatenate([up_parts.reshape(shape), down_parts.reshape(shape)], axis=2)
        feed_pieces = feed_pieces.reshape(PIECES, -1, 2 * lane)

    table_spec = whole((16, width))
    joint_scratch = [
        pltpu.VMEM((COL_TILES, ROW_TILES, depth, wide_span), BF),
        pltpu.SemaphoreType.DMA((PIECES,)),
    ]

    mixed, first_t, table, up_rows = launch(
        qkv_kernel,
        "qkv",
        images_here,
        (dest,),
        [normed_one, *first],
        [row_block] + [ANY] * GROUPS,
        [((3 * width, rows), BF), (wide, BF), ((16, width), F32), ((PARTS, part), F32)],
        [mixed_block, column_block, whole_out((16, width)), whole_out((PARTS, part))],
        joint_scratch,
        (6 * area * width, 14 * area),
        after_first,
        covers=LIGHT,
    )

    def attend(start, stop, into, after, covers):
        return launch(
            functools.partial(attention_kernel, start),
            "attention",
            stop - start,
            (counts,),
            [mixed, *into],
            [pl.BlockSpec((3 * width, length), lambda i, *_: (0, i + start))] + [ANY] * len(into),
            [(wide, BF), ((images_here, heads, length, length), BF)],
            [
                pl.BlockSpec((width, length), lambda i, *_: (0, i + start)),
                pl.BlockSpec((1, heads, length, length), lambda i, *_: (i + start, 0, 0, 0)),
            ],
            (),
            (16 * area * length // 2, 16 * area // 2),
            after,
            {2: 0, 3: 1} if into else None,
            covers,
        )

    attended, probs = attend(0, images_here, (), (), LIGHT)

    resid, branch, second, second_t, dfeed, dfeed_t, out_full = launch(
        second_kernel,
        "second_norm",
        images_here,
        (dest, counts),
        [images, cotangent, attended, table, *first],
        [image_block, image_block, column_block, table_spec] + [ANY] * GROUPS,
        [(tall, BF), (tall, BF), (tall, BF), (wide, BF), (tall, BF), (wide, BF)]
        + [((width, width), BF)],
        [row_block, row_block, row_block, column_block, row_block, column_block]
        + [whole_out((width, width))],
        [
            pltpu.VMEM((COL_TILES, ROW_TILES, depth, 2 * lane), BF),
            pltpu.SemaphoreType.DMA((PIECES,)),
            pltpu.VMEM((length, width), F32),
        ],
        (2 * area * width, 20 * area),
        covers=0.0,
    )

    def feed_forward(parts, carried, split, after=(), covers=1.0):
        ins = [up_rows, second, second_t, dfeed, dfeed_t, feed_pieces, *carried]
        count = len(parts)
        slots = (HALF if split else PIECES, count * 2 * depth, 2 * lane)
        tiles = rows // ROWS
        dma = pltpu.SemaphoreType.DMA
        return launch(
            functools.partial(mlp_kernel, parts, split),
            "feed_forward",
            1,
            (dest,),
            ins,
            [whole(up_rows.shape)] + [ANY] * (len(ins) - 1),
            [(tall, BF), (tall, BF), ((count, part), F32)] + [(slots, BF)] * (1 + split),
            [ANY, ANY, whole_out((count, part))] + [ANY] * (1 + split),
            [
                pltpu.VMEM((2, rows, width), BF),
                pltpu.VMEM((2, width, rows), BF),
                pltpu.VMEM((2, rows, width), BF),
                pltpu.VMEM((count, 2, width, part), BF),
                pltpu.VMEM((rows, part), BF),
                pltpu.VMEM((rows, part), BF),
                pltpu.VMEM((count, 2, width, part), BF),
                dma((count, PIECES, 2)),
                dma((2, tiles)),
                dma((2,)),
                dma((2, tiles)),
                dma((count, PIECES, 2)),
            ],
            (12 * area * part * count, 20 * area),
            after,
            covers=covers,
        )

    early = tuple(range(PARTS - 1))
    feed, dsecond, early_bias, early_grads = feed_forward(early, (), False, (), 0.0)
    feed, dsecond, late_bias, *late_grads = feed_forward(
        (PARTS - 1,), (feed, dsecond), True, (early_grads,)
    )

    waits = {}
    if cube is not None:
        early_total = lax.psum_scatter(early_grads, BOTH, scatter_dimension=0)
        late_got = cube.over(late_grads[1])

    block_out, dresid, dattended, out_grad, middle_sums = launch(
        middle_kernel,
        "middle",
        images_here,
        (counts,),
        [cotangent, feed, dsecond, resid, branch, attended, out_full, table],
        [image_block, row_block, row_block, row_block, row_block, column_block]
        + [whole((width, width)), table_spec],
        [(images.shape, BF), (tall, BF), (wide, BF), ((width, width), BF), ((8, width), F32)],
        [image_block, row_block, column_block, whole_out((width, width)), whole_out((8, width))],
        [
            pltpu.VMEM((width, width), F32),
            pltpu.VMEM((6, 8, width), F32),
            pltpu.VMEM((length, width), BF),
        ],
        (4 * area * width, 30 * area),
        waits.get("middle", ()),
    )

    if cube is not None:
        late_low, late_high = add_halves(late_grads[0], None, late_got, (dresid,))
        late_got = cube.far(late_high)
        waits["attention_back"] = (late_high,)

    dmixed, attention_sums, send_first = launch(
        attention_back_kernel,
        "attention_back",
        images_here,
        (dest,),
        [mixed, probs, attended, dattended, first_t, out_grad],
        [mixed_block, probs_block, column_block, column_block, ANY, ANY],
        [((3 * width, rows), BF), ((8, width), F32), ((HALF, depth, width), BF)],
        [mixed_block, whole_out((8, width)), ANY],
        [
            pltpu.VMEM((width, 128), F32),
            pltpu.VMEM((width, 128), F32),
            pltpu.VMEM((heads, length, length), BF),
            pltpu.VMEM((images_here, 3 * width, length), BF),
            pltpu.VMEM((width, rows), BF),
            pltpu.VMEM((width, width), BF),
            pltpu.VMEM((2, width, width), BF),
            pltpu.SemaphoreType.DMA((2 + HALF,)),
        ],
        (32 * area * length, 24 * area),
        waits.get("attention_back", ()),
    )

    if cube is not None:
        late_low, late_high = add_halves(late_low, None, late_got, (dmixed,))
        late_got = cube.near(late_high)
        waits["joint_grad"] = (late_high,)

    if cube is not None:
        first_got = cube.over(send_first)

    def column_tile(g):
        return pl.BlockSpec((span, rows), lambda _, dest: (2 * g + lax.rem(dest[0], 2), 0))

    keep_first = launch(
        joint_grad_kernel,
        "joint_grad",
        1,
        (dest,),
        [first_t, dmixed, dmixed, out_grad],
        [whole(wide), column_tile(0), column_tile(1), whole((width, width))],
        [((HALF, depth, width), BF)],
        [ANY],
        [pltpu.VMEM((2, width, width), BF), pltpu.SemaphoreType.DMA((HALF,))],
        (3 * area * width, 10 * area),
        waits.get("joint_grad", ()),
    )[0]

    after_input = ()
    if cube is not None:
        first_low, first_high = add_halves(keep_first, None, first_got)
        first_got = cube.far(first_high)
        late_last = add_four(late_low, late_got, (first_high,))
        late_terms = cube.reduce_z(late_last)
        after_input = (late_last[0],)

    image_grad, input_sums = launch(
        input_grad_kernel,
        "input_grad",
        images_here,
        (dest,),
        [normed_one, inverse_one, dresid, dmixed, table, *first],
        [row_block, pl.BlockSpec((length, 128), lambda i, *_: (i, 0)), row_block, mixed_block]
        + [table_spec]
        + [ANY] * GROUPS,
        [(images.shape, F32), ((8, width), F32)],
        [image_block, whole_out((8, width))],
        joint_scratch
        + [pltpu.VMEM((2, 8, width), F32), pltpu.VMEM((length, width), F32)],
        (6 * area * width, 20 * area),
        after_input,
    )

    after = ()
    if cube is not None:
        first_low, first_high = add_halves(first_low, None, first_got, (image_grad,))
        first_got = cube.near(first_high)
        after = (first_high,)
    ins = [input_sums, attention_sums, middle_sums, early_bias, late_bias]
    sums = launch(
        collect_kernel,
        "collect",
        1,
        (),
        ins,
        [whole(v.shape) for v in ins],
        [((16, width), F32)],
        [whole_out((16, width))],
        (),
        (10**8, 0),
        after,
    )[0]
    short = first_gain.shape[0]
    if cube is not None:
        late_total = totals(
            late_total_kernel, "late_total", late_terms, (late_terms[0].shape,), (image_grad,)
        )
        first_last = add_four(first_low, first_got, (sums, *late_total))
        first_terms = cube.reduce_z(first_last)
        sums = cube.total(sums, cube.z[:2])
        sums = gate(sums, first_last[:1], 5.0)
        sums = cube.total(sums, (cube.core, cube.x, cube.y))
        joint_grad, out_weight_grad = totals(
            first_total_kernel,
            "first_total",
            first_terms,
            (joint_weight.shape, out_weight.shape),
        )
        device = lax.axis_index("fsdp") * sub + lax.axis_index("sub")
        vectors = lax.dynamic_slice(sums[:10], (0, device * short), (10, short))
        up_bias_grad = lax.dynamic_slice(
            sums[VECTORS : VECTORS + 4].reshape(-1), (device * up_bias.shape[0],), up_bias.shape
        )
        up_grad, down_grad = totals(
            feed_total_kernel,
            "feed_total",
            (early_total, *late_total),
            (up_weight.shape, down_weight.shape[::-1]),
            first_last[:1],
        )
        down_grad = down_grad.T
    else:

        def hand_out(value):
            value = lax.psum_scatter(value.astype(BF), "fsdp", scatter_dimension=0, tiled=True)
            value = lax.psum_scatter(value, "sub", scatter_dimension=1, tiled=True)
            return value.astype(F32)

        def uncut(value, columns):
            value = value.reshape(ROW_TILES, COL_TILES, depth, columns)
            return value.transpose(0, 2, 1, 3).reshape(width, COL_TILES * columns)

        def in_order(value):
            return jnp.stack([value[i] for i in back_order])

        grads = in_order(jnp.concatenate([keep_first, send_first]))
        joint_grad = hand_out(uncut(grads[:, :, :span], span))
        out_weight_grad = hand_out(uncut(grads[:, :, span:], piece))
        late_grads = in_order(jnp.concatenate(late_grads))
        grads = jnp.concatenate([early_grads, late_grads], axis=1)
        grads = grads.reshape(ROW_TILES, COL_TILES, PARTS, 2, depth, 2, lane)
        up_grad = grads[:, :, :, 0].transpose(0, 3, 1, 4, 2, 5).reshape(width, hidden_units)
        down_grad = grads[:, :, :, 1].transpose(0, 2, 5, 1, 4, 3).reshape(hidden_units, width)
        up_grad, down_grad = hand_out(up_grad), hand_out(down_grad)

        def hand_vector(value):
            return lax.psum_scatter(value, BOTH, scatter_dimension=0, tiled=True)

        vectors = [hand_vector(sums[v]) for v in range(10)]
        up_bias_grad = hand_vector(sums[VECTORS : VECTORS + 4].reshape(-1))
    return (
        block_out,
        image_grad,
        joint_grad,
        out_weight_grad,
        up_grad,
        down_grad,
        vectors[0],
        vectors[1],
        vectors[2],
        vectors[3],
        vectors[4],
        vectors[5],
        vectors[6],
        vectors[7],
        up_bias_grad,
        vectors[8],
        vectors[9],
    )


def solution(mesh):
    rows = P(BOTH, None, None)
    matrix = P("fsdp", "sub")
    vector = P(BOTH)
    sizes = (mesh.shape["fsdp"], mesh.shape["sub"])
    return jax.shard_map(
        functools.partial(shards, sizes=sizes),
        mesh=mesh,
        in_specs=(rows, vector) + (matrix,) * 4 + (vector,) * 11 + (rows,),
        out_specs=(rows, rows) + (matrix,) * 4 + (vector,) * 11,
        check_vma=False,
    )
```
